128 devices in a mesh: head: 8 (over y, core), exp: 16 (over z, x).
Axes of the slice: x: 4, y: 4, z: 4, core: 2. Of those that a mesh axis runs over, the one named last changes fastest.
Arguments:
- hidden_in: bfloat16 [4, 128, 6144], P(None, 'exp'), may hold values from -6 to 6
- step_qkv: bfloat16 [4, 128, 3, 8192], P(None, 'exp', None, 'head'), may hold values from -6 to 6
- decay_rates: float32 [4, 64], P(None, 'head'), may hold values from 0.005 to 1
- kv_state: float32 [128, 64, 128, 128], P('exp', 'head'), may hold values from -6 to 6
- attn_gain: float32 [8192], P('head'), may hold values from 0.1 to 1.9
- out_proj: bfloat16 [8192, 6144], P('head', 'exp'), may hold values from -0.0625 to 0.0625
- ffn_gain: float32 [6144], replicated, may hold values from 0.1 to 1.9
- routes: int32 [4, 128, 2], P(None, 'exp'), may hold values from 0 to 15, all different within a row; in each aligned block of 8 rows (0 to 7, 8 to 15, ..., all dimensions but the last counted through in order) at most 2 rows name the same one
- route_weights: float32 [4, 128, 2], P(None, 'exp'), may hold values from 0.2 to 1
- w_gate: bfloat16 [16, 6144, 4608], P('exp', None, 'head'), may hold values from -0.078125 to 0.078125
- w_up: bfloat16 [16, 6144, 4608], P('exp', None, 'head'), may hold values from -0.078125 to 0.078125
- w_down: bfloat16 [16, 4608, 6144], P('exp', 'head'), may hold values from -0.09375 to 0.09375
Outputs:
- attended: bfloat16 [4, 128, 6144], P(None, 'exp', 'head')
- expert_out: bfloat16 [4, 128, 6144], P(None, 'exp', 'head')
The draws below stay inside these ranges and needn't reach their ends.
Inputs may be any that keep to these rules, and one draw needn't show every extreme that they name: `routes`: in each step the two experts of a row differ; in each step the rows of one device name one expert at most 2 times, a bound that some block reaches.
All inputs are finite; a program needn't handle non-finite values.
Results may differ from the reference program's by a relative error of at most 0.013.
Values may be sent and summed in bfloat16 or wider, within the bound.
No kernel may reach another device: no remote copies, remote signals or barrier semaphores. Data moves between devices by JAX's collectives and lax.ppermute only.
A program may use at most 128 MiB of HBM per device.

```python
import math
import jax
import jax.numpy as jnp
import numpy as np
from jax import lax

D = 6144
LIGHTNING_HEADS = 64
HEAD_DIM = 128
HID = 4608
DECODE_STEPS = 4
B_DEV = 8
EXPERTS = 16
MOST = 2
ROWS = 128


def draw_decay_rates(key, part):
    key = jax.random.fold_in(key, 7)
    decay_random_key, spike_random_key, reduction_random_key = jax.random.split(key, 3)
    low_rate, high_rate = (0.02, 4.0)
    decay_values = jnp.exp(jax.random.uniform(decay_random_key, (1, LIGHTNING_HEADS), jnp.float32, math.log(low_rate), math.log(high_rate)))
    spike_events = jax.random.bernoulli(spike_random_key, 0.25, (DECODE_STEPS, LIGHTNING_HEADS))
    reduction_factor = jax.random.uniform(reduction_random_key, (DECODE_STEPS, LIGHTNING_HEADS), jnp.float32, 0.5, 0.8)
    return (jnp.exp(-decay_values) * jnp.where(spike_events, reduction_factor, 1.0)).astype(jnp.float32)


def shard_levels(rng, dims, cuts, smallest, top_value):
    gain, own = 1.0, jax.random.fold_in(rng, 6)
    for position, blocks in cuts:
        draws = jnp.exp(jax.random.uniform(jax.random.fold_in(own, position), (blocks,), jnp.float32, smallest / len(cuts), top_value / len(cuts)))
        gain = gain * jnp.repeat(draws, dims[position] // blocks).reshape([-1 if axis == position else 1 for axis in range(len(dims))])
    return gain


def deal_out(key, own, number, rows, amount, top, bound, skew):
    order = jax.random.permutation(key, amount)
    heavy_load, common = load_shares(amount, rows * top, bound, skew, True), load_shares(amount, rows * top, bound, skew, False)
    places = jnp.arange(amount)

    def named(sizes, offset_by):
        used = int((sizes > 0).sum())
        fixed = max(1, used // 4)
        moved = fixed + (places - fixed + offset_by * (used - fixed)) % max(1, amount - fixed)
        return jnp.zeros((amount,), jnp.int32).at[order[jnp.where(places < fixed, places, moved)]].set(jnp.asarray(sizes, jnp.int32))

    sizes = jnp.where(number % 4 == 0, named(heavy_load, number // 4), named(common, number - number // 4 - 1))
    mixed = jax.random.permutation(jax.random.fold_in(own, 3), amount)
    source_of, sink = mixed[0:amount // 2 * 2:2], mixed[1:amount // 2 * 2:2]
    room = jnp.minimum(sizes[source_of] - 1, bound - sizes[sink]) // 2
    room = jnp.where((source_of == order[0]) | (sink == order[0]) | (sizes[sink] == 0), 0, jnp.maximum(room, 0))
    moved = jax.random.randint(jax.random.fold_in(own, 4), (amount // 2,), 0, 1 << 20) % (room + 1)
    sizes = sizes.at[source_of].add(-moved).at[sink].add(moved)
    members = jnp.searchsorted(jnp.cumsum(sizes), jnp.arange(rows * top), side="right").astype(jnp.int32)
    listing = members.reshape(top, rows).T
    listing = listing[jax.random.permutation(jax.random.fold_in(own, 1), rows)]
    offset_by = jax.random.randint(jax.random.fold_in(own, 2), (rows, 1), 0, top)
    return jnp.take_along_axis(listing, (jnp.arange(top)[None, :] + offset_by) % top, axis=1)


def load_shares(amount, total, bound, slope, full):
    loads = [(1 << 20) // math.isqrt(grade ** slope) + 1 for grade in range(1, amount + 1)]
    largest = bound if full else min(bound, max(-(-total // amount), total * loads[0] // sum(loads)))
    least = 1 if total - largest >= amount - 1 else 0
    given, spare = [largest] + [least] * (amount - 1), total - largest - least * (amount - 1)
    while spare > 0:
        movable = [i for i in range(1, amount) if given[i] < largest] or [i for i in range(1, amount) if given[i] < bound]
        whole, left = sum([loads[i] for i in movable]), spare
        for i in movable:
            more = min(bound - given[i], max(1, left * loads[i] // whole), spare)
            given[i] = given[i] + more
            spare = spare - more
    return np.array(given)


def centred(key, shape, scale, most, cuts=(), kind=jnp.bfloat16):
    values = jax.random.normal(key, shape, jnp.float32) * scale
    if len(cuts) > 0:
        values = shard_levels(key, shape, cuts, -0.22, 0.18) * values
    return jnp.clip(values, min=-most, max=most).astype(kind)


def setup_inputs(seed: int = 0) -> dict:
    seeds = jax.random.split(jax.random.key(seed), 13)
    hidden_in = centred(seeds[0], (DECODE_STEPS, ROWS, D), 1.0, 6.0, ((1, 16),))
    step_qkv = centred(seeds[1], (DECODE_STEPS, ROWS, 3, LIGHTNING_HEADS * HEAD_DIM), 1.0, 6.0, ((1, 16), (3, 8)))
    decay_rates = draw_decay_rates(jax.random.fold_in(seeds[12], 71), 0)
    kv_state = centred(seeds[3], (ROWS, LIGHTNING_HEADS, HEAD_DIM, HEAD_DIM), 1.0, 6.0, ((0, 16), (1, 8)), jnp.float32)
    attn_gain = jnp.clip(1.0 + 0.18 * jax.random.normal(seeds[4], (LIGHTNING_HEADS * HEAD_DIM,), jnp.float32), 0.1, 1.9)
    out_proj = centred(seeds[5], (LIGHTNING_HEADS * HEAD_DIM, D), (LIGHTNING_HEADS * HEAD_DIM) ** -0.5, 0.0625, ((0, 8), (1, 16)))
    ffn_gain = jnp.clip(1.0 + 0.18 * jax.random.normal(seeds[6], (D,), jnp.float32), 0.1, 1.9)
    routes_keys = jax.random.split(jax.random.fold_in(seeds[7], 1), DECODE_STEPS * ROWS // B_DEV)
    routes_turns = jax.random.permutation(jax.random.fold_in(seeds[7], 3), DECODE_STEPS * ROWS // B_DEV)
    routes = jax.vmap(lambda own, number: deal_out(jax.random.fold_in(seeds[7], 2), own, number, B_DEV, EXPERTS, 2, MOST, 2))(routes_keys, routes_turns).reshape((DECODE_STEPS, ROWS, 2))
    route_weights = jnp.clip(0.2 + 0.8 * jax.random.uniform(seeds[8], (DECODE_STEPS, ROWS, 2), jnp.float32) ** shard_levels(seeds[8], (DECODE_STEPS, ROWS, 2), ((1, 16),), -0.2, 0.2), 0.2, 1.0)
    w_gate = centred(seeds[9], (EXPERTS, D, HID), D ** -0.5, 0.078125, ((0, 16), (2, 8)))
    w_up = centred(seeds[10], (EXPERTS, D, HID), D ** -0.5, 0.078125, ((0, 16), (2, 8)))
    w_down = centred(seeds[11], (EXPERTS, HID, D), HID ** -0.5, 0.09375, ((0, 16), (1, 8)))
    return {"hidden_in": hidden_in, "step_qkv": step_qkv, "decay_rates": decay_rates, "kv_state": kv_state, "attn_gain": attn_gain, "out_proj": out_proj, "ffn_gain": ffn_gain, "routes": routes, "route_weights": route_weights, "w_gate": w_gate, "w_up": w_up, "w_down": w_down}


def rms_rows(values, gain_vec):
    return values * lax.rsqrt(lax.optimization_barrier(jnp.mean(values * values, axis=-1, keepdims=True)) + 1e-06) * gain_vec

def slot_tables(route_ids, gate_weights, experts, capacity):
    row_count = route_ids.shape[0]
    flat_ids = route_ids.reshape(-1)
    expert_iota = jnp.arange(experts, dtype=jnp.int32)
    hit_table = (flat_ids[:, None] == expert_iota[None, :]).astype(jnp.int32)
    before = jnp.cumsum(hit_table, axis=0) - hit_table
    rank_pos = lax.optimization_barrier(jnp.sum(before * hit_table, axis=1))
    target = flat_ids * capacity + rank_pos
    slot_iota = jnp.arange(experts * capacity, dtype=jnp.int32)
    slot_match = (target[None, :] == slot_iota[:, None]).astype(jnp.float32)
    placed = slot_match.reshape(experts * capacity, row_count, 2)
    send_table = lax.optimization_barrier(jnp.sum(placed, axis=2))
    mix_table = lax.optimization_barrier(jnp.sum(placed * gate_weights.astype(jnp.float32)[None, :, :], axis=2))
    return (send_table, mix_table)

def reference(hidden_in, step_qkv, decay_rates, kv_state, attn_gain, out_proj, ffn_gain, routes, route_weights, w_gate, w_up, w_down):
    row_total = hidden_in.shape[1]
    width = hidden_in.shape[2]
    head_count = decay_rates.shape[1]
    head_size = kv_state.shape[2]
    experts = w_gate.shape[0]
    capacity = MOST
    blocks = row_total // B_DEV
    gain_heads = attn_gain.reshape(head_count, head_size)
    state_now = kv_state
    attended_list = []
    expert_list = []
    for step in range(DECODE_STEPS):
        queries = step_qkv[step, :, 0].astype(jnp.float32).reshape(row_total, head_count, head_size)
        key_vecs = step_qkv[step, :, 1].reshape(row_total, head_count, head_size)
        value_vecs = step_qkv[step, :, 2].reshape(row_total, head_count, head_size)
        outer = jnp.einsum('bhk,bhv->bhkv', key_vecs, value_vecs, preferred_element_type=jnp.float32)
        state_now = decay_rates[step][None, :, None, None] * state_now + outer
        readout = jnp.einsum('bhk,bhkv->bhv', queries, state_now, precision=lax.Precision.HIGHEST)
        readout = rms_rows(readout, gain_heads).reshape(row_total, head_count * head_size).astype(jnp.bfloat16)
        projected = jnp.dot(readout, out_proj, preferred_element_type=jnp.float32)
        attended_now = (hidden_in[step].astype(jnp.float32) + projected).astype(jnp.bfloat16)
        normed = rms_rows(attended_now.astype(jnp.float32), ffn_gain).astype(jnp.bfloat16)

        def build(block_rows, block_ids, block_weights):
            send_table, mix_table = slot_tables(block_ids, block_weights, experts, capacity)
            sent = jnp.dot(send_table.astype(jnp.bfloat16), block_rows, preferred_element_type=jnp.float32)
            return (sent.astype(jnp.bfloat16).reshape(experts, capacity, width), mix_table)
        sent_all, mix_all = jax.vmap(build)(normed.reshape(blocks, B_DEV, width), routes[step].reshape(blocks, B_DEV, 2), route_weights[step].reshape(blocks, B_DEV, 2))
        by_expert = jnp.transpose(sent_all, (1, 0, 2, 3)).reshape(experts, blocks * capacity, width)

        def expert_apply(operands):
            rows_in, gate_mat, up_mat, down_mat = operands
            gate_val = jnp.dot(rows_in, gate_mat, preferred_element_type=jnp.float32)
            up_val = jnp.dot(rows_in, up_mat, preferred_element_type=jnp.float32)
            hidden_val = (jax.nn.silu(gate_val) * up_val).astype(jnp.bfloat16)
            return jnp.dot(hidden_val, down_mat, preferred_element_type=jnp.float32).astype(jnp.bfloat16)
        results = lax.map(expert_apply, (by_expert, w_gate, w_up, w_down))
        back = jnp.transpose(results.reshape(experts, blocks, capacity, width), (1, 0, 2, 3)).reshape(blocks, experts * capacity, width)
        mixed = jnp.einsum('nsr,nsd->nrd', mix_all, back.astype(jnp.float32), precision=lax.Precision.HIGHEST)
        attended_list.append(attended_now)
        expert_list.append(mixed.reshape(row_total, width).astype(jnp.bfloat16))
    return (jnp.stack(attended_list, 0), jnp.stack(expert_list, 0))
```

```python
import functools

import jax
import jax.numpy as jnp
from jax import lax
from jax.experimental import pallas as pl
from jax.experimental.pallas import tpu as pltpu
from jax.sharding import PartitionSpec as P

STEPS = 4
ROWS = 8
EPS = 1e-06
F32 = jnp.float32
BF16 = jnp.bfloat16
MIB = 1 << 20


def vmem_params(mib):
    return pltpu.CompilerParams(vmem_limit_bytes=mib * MIB)


def over_head(value, bits):
    return lax.ppermute(value, "head", [(i, i ^ bits) for i in range(8)])


def over_exp(value, bits):
    return lax.ppermute(value, "exp", [(i, i ^ bits) for i in range(16)])


def over_all(value, dest):
    pairs = []
    for i in range(128):
        y, c, z, x = i // 32, i // 16 % 2, i // 4 % 4, i % 4
        y, c, z, x = dest(y, c, z, x)
        pairs.append((i, ((y * 2 + c) * 4 + z) * 4 + x))
    return lax.ppermute(value, ("head", "exp"), pairs)


def readout_kernel(qkv_ref, state_ref, first_ref, mix_ref, gain_ref, out_ref, acc_ref):
    row = pl.program_id(0)
    heads = state_ref.shape[1]
    size = state_ref.shape[2]
    q = qkv_ref[0, 0]
    k = qkv_ref[0, 1]
    v = qkv_ref[0, 2]
    row_head = lax.broadcasted_iota(jnp.int32, (heads * STEPS, size), 0) % heads
    q_twice = jnp.concatenate([q, q], axis=1)
    scores = lax.dot_general(q, k, (((1,), (1,)), ((), ())), preferred_element_type=F32)
    carried = jnp.zeros((heads * STEPS, size), F32)
    for pair in range(heads // 2):
        wide = jnp.concatenate([state_ref[0, 2 * pair], state_ref[0, 2 * pair + 1]], axis=1)
        high = wide.astype(BF16)
        low = (wide - high.astype(F32)).astype(BF16)
        both = jnp.dot(
            q_twice, jnp.concatenate([high, low], axis=0), preferred_element_type=F32
        )
        carried = jnp.where(row_head == 2 * pair, both[:, :size], carried)
        carried = jnp.where(row_head == 2 * pair + 1, both[:, size:], carried)
    o = carried * first_ref[...]
    o += jnp.dot(
        scores * mix_ref[...],
        v.astype(F32),
        precision=lax.Precision.HIGHEST,
        preferred_element_type=F32,
    )
    o = o * lax.rsqrt(jnp.mean(o * o, axis=-1, keepdims=True) + EPS) * gain_ref[...]
    for t in range(STEPS):
        acc_ref[t * ROWS + row] = o[t * heads : (t + 1) * heads]

    @pl.when(row == pl.num_programs(0) - 1)
    def _():
        for head in range(heads):
            out_ref[:, head * size : (head + 1) * size] = acc_ref[:, head, :].astype(BF16)


def readouts(step_qkv, decay, state, attn_gain):
    heads, size = state.shape[1], state.shape[2]
    n = heads * STEPS
    qkv = step_qkv.reshape(STEPS, ROWS, 3, heads, size).transpose(1, 2, 0, 3, 4)
    qkv = qkv.reshape(ROWS, 3, n, size)
    one = jnp.ones((heads,), F32)
    zero = jnp.zeros((heads,), F32)
    first = [decay[0]]
    for t in range(1, STEPS):
        first.append(first[-1] * decay[t])
    first = jnp.stack(first, 0).reshape(n, 1)
    rows = []
    for t in range(STEPS):
        row, run = [zero] * STEPS, one
        for s in range(t, -1, -1):
            row[s] = run
            run = run * decay[s]
        rows.append(jnp.stack(row, 0))
    causal = jnp.stack(rows, 0)
    same = jnp.eye(heads, dtype=F32)
    mix = (causal[:, None, :, :] * same[None, :, None, :]).reshape(n, n)
    gain = jnp.broadcast_to(attn_gain.reshape(1, heads, size), (STEPS, heads, size))
    return pl.pallas_call(
        readout_kernel,
        out_shape=jax.ShapeDtypeStruct((STEPS * ROWS, heads * size), BF16),
        grid=(ROWS,),
        in_specs=[
            pl.BlockSpec((1, 3, n, size), lambda i: (i, 0, 0, 0)),
            pl.BlockSpec((1, heads, size, size), lambda i: (i, 0, 0, 0)),
            pl.BlockSpec((n, size), lambda i: (0, 0)),
            pl.BlockSpec((n, n), lambda i: (0, 0)),
            pl.BlockSpec((n, size), lambda i: (0, 0)),
        ],
        out_specs=pl.BlockSpec((STEPS * ROWS, heads * size), lambda i: (0, 0)),
        scratch_shapes=[pltpu.VMEM((STEPS * ROWS, heads, size), F32)],
        compiler_params=vmem_params(16),
        cost_estimate=pl.CostEstimate(
            flops=2 * ROWS * 2 * STEPS * heads * size * size * 2,
            bytes_accessed=state.size * 4,
            transcendentals=0,
        ),
        name="readout",
    )(qkv, state, jnp.broadcast_to(first, (n, size)), mix, gain.reshape(n, size))


def ranks(ids, experts):
    blocks = ids.shape[0]
    flat = ids.reshape(blocks, 2 * ROWS)
    same = flat[:, :, None] == flat[:, None, :]
    index = jnp.arange(2 * ROWS)
    earlier = index[None, :] < index[:, None]
    return jnp.sum((same & earlier[None]).astype(jnp.int32), axis=2).reshape(ids.shape)


def gate_up_kernel(*refs):
    x_refs, (gate_ref, up_ref, out_ref, gate_acc, up_acc) = refs[:8], refs[8:]
    step = pl.program_id(0)
    x = jnp.concatenate([r[...] for r in x_refs], axis=0)
    gate = jnp.dot(x, gate_ref[0], preferred_element_type=F32)
    up = jnp.dot(x, up_ref[0], preferred_element_type=F32)

    @pl.when(step == 0)
    def _():
        gate_acc[...] = gate
        up_acc[...] = up

    @pl.when(step > 0)
    def _():
        gate_acc[...] += gate
        up_acc[...] += up

    @pl.when(step == pl.num_programs(0) - 1)
    def _():
        g = gate_acc[...]
        out_ref[...] = (g / (1.0 + jnp.exp(-g)) * up_acc[...]).astype(BF16)


def gate_up(pieces, w_gate, w_up):
    slots, width = pieces[0].shape
    hidden = w_gate.shape[2]
    chunk = width // 8
    rows = slots * len(pieces)
    return pl.pallas_call(
        gate_up_kernel,
        out_shape=jax.ShapeDtypeStruct((rows, hidden), BF16),
        grid=(width // chunk,),
        in_specs=[pl.BlockSpec((slots, chunk), lambda i: (0, i))] * len(pieces)
        + [pl.BlockSpec((1, chunk, hidden), lambda i: (0, i, 0))] * 2,
        out_specs=pl.BlockSpec((rows, hidden), lambda i: (0, 0)),
        scratch_shapes=[pltpu.VMEM((rows, hidden), F32)] * 2,
        compiler_params=vmem_params(24),
        cost_estimate=pl.CostEstimate(
            flops=4 * rows * width * hidden,
            bytes_accessed=4 * width * hidden,
            transcendentals=rows * hidden,
        ),
        name="gate_up",
    )(*pieces, w_gate, w_up)


def down_kernel(place_ref, x_ref, w_ref, out_ref):
    out_ref[0] = jnp.dot(x_ref[...], w_ref[0], preferred_element_type=F32).astype(BF16)


def down(place, x, w_down, share):
    rows, hidden = x.shape
    parts = place.shape[0]
    return pl.pallas_call(
        down_kernel,
        out_shape=jax.ShapeDtypeStruct((parts, rows, share), BF16),
        grid_spec=pltpu.PrefetchScalarGridSpec(
            num_scalar_prefetch=1,
            grid=(parts,),
            in_specs=[
                pl.BlockSpec((rows, hidden), lambda i, p: (0, 0)),
                pl.BlockSpec((1, hidden, share), lambda i, p: (0, 0, p[i])),
            ],
            out_specs=pl.BlockSpec((1, rows, share), lambda i, p: (i, 0, 0)),
        ),
        compiler_params=vmem_params(16),
        cost_estimate=pl.CostEstimate(
            flops=2 * rows * hidden * share * parts,
            bytes_accessed=2 * hidden * share * parts,
            transcendentals=0,
        ),
        name="down",
    )(place, x, w_down)


def final_sum_kernel(place_ref, own_ref, got1_ref, got2_ref, got3_ref, out_ref):
    y, c = place_ref[0], place_ref[1]
    for ky in range(4):
        sums = []
        for kc in range(2):
            total = own_ref[0, kc, ky].astype(F32)
            for k, ref in ((1, got1_ref), (2, got2_ref), (3, got3_ref)):
                total += ref[kc, ky ^ k].astype(F32)
            sums.append(total)
        low = jnp.where(c == 0, sums[0], sums[1])
        high = jnp.where(c == 0, sums[1], sums[0])
        for x in range(4):
            block = jnp.concatenate([low[4 * x : 4 * x + 4], high[4 * x : 4 * x + 4]], axis=0)
            out_ref[lax.bitwise_xor(y, ky) * 4 + x] = block.astype(BF16)


def final_sum(place, own, got):
    share = own.shape[-1]
    return pl.pallas_call(
        final_sum_kernel,
        out_shape=jax.ShapeDtypeStruct((16, 8, share), BF16),
        in_specs=[pl.BlockSpec(memory_space=pltpu.SMEM)]
        + [pl.BlockSpec(memory_space=pltpu.VMEM)] * 4,
        out_specs=pl.BlockSpec(memory_space=pltpu.VMEM),
        compiler_params=vmem_params(16),
        cost_estimate=pl.CostEstimate(flops=4 * 128 * share, bytes_accessed=1 << 20, transcendentals=0),
        name="final_sum",
    )(place, own, *got)


def shards(
    hidden_in,
    step_qkv,
    decay_rates,
    kv_state,
    attn_gain,
    out_proj,
    ffn_gain,
    routes,
    route_weights,
    w_gate,
    w_up,
    w_down,
):
    width = hidden_in.shape[2]
    experts = 16
    cols = width // 16
    share = width // 8
    head, exp = lax.axis_index("head"), lax.axis_index("exp")
    y, c, z, x = head // 2, head % 2, exp // 4, exp % 4

    pair_rows = lax.dynamic_slice(hidden_in, (2 * c, 0, y * 4 * cols), (2, ROWS, 4 * cols))
    pair_rows = pair_rows.reshape(2 * ROWS, 4 * cols)
    pair_routes = lax.dynamic_slice(routes, (2 * c, 0, 0), (2, ROWS, 2)).reshape(2 * ROWS, 2)
    pair_routes = jnp.pad(pair_routes.astype(BF16), ((0, 0), (0, 126)))
    arrived = []
    for k in range(4):
        block = lax.dynamic_slice(pair_rows, (0, (x ^ k) * cols), (2 * ROWS, cols))
        block = jnp.concatenate([block, pair_routes], axis=1)
        arrived.append(over_all(block, lambda y, c, z, x, k=k: (z, c, y, x ^ k)))
    arrived = jnp.stack(arrived, 0)
    hidden_rows = arrived[:, :, :cols]
    row_routes = arrived[:, :, cols : cols + 2].astype(jnp.int32)

    readout = readouts(step_qkv, decay_rates, kv_state, attn_gain)
    half_a, half_b = readout[: 2 * ROWS], readout[2 * ROWS :]
    by_z = jnp.stack([half_a] + [over_exp(half_a, 4 * k) for k in (1, 2, 3)], 0)
    by_x = jnp.stack([half_b] + [over_exp(half_b, k) for k in (1, 2, 3)], 0)
    all_a = [by_z] + [over_exp(by_z, k) for k in (1, 2, 3)]
    all_b = [by_x] + [over_exp(by_x, 4 * k) for k in (1, 2, 3)]
    depth = readout.shape[1]

    def project(pieces):
        rows = jnp.concatenate([p.reshape(8 * ROWS, depth) for p in pieces], axis=0)
        out = jnp.dot(rows, out_proj, preferred_element_type=F32).astype(BF16)
        return out.reshape(4, 4, 2 * ROWS, cols)

    part_a = project(all_a)
    part_b = project(all_b).transpose(1, 0, 2, 3)
    mine = jnp.where(c == 0, part_a, part_b)
    other = jnp.where(c == 0, part_b, part_a)
    mine = (mine.astype(F32) + over_head(other, 1).astype(F32)).astype(BF16)

    def for_y(k):
        return lax.dynamic_index_in_dim(mine, y ^ k ^ z, 1, keepdims=False)

    summed = for_y(0).astype(F32)
    for k in (1, 2, 3):
        summed += over_head(for_y(k), 2 * k).astype(F32)
    attended = (hidden_rows.astype(F32) + summed).astype(BF16)

    pieces = []
    for k in range(4):
        source = (2 * c + x % 2) ^ k
        block = lax.dynamic_index_in_dim(attended, source ^ x, 0, keepdims=False)
        pieces.append(
            over_all(block, lambda y, c, z, x, k=k: (z, x // 2, y, (2 * c + x % 2) ^ k))
        )
    pieces = jnp.stack(pieces, 0)
    ordered = [lax.dynamic_index_in_dim(pieces, j ^ x, 0, keepdims=False) for j in range(4)]
    attended_out = jnp.concatenate(
        [jnp.concatenate(ordered[:2], axis=1), jnp.concatenate(ordered[2:], axis=1)], axis=0
    ).reshape(STEPS, ROWS, share)

    ids = row_routes.reshape(8, ROWS, 2)
    rank = ranks(ids, experts)
    group = jnp.arange(8)
    base = ((group // 2) ^ x) * 4 + (group % 2) * 2
    target = (ids * 16 + base[:, None, None] + rank).reshape(8 * ROWS, 2)
    slot = jnp.arange(16 * experts)
    select = jnp.sum((slot[:, None, None] == target[None]).astype(F32), axis=2).astype(BF16)
    sent = jnp.dot(select, attended.reshape(8 * ROWS, cols), preferred_element_type=F32)
    sent = sent.astype(BF16).reshape(experts, 16, cols)
    got = lax.all_to_all(sent, "exp", split_axis=0, concat_axis=0, tiled=True)
    got = got.transpose(1, 0, 2).reshape(16, width).astype(F32)
    normed = got * lax.rsqrt(jnp.mean(got * got, axis=-1, keepdims=True) + EPS) * ffn_gain
    normed = normed.astype(BF16)
    by_y = [normed] + [over_head(normed, 2 * k) for k in (1, 2, 3)]
    by_core = [over_head(piece, 1) for piece in by_y]

    hidden = gate_up(by_y + by_core, w_gate, w_up)
    ky = jnp.arange(4)
    theirs = down((y ^ ky) * 2 + (1 - c), hidden, w_down, share)
    theirs = over_head(theirs, 1)
    ours = down((y ^ ky) * 2 + c, hidden, w_down, share)
    theirs = theirs.reshape(4, 2, 4, 16, share)
    ours = ours.reshape(4, 2, 4, 16, share)
    both = (ours.astype(F32) + theirs[:, ::-1].astype(F32)).astype(BF16)
    got = [over_head(both[k], 2 * k) for k in (1, 2, 3)]
    place = jnp.stack([y, c]).astype(jnp.int32)
    results = final_sum(place, both, got)
    back = lax.all_to_all(results, "exp", split_axis=0, concat_axis=0, tiled=True)

    rank = ranks(routes, experts)
    target = routes * 8 + jnp.arange(STEPS)[:, None, None] * 2 + rank
    slot = jnp.arange(8 * experts)
    match = (target.reshape(STEPS * ROWS, 2, 1) == slot).astype(F32)
    mix = jnp.sum(match * route_weights.reshape(STEPS * ROWS, 2, 1), axis=1)
    mixed = jnp.dot(
        mix,
        back.reshape(8 * experts, share).astype(F32),
        precision=lax.Precision.HIGHEST,
        preferred_element_type=F32,
    )
    return attended_out, mixed.astype(BF16).reshape(STEPS, ROWS, share)


def solution(mesh):
    return jax.shard_map(
        shards,
        mesh=mesh,
        in_specs=(
            P(None, "exp", None),
            P(None, "exp", None, "head"),
            P(None, "head"),
            P("exp", "head", None, None),
            P("head"),
            P("head", "exp"),
            P(),
            P(None, "exp", None),
            P(None, "exp", None),
            P("exp", None, "head"),
            P("exp", None, "head"),
            P("exp", "head", None),
        ),
        out_specs=(P(None, "exp", "head"), P(None, "exp", "head")),
        check_vma=False,
    )
```

```python
import functools

import jax
import jax.numpy as jnp
from jax import lax
from jax.experimental import pallas as pl
from jax.experimental.pallas import tpu as pltpu
from jax.sharding import PartitionSpec as P

STEPS = 4
ROWS = 8
EPS = 1e-06
F32 = jnp.float32
BF16 = jnp.bfloat16
MIB = 1 << 20


def vmem_params(mib):
    return pltpu.CompilerParams(vmem_limit_bytes=mib * MIB)


def over_head(value, bits):
    return lax.ppermute(value, "head", [(i, i ^ bits) for i in range(8)])


def over_exp(value, bits):
    return lax.ppermute(value, "exp", [(i, i ^ bits) for i in range(16)])


def over_all(value, dest):
    pairs = []
    for i in range(128):
        y, c, z, x = i // 32, i // 16 % 2, i // 4 % 4, i % 4
        y, c, z, x = dest(y, c, z, x)
        pairs.append((i, ((y * 2 + c) * 4 + z) * 4 + x))
    return lax.ppermute(value, ("head", "exp"), pairs)


def readout_kernel(decay_ref, qkv_ref, state_ref, gain_ref, out_ref):
    head = pl.program_id(0)
    n, size = STEPS * ROWS, state_ref.shape[2]
    q, k, v = [qkv_ref[:, i].astype(F32).reshape(n, size).astype(BF16) for i in range(3)]
    row = lax.broadcasted_iota(jnp.int32, (n, size), 0)
    row_in = row % ROWS
    q_twice = jnp.concatenate([q, q], axis=1)
    carried = jnp.zeros((n, size), F32)
    for pair in range(ROWS // 2):
        wide = jnp.concatenate([state_ref[2 * pair, 0], state_ref[2 * pair + 1, 0]], axis=1)
        high = wide.astype(BF16)
        low = (wide - high.astype(F32)).astype(BF16)
        both = jnp.dot(
            q_twice, jnp.concatenate([high, low], axis=0), preferred_element_type=F32
        )
        carried = jnp.where(row_in == 2 * pair, both[:, :size], carried)
        carried = jnp.where(row_in == 2 * pair + 1, both[:, size:], carried)
    decay = [decay_ref[t, head] for t in range(STEPS)]
    run = decay[0]
    first = jnp.full((n, size), run, F32)
    for t in range(1, STEPS):
        run = run * decay[t]
        first = jnp.where(row // ROWS == t, run, first)
    row_t = lax.broadcasted_iota(jnp.int32, (n, n), 0)
    row_s = lax.broadcasted_iota(jnp.int32, (n, n), 1)
    mix = jnp.zeros((n, n), F32)
    for t in range(STEPS):
        run = None
        for s in range(t, -1, -1):
            here = row_t - row_s == (t - s) * ROWS
            mix = jnp.where(here & (row_s // ROWS == s), 1.0 if run is None else run, mix)
            run = decay[s] if run is None else run * decay[s]
    scores = lax.dot_general(q, k, (((1,), (1,)), ((), ())), preferred_element_type=F32)
    o = carried * first + jnp.dot(
        scores * mix,
        v.astype(F32),
        precision=lax.Precision.HIGHEST,
        preferred_element_type=F32,
    )
    o = o * lax.rsqrt(jnp.mean(o * o, axis=-1, keepdims=True) + EPS) * gain_ref[...]
    out_ref[...] = o.astype(BF16)


def readouts(step_qkv, decay, state, attn_gain):
    heads, size = state.shape[1], state.shape[2]
    return pl.pallas_call(
        readout_kernel,
        out_shape=jax.ShapeDtypeStruct((STEPS * ROWS, heads * size), BF16),
        grid=(heads,),
        in_specs=[
            pl.BlockSpec(memory_space=pltpu.SMEM),
            pl.BlockSpec((STEPS, 3, ROWS, size), lambda i: (0, 0, 0, i)),
            pl.BlockSpec((ROWS, 1, size, size), lambda i: (0, i, 0, 0)),
            pl.BlockSpec((1, size), lambda i: (0, i)),
        ],
        out_specs=pl.BlockSpec((STEPS * ROWS, size), lambda i: (0, i)),
        compiler_params=vmem_params(56),
        cost_estimate=pl.CostEstimate(
            flops=2 * STEPS * ROWS * ROWS * heads * size * size * 2,
            bytes_accessed=state.size * 4,
            transcendentals=0,
        ),
        name="readout",
    )(decay, step_qkv.transpose(0, 2, 1, 3), state, attn_gain.reshape(1, -1))


def attend_kernel(place_ref, own_ref, got1_ref, got2_ref, got3_ref, *refs):
    hidden_refs, attended_ref, sent_ref = refs[:4], refs[4], refs[5]
    x, z = place_ref[0], place_ref[1]
    rows = []
    for k in range(4):
        total = own_ref[k].astype(F32) + got1_ref[k].astype(F32)
        total += got2_ref[k].astype(F32) + got3_ref[k].astype(F32)
        total += hidden_refs[k][:, : total.shape[1]].astype(F32)
        rows.append(total.astype(BF16))
        attended_ref[k] = rows[k]
    rows = jnp.concatenate(rows, axis=0)
    n = rows.shape[0]
    cols = rows.shape[1]
    names = jnp.concatenate([r[:, cols:].astype(F32) for r in hidden_refs], axis=0)
    across = names.T
    down_i = lax.broadcasted_iota(jnp.int32, (n, n), 0)
    over_i = lax.broadcasted_iota(jnp.int32, (n, n), 1)
    earlier = (down_i // ROWS == over_i // ROWS) & (down_i < over_i)
    slot = lax.broadcasted_iota(jnp.int32, (256, n), 0)
    lane = lax.broadcasted_iota(jnp.int32, (1, n), 1)
    base = lax.bitwise_xor(lane // 16, x) * 4 + lane // ROWS % 2 * 2
    select = jnp.zeros((256, n), F32)
    for j in range(2):
        mine = across[j : j + 1, :]
        rank = jnp.zeros((1, n), F32)
        for other in range(2):
            same = (names[:, other : other + 1] == mine) & earlier
            rank += jnp.sum(same.astype(F32), axis=0, keepdims=True)
        expert = mine.astype(jnp.int32)
        kz = lax.bitwise_xor(expert // 4, z)
        kx = lax.bitwise_xor(expert % 4, x)
        target = (kz * 4 + kx) * 16 + base + rank.astype(jnp.int32)
        select += (slot == target).astype(F32)
    sent = jnp.dot(select.astype(BF16), rows, preferred_element_type=F32).astype(BF16)
    for k in range(16):
        sent_ref[k // 4, k % 4] = sent[16 * k : 16 * k + 16]


def attend(place, own, got, hidden):
    cols = own.shape[-1]
    return pl.pallas_call(
        attend_kernel,
        out_shape=(
            jax.ShapeDtypeStruct((4, 16, cols), BF16),
            jax.ShapeDtypeStruct((4, 4, 16, cols), BF16),
        ),
        in_specs=[pl.BlockSpec(memory_space=pltpu.SMEM)]
        + [pl.BlockSpec(memory_space=pltpu.VMEM)] * 8,
        out_specs=[pl.BlockSpec(memory_space=pltpu.VMEM)] * 2,
        compiler_params=vmem_params(16),
        cost_estimate=pl.CostEstimate(flops=1 << 23, bytes_accessed=1 << 20, transcendentals=0),
        name="attend",
    )(place, own, *got, *hidden)


def norm_kernel(place_ref, gain_ref, *refs):
    got_refs, out_ref = refs[:4], refs[4]
    x, z = place_ref[0], place_ref[1]
    cols = got_refs[0].shape[2]
    total = jnp.zeros((16, cols), F32)
    for ref in got_refs:
        for kz in range(4):
            value = ref[kz].astype(F32)
            total += value * value
    mean = jnp.sum(total, axis=-1, keepdims=True) / (16 * cols)
    scale = lax.rsqrt(mean + EPS)
    for kx, ref in enumerate(got_refs):
        for kz in range(4):
            block = lax.bitwise_xor(z, kz) * 4 + lax.bitwise_xor(x, kx)
            at = pl.ds(pl.multiple_of(block * cols, 128), cols)
            out_ref[:, at] = (ref[kz].astype(F32) * scale * gain_ref[:, at]).astype(BF16)


def norm(place, gain, got):
    cols = got[0].shape[2]
    return pl.pallas_call(
        norm_kernel,
        out_shape=jax.ShapeDtypeStruct((16, 16 * cols), BF16),
        in_specs=[pl.BlockSpec(memory_space=pltpu.SMEM)]
        + [pl.BlockSpec(memory_space=pltpu.VMEM)] * 5,
        out_specs=pl.BlockSpec(memory_space=pltpu.VMEM),
        compiler_params=vmem_params(16),
        cost_estimate=pl.CostEstimate(flops=1 << 20, bytes_accessed=1 << 19, transcendentals=0),
        name="norm",
    )(place, gain.reshape(1, -1), *got)


def gate_up_kernel(*refs):
    x_refs, (gate_ref, up_ref, out_ref, gate_acc, up_acc) = refs[:8], refs[8:]
    step = pl.program_id(0)
    x = jnp.concatenate([r[...] for r in x_refs], axis=0)
    across = (((1,), (1,)), ((), ()))
    gate = lax.dot_general(x, gate_ref[0], across, preferred_element_type=F32)
    up = lax.dot_general(x, up_ref[0], across, preferred_element_type=F32)

    @pl.when(step == 0)
    def _():
        gate_acc[...] = gate
        up_acc[...] = up

    @pl.when(step > 0)
    def _():
        gate_acc[...] += gate
        up_acc[...] += up

    @pl.when(step == pl.num_programs(0) - 1)
    def _():
        g = gate_acc[...]
        out_ref[...] = (g / (1.0 + jnp.exp(-g)) * up_acc[...]).astype(BF16)


def gate_up(pieces, w_gate, w_up):
    slots, width = pieces[0].shape
    hidden = w_gate.shape[2]
    chunk = width // 8
    rows = slots * len(pieces)
    return pl.pallas_call(
        gate_up_kernel,
        out_shape=jax.ShapeDtypeStruct((rows, hidden), BF16),
        grid=(width // chunk,),
        in_specs=[pl.BlockSpec((slots, chunk), lambda i: (0, i))] * len(pieces)
        + [pl.BlockSpec((1, hidden, chunk), lambda i: (0, 0, i))] * 2,
        out_specs=pl.BlockSpec((rows, hidden), lambda i: (0, 0)),
        scratch_shapes=[pltpu.VMEM((rows, hidden), F32)] * 2,
        compiler_params=vmem_params(56),
        cost_estimate=pl.CostEstimate(
            flops=4 * rows * width * hidden,
            bytes_accessed=4 * width * hidden,
            transcendentals=rows * hidden,
        ),
        name="gate_up",
    )(*pieces, w_gate.transpose(0, 2, 1), w_up.transpose(0, 2, 1))


def down_kernel(place_ref, x_ref, w_ref, out_ref):
    out_ref[0] = jnp.dot(x_ref[...], w_ref[0], preferred_element_type=F32).astype(BF16)


def down(place, x, w_down, share):
    rows, hidden = x.shape
    parts = place.shape[0]
    return pl.pallas_call(
        down_kernel,
        out_shape=jax.ShapeDtypeStruct((parts, rows, share), BF16),
        grid_spec=pltpu.PrefetchScalarGridSpec(
            num_scalar_prefetch=1,
            grid=(parts,),
            in_specs=[
                pl.BlockSpec((rows, hidden), lambda i, p: (0, 0)),
                pl.BlockSpec((1, hidden, share), lambda i, p: (0, 0, p[i])),
            ],
            out_specs=pl.BlockSpec((1, rows, share), lambda i, p: (i, 0, 0)),
        ),
        compiler_params=vmem_params(56),
        cost_estimate=pl.CostEstimate(
            flops=2 * rows * hidden * share * parts,
            bytes_accessed=2 * hidden * share * parts,
            transcendentals=0,
        ),
        name="down",
    )(place, x, w_down)


def final_sum_kernel(place_ref, own_ref, got1_ref, got2_ref, got3_ref, out_ref):
    x, z, y, c = [place_ref[i] for i in range(4)]
    for ky in range(4):
        sums = []
        for kc in range(2):
            total = own_ref[0, kc, ky].astype(F32)
            for k, ref in ((1, got1_ref), (2, got2_ref), (3, got3_ref)):
                total += ref[kc, ky ^ k].astype(F32)
            sums.append(total)
        low = jnp.where(c == 0, sums[0], sums[1])
        high = jnp.where(c == 0, sums[1], sums[0])
        for source in range(4):
            at = slice(4 * source, 4 * source + 4)
            block = jnp.concatenate([low[at], high[at]], axis=0)
            kz = lax.bitwise_xor(lax.bitwise_xor(y, ky), z)
            out_ref[kz, lax.bitwise_xor(x, source)] = block.astype(BF16)


def final_sum(place, own, got):
    share = own.shape[-1]
    return pl.pallas_call(
        final_sum_kernel,
        out_shape=jax.ShapeDtypeStruct((4, 4, 8, share), BF16),
        in_specs=[pl.BlockSpec(memory_space=pltpu.SMEM)]
        + [pl.BlockSpec(memory_space=pltpu.VMEM)] * 4,
        out_specs=pl.BlockSpec(memory_space=pltpu.VMEM),
        compiler_params=vmem_params(16),
        cost_estimate=pl.CostEstimate(flops=1 << 20, bytes_accessed=1 << 20, transcendentals=0),
        name="final_sum",
    )(place, own, *got)


def mix_kernel(place_ref, routes_ref, weights_ref, *refs):
    back_refs, out_ref = refs[:4], refs[4]
    x, z = place_ref[0], place_ref[1]
    n = STEPS * ROWS
    names = routes_ref[...]
    weights = weights_ref[...]
    down_i = lax.broadcasted_iota(jnp.int32, (n, n), 0)
    over_i = lax.broadcasted_iota(jnp.int32, (n, n), 1)
    earlier = (down_i // ROWS == over_i // ROWS) & (over_i < down_i)
    across = names.T
    slot = lax.broadcasted_iota(jnp.int32, (n, 128), 1)
    step = lax.broadcasted_iota(jnp.int32, (n, 1), 0) // ROWS
    mix = jnp.zeros((n, 128), F32)
    for j in range(2):
        mine = names[:, j : j + 1]
        rank = jnp.zeros((n, 1), F32)
        for other in range(2):
            same = (across[other : other + 1, :] == mine) & earlier
            rank += jnp.sum(same.astype(F32), axis=1, keepdims=True)
        expert = mine.astype(jnp.int32)
        kz = lax.bitwise_xor(expert // 4, z)
        kx = lax.bitwise_xor(expert % 4, x)
        target = (kx * 4 + kz) * 8 + 2 * step + rank.astype(jnp.int32)
        mix += jnp.where(slot == target, weights[:, j : j + 1], 0.0)
    back = jnp.concatenate(
        [ref[kz].astype(F32) for ref in back_refs for kz in range(4)], axis=0
    )
    out_ref[...] = jnp.dot(
        mix, back, precision=lax.Precision.HIGHEST, preferred_element_type=F32
    ).astype(BF16)


def mixed_rows(place, routes, weights, back):
    share = back[0].shape[-1]
    n = STEPS * ROWS
    routes = jnp.pad(routes.astype(F32).reshape(n, 2), ((0, 0), (0, 126)))
    weights = jnp.pad(weights.reshape(n, 2), ((0, 0), (0, 126)))
    return pl.pallas_call(
        mix_kernel,
        out_shape=jax.ShapeDtypeStruct((n, share), BF16),
        in_specs=[pl.BlockSpec(memory_space=pltpu.SMEM)]
        + [pl.BlockSpec(memory_space=pltpu.VMEM)] * 6,
        out_specs=pl.BlockSpec(memory_space=pltpu.VMEM),
        compiler_params=vmem_params(16),
        cost_estimate=pl.CostEstimate(flops=1 << 24, bytes_accessed=1 << 19, transcendentals=0),
        name="mix",
    )(place, routes, weights, *back)


def shards(
    hidden_in,
    step_qkv,
    decay_rates,
    kv_state,
    attn_gain,
    out_proj,
    ffn_gain,
    routes,
    route_weights,
    w_gate,
    w_up,
    w_down,
):
    width = hidden_in.shape[2]
    cols = width // 16
    share = width // 8
    head, exp = lax.axis_index("head"), lax.axis_index("exp")
    y, c, z, x = head // 2, head % 2, exp // 4, exp % 4
    place = jnp.stack([x, z, y, c]).astype(jnp.int32)

    readout = readouts(step_qkv, decay_rates, kv_state, attn_gain)
    half_a, half_b = readout[: 2 * ROWS], readout[2 * ROWS :]
    by_z = jnp.stack([half_a] + [over_exp(half_a, 4 * k) for k in (1, 2, 3)], 0)
    by_x = jnp.stack([half_b] + [over_exp(half_b, k) for k in (1, 2, 3)], 0)
    all_a = [by_z] + [over_exp(by_z, k) for k in (1, 2, 3)]
    all_b = [by_x] + [over_exp(by_x, 4 * k) for k in (1, 2, 3)]
    depth = readout.shape[1]

    pair_rows = lax.dynamic_slice(hidden_in, (2 * c, 0, y * 4 * cols), (2, ROWS, 4 * cols))
    pair_rows = pair_rows.reshape(2 * ROWS, 4 * cols)
    pair_routes = lax.dynamic_slice(routes, (2 * c, 0, 0), (2, ROWS, 2)).reshape(2 * ROWS, 2)
    pair_routes = jnp.pad(pair_routes.astype(BF16), ((0, 0), (0, 126)))
    blocks = []
    for k in range(4):
        block = lax.dynamic_slice(pair_rows, (0, (x ^ k) * cols), (2 * ROWS, cols))
        blocks.append(jnp.concatenate([block, pair_routes], axis=1))
    blocks, all_b[1] = lax.optimization_barrier((blocks, all_b[1]))
    hidden_rows = [
        over_all(blocks[k], lambda y, c, z, x, k=k: (z, c, y, x ^ k)) for k in range(4)
    ]

    def project(pieces):
        rows = jnp.concatenate([p.reshape(8 * ROWS, depth) for p in pieces], axis=0)
        out = jnp.dot(rows, out_proj, preferred_element_type=F32).astype(BF16)
        return out.reshape(4, 4, 2 * ROWS, cols)

    part_a = project(all_a)
    part_b = project(all_b).transpose(1, 0, 2, 3)
    mine = jnp.where(c == 0, part_a, part_b)
    other = jnp.where(c == 0, part_b, part_a)
    mine = (mine.astype(F32) + over_head(other, 1).astype(F32)).astype(BF16)

    def for_y(k):
        return lax.dynamic_index_in_dim(mine, y ^ k ^ z, 1, keepdims=False)

    got = [over_head(for_y(k), 2 * k) for k in (1, 2, 3)]
    attended, sent = attend(place, for_y(0), got, hidden_rows)

    by_kz = [sent[0]] + [over_exp(sent[k], 4 * k) for k in (1, 2, 3)]
    by_kx = [jnp.stack([by_kz[kz][kx] for kz in range(4)], 0) for kx in range(4)]
    by_kx = by_kx[:1] + [over_exp(by_kx[k], k) for k in (1, 2, 3)]
    normed = norm(place, ffn_gain, by_kx)
    by_y = [normed] + [over_head(normed, 2 * k) for k in (1, 2, 3)]

    attended, by_y[1] = lax.optimization_barrier((attended, by_y[1]))
    by_core = [over_head(piece, 1) for piece in by_y]
    pieces = []
    for k in range(4):
        source = (2 * c + x % 2) ^ k
        block = lax.dynamic_index_in_dim(attended, source ^ x, 0, keepdims=False)
        pieces.append(
            over_all(block, lambda y, c, z, x, k=k: (z, x // 2, y, (2 * c + x % 2) ^ k))
        )
    pieces = jnp.stack(pieces, 0)
    ordered = [lax.dynamic_index_in_dim(pieces, j ^ x, 0, keepdims=False) for j in range(4)]
    attended_out = jnp.concatenate(
        [jnp.concatenate(ordered[:2], axis=1), jnp.concatenate(ordered[2:], axis=1)], axis=0
    ).reshape(STEPS, ROWS, share)

    hidden = gate_up(by_y + by_core, w_gate, w_up)
    ky = jnp.arange(4)
    theirs = down((y ^ ky) * 2 + (1 - c), hidden, w_down, share)
    theirs = over_head(theirs, 1)
    ours = down((y ^ ky) * 2 + c, hidden, w_down, share)
    theirs = theirs.reshape(4, 2, 4, 16, share)
    ours = ours.reshape(4, 2, 4, 16, share)
    both = (ours.astype(F32) + theirs[:, ::-1].astype(F32)).astype(BF16)
    got = [over_head(both[k], 2 * k) for k in (1, 2, 3)]
    results = final_sum(place, both, got)
    by_kz = [results[0]] + [over_exp(results[k], 4 * k) for k in (1, 2, 3)]
    by_kx = [jnp.stack([by_kz[kz][kx] for kz in range(4)], 0) for kx in range(4)]
    by_kx = by_kx[:1] + [over_exp(by_kx[k], k) for k in (1, 2, 3)]
    mixed = mixed_rows(place, routes, route_weights, by_kx)
    return attended_out, mixed.reshape(STEPS, ROWS, share)


def solution(mesh):
    return jax.shard_map(
        shards,
        mesh=mesh,
        in_specs=(
            P(None, "exp", None),
            P(None, "exp", None, "head"),
            P(None, "head"),
            P("exp", "head", None, None),
            P("head"),
            P("head", "exp"),
            P(),
            P(None, "exp", None),
            P(None, "exp", None),
            P("exp", None, "head"),
            P("exp", None, "head"),
            P("exp", "head", None),
        ),
        out_specs=(P(None, "exp", "head"), P(None, "exp", "head")),
        check_vma=False,
    )
```

```python
import functools

import jax
import jax.numpy as jnp
from jax import lax
from jax.experimental import pallas as pl
from jax.experimental.pallas import tpu as pltpu
from jax.sharding import PartitionSpec as P

STEPS = 4
ROWS = 8
EPS = 1e-06
F32 = jnp.float32
BF16 = jnp.bfloat16
MIB = 1 << 20


def vmem_params(mib):
    return pltpu.CompilerParams(vmem_limit_bytes=mib * MIB)


def over_head(value, bits):
    return lax.ppermute(value, "head", [(i, i ^ bits) for i in range(8)])


def over_exp(value, bits):
    return lax.ppermute(value, "exp", [(i, i ^ bits) for i in range(16)])


def over_all(value, dest):
    pairs = []
    for i in range(128):
        y, c, z, x = i // 32, i // 16 % 2, i // 4 % 4, i % 4
        y, c, z, x = dest(y, c, z, x)
        pairs.append((i, ((y * 2 + c) * 4 + z) * 4 + x))
    return lax.ppermute(value, ("head", "exp"), pairs)


def bf16_parts(value, count):
    parts = []
    for _ in range(count - 1):
        parts.append(value.astype(BF16))
        value = value - parts[-1].astype(F32)
    return parts + [value.astype(BF16)]


def readout_kernel(decay_ref, qkv_ref, state_ref, gain_ref, first_out_ref, last_out_ref):
    n, size = STEPS * ROWS, state_ref.shape[2]
    heads = state_ref.shape[1]
    row = lax.broadcasted_iota(jnp.int32, (n, size), 0)
    row_in = row % ROWS
    row_t = lax.broadcasted_iota(jnp.int32, (n, n), 0)
    row_s = lax.broadcasted_iota(jnp.int32, (n, n), 1)
    for h in range(heads):
        lanes = slice(h * size, (h + 1) * size)
        q, k, v = [
            qkv_ref[:, i, :, lanes].astype(F32).reshape(n, size).astype(BF16) for i in range(3)
        ]
        q_twice = jnp.concatenate([q, q], axis=1)
        carried = jnp.zeros((n, size), F32)
        for pair in range(ROWS // 2):
            wide = jnp.concatenate([state_ref[2 * pair, h], state_ref[2 * pair + 1, h]], axis=1)
            both = jnp.dot(
                q_twice, jnp.concatenate(bf16_parts(wide, 2), axis=0), preferred_element_type=F32
            )
            carried = jnp.where(row_in == 2 * pair, both[:, :size], carried)
            carried = jnp.where(row_in == 2 * pair + 1, both[:, size:], carried)
        decay = [decay_ref[t, pl.program_id(0) * heads + h] for t in range(STEPS)]
        run = decay[0]
        first = jnp.full((n, size), run, F32)
        for t in range(1, STEPS):
            run = run * decay[t]
            first = jnp.where(row // ROWS == t, run, first)
        mix = jnp.zeros((n, n), F32)
        for t in range(STEPS):
            run = None
            for s in range(t, -1, -1):
                here = row_t - row_s == (t - s) * ROWS
                mix = jnp.where(here & (row_s // ROWS == s), 1.0 if run is None else run, mix)
                run = decay[s] if run is None else run * decay[s]
        scores = lax.dot_general(q, k, (((1,), (1,)), ((), ())), preferred_element_type=F32)
        o = carried * first + jnp.dot(
            jnp.concatenate(bf16_parts(scores * mix, 2), axis=1),
            jnp.concatenate([v, v], axis=0),
            preferred_element_type=F32,
        )
        o = o * lax.rsqrt(jnp.mean(o * o, axis=-1, keepdims=True) + EPS) * gain_ref[:, lanes]
        o = o.astype(BF16)
        first_out_ref[:, lanes] = o[: n // 2]
        last_out_ref[:, lanes] = o[n // 2 :]


def readouts(step_qkv, decay, state, attn_gain):
    heads, size = state.shape[1], state.shape[2]
    at_once = min(heads, 4)
    half = STEPS * ROWS // 2
    return pl.pallas_call(
        readout_kernel,
        out_shape=[jax.ShapeDtypeStruct((half, heads * size), BF16)] * 2,
        grid=(heads // at_once,),
        in_specs=[
            pl.BlockSpec(memory_space=pltpu.SMEM),
            pl.BlockSpec((STEPS, 3, ROWS, at_once * size), lambda i: (0, 0, 0, i)),
            pl.BlockSpec((ROWS, at_once, size, size), lambda i: (0, i, 0, 0)),
            pl.BlockSpec((1, at_once * size), lambda i: (0, i)),
        ],
        out_specs=[pl.BlockSpec((half, at_once * size), lambda i: (0, i))] * 2,
        compiler_params=vmem_params(56),
        cost_estimate=pl.CostEstimate(
            flops=2 * STEPS * ROWS * ROWS * heads * size * size * 2,
            bytes_accessed=state.size * 4,
            transcendentals=0,
        ),
        name="readout",
    )(decay, step_qkv.transpose(0, 2, 1, 3), state, attn_gain.reshape(1, -1))


def attend_kernel(place_ref, own_ref, got1_ref, got2_ref, got3_ref, *refs):
    hidden_refs, attended_ref, sent_ref = refs[:4], refs[4], refs[5]
    x, z = place_ref[0], place_ref[1]
    rows = []
    for k in range(4):
        total = own_ref[k].astype(F32) + got1_ref[k].astype(F32)
        total += got2_ref[k].astype(F32) + got3_ref[k].astype(F32)
        total += hidden_refs[k][:, : total.shape[1]].astype(F32)
        rows.append(total.astype(BF16))
        attended_ref[k] = rows[k]
    rows = jnp.concatenate(rows, axis=0)
    n = rows.shape[0]
    cols = rows.shape[1]
    names = jnp.concatenate([r[:, cols:].astype(F32) for r in hidden_refs], axis=0)
    across = names.T
    down_i = lax.broadcasted_iota(jnp.int32, (n, n), 0)
    over_i = lax.broadcasted_iota(jnp.int32, (n, n), 1)
    earlier = (down_i // ROWS == over_i // ROWS) & (down_i < over_i)
    slot = lax.broadcasted_iota(jnp.int32, (256, n), 0)
    lane = lax.broadcasted_iota(jnp.int32, (1, n), 1)
    base = lax.bitwise_xor(lane // 16, x) * 4 + lane // ROWS % 2 * 2
    select = jnp.zeros((256, n), F32)
    for j in range(2):
        mine = across[j : j + 1, :]
        rank = jnp.zeros((1, n), F32)
        for other in range(2):
            same = (names[:, other : other + 1] == mine) & earlier
            rank += jnp.sum(same.astype(F32), axis=0, keepdims=True)
        expert = mine.astype(jnp.int32)
        kz = lax.bitwise_xor(expert // 4, z)
        kx = lax.bitwise_xor(expert % 4, x)
        target = (kz * 4 + kx) * 16 + base + rank.astype(jnp.int32)
        select += (slot == target).astype(F32)
    sent = jnp.dot(select.astype(BF16), rows, preferred_element_type=F32).astype(BF16)
    for k in range(16):
        sent_ref[k // 4, k % 4] = sent[16 * k : 16 * k + 16]


def attend(place, own, got, hidden):
    cols = own.shape[-1]
    return pl.pallas_call(
        attend_kernel,
        out_shape=(
            jax.ShapeDtypeStruct((4, 16, cols), BF16),
            jax.ShapeDtypeStruct((4, 4, 16, cols), BF16),
        ),
        in_specs=[pl.BlockSpec(memory_space=pltpu.SMEM)]
        + [pl.BlockSpec(memory_space=pltpu.VMEM)] * 8,
        out_specs=[pl.BlockSpec(memory_space=pltpu.VMEM)] * 2,
        compiler_params=vmem_params(16),
        cost_estimate=pl.CostEstimate(flops=1 << 23, bytes_accessed=1 << 20, transcendentals=0),
        name="attend",
    )(place, own, *got, *hidden)


def norm_kernel(place_ref, gain_ref, *refs):
    got_refs, out_ref = refs[:4], refs[4]
    x, z = place_ref[0], place_ref[1]
    cols = got_refs[0].shape[2]
    total = jnp.zeros((16, cols), F32)
    for ref in got_refs:
        for kz in range(4):
            value = ref[kz].astype(F32)
            total += value * value
    mean = jnp.sum(total, axis=-1, keepdims=True) / (16 * cols)
    scale = lax.rsqrt(mean + EPS)
    for kx, ref in enumerate(got_refs):
        for kz in range(4):
            block = lax.bitwise_xor(z, kz) * 4 + lax.bitwise_xor(x, kx)
            at = pl.ds(pl.multiple_of(block * cols, 128), cols)
            out_ref[:, at] = (ref[kz].astype(F32) * scale * gain_ref[:, at]).astype(BF16)


def norm(place, gain, got):
    cols = got[0].shape[2]
    return pl.pallas_call(
        norm_kernel,
        out_shape=jax.ShapeDtypeStruct((16, 16 * cols), BF16),
        in_specs=[pl.BlockSpec(memory_space=pltpu.SMEM)]
        + [pl.BlockSpec(memory_space=pltpu.VMEM)] * 5,
        out_specs=pl.BlockSpec(memory_space=pltpu.VMEM),
        compiler_params=vmem_params(16),
        cost_estimate=pl.CostEstimate(flops=1 << 20, bytes_accessed=1 << 19, transcendentals=0),
        name="norm",
    )(place, gain.reshape(1, -1), *got)


def fetch_kernel(after_ref, *refs):
    sems = refs[-1]
    copies = [
        pltpu.make_async_copy(refs[i], refs[3 + i], sems.at[i]) for i in range(3)
    ]
    for copy in copies:
        copy.start()
    for copy in copies:
        copy.wait()


def fetch(after, *weights):
    return pl.pallas_call(
        fetch_kernel,
        out_shape=[pltpu.VMEM(w.shape, w.dtype) for w in weights],
        in_specs=[pl.BlockSpec(memory_space=pl.ANY)] + [pl.BlockSpec(memory_space=pltpu.HBM)] * 3,
        out_specs=[pl.BlockSpec(memory_space=pltpu.VMEM)] * 3,
        scratch_shapes=[pltpu.SemaphoreType.DMA((3,))],
        compiler_params=vmem_params(30),
        cost_estimate=pl.CostEstimate(
            flops=0, bytes_accessed=sum(2 * w.size for w in weights), transcendentals=0
        ),
        name="fetch",
    )(after, *weights)


def hidden_kernel(place_ref, *refs):
    x_refs, (gate_ref, up_ref, down_ref, hidden_ref, theirs_ref) = refs[:8], refs[8:]
    share = theirs_ref.shape[2]
    y, c = place_ref[2], place_ref[3]
    x = jnp.concatenate([r[...] for r in x_refs], axis=0)
    across = (((1,), (1,)), ((), ()))
    gate = lax.dot_general(gate_ref[...], x, across, preferred_element_type=F32)
    up = lax.dot_general(up_ref[...], x, across, preferred_element_type=F32)
    hidden = (gate / (1.0 + jnp.exp(-gate)) * up).T.astype(BF16)
    hidden_ref[...] = hidden
    for k in range(4):
        block = lax.bitwise_xor(y, k) * 2 + (1 - c)
        at = pl.ds(pl.multiple_of(block * share, 128), share)
        theirs_ref[k] = jnp.dot(hidden, down_ref[:, at], preferred_element_type=F32).astype(BF16)


def hidden_units(place, pieces, gate, up, down, share):
    units = gate.shape[0]
    rows = sum(p.shape[0] for p in pieces)
    return pl.pallas_call(
        hidden_kernel,
        out_shape=(
            jax.ShapeDtypeStruct((rows, units), BF16),
            jax.ShapeDtypeStruct((4, rows, share), BF16),
        ),
        in_specs=[pl.BlockSpec(memory_space=pltpu.SMEM)]
        + [pl.BlockSpec(memory_space=pltpu.VMEM)] * (len(pieces) + 3),
        out_specs=[pl.BlockSpec(memory_space=pltpu.VMEM)] * 2,
        compiler_params=vmem_params(30),
        cost_estimate=pl.CostEstimate(
            flops=5 * rows * gate.size, bytes_accessed=1 << 20, transcendentals=rows * units
        ),
        name="hidden_units",
    )(place, *pieces, gate, up, down)


def down_kernel(place_ref, hidden_ref, down_ref, theirs_ref, out_ref):
    share = out_ref.shape[2]
    y, c = place_ref[2], place_ref[3]
    half = hidden_ref.shape[0] // 2
    for k in range(4):
        block = lax.bitwise_xor(y, k) * 2 + c
        at = pl.ds(pl.multiple_of(block * share, 128), share)
        ours = jnp.dot(hidden_ref[...], down_ref[:, at], preferred_element_type=F32)
        out_ref[k, :half] = (ours[:half] + theirs_ref[k, half:].astype(F32)).astype(BF16)
        out_ref[k, half:] = (ours[half:] + theirs_ref[k, :half].astype(F32)).astype(BF16)


def down(place, hidden, weight, theirs):
    return pl.pallas_call(
        down_kernel,
        out_shape=jax.ShapeDtypeStruct(theirs.shape, BF16),
        in_specs=[pl.BlockSpec(memory_space=pltpu.SMEM)]
        + [pl.BlockSpec(memory_space=pltpu.VMEM)] * 3,
        out_specs=pl.BlockSpec(memory_space=pltpu.VMEM),
        compiler_params=vmem_params(30),
        cost_estimate=pl.CostEstimate(
            flops=hidden.shape[0] * weight.size, bytes_accessed=1 << 20, transcendentals=0
        ),
        name="down",
    )(place, hidden, weight, theirs)


def final_sum_kernel(place_ref, own_ref, got1_ref, got2_ref, got3_ref, out_ref):
    x, z, y, c = [place_ref[i] for i in range(4)]
    for ky in range(4):
        sums = []
        for kc in range(2):
            total = own_ref[0, kc, ky].astype(F32)
            for k, ref in ((1, got1_ref), (2, got2_ref), (3, got3_ref)):
                total += ref[kc, ky ^ k].astype(F32)
            sums.append(total)
        low = jnp.where(c == 0, sums[0], sums[1])
        high = jnp.where(c == 0, sums[1], sums[0])
        for source in range(4):
            at = slice(4 * source, 4 * source + 4)
            block = jnp.concatenate([low[at], high[at]], axis=0)
            kz = lax.bitwise_xor(lax.bitwise_xor(y, ky), z)
            out_ref[kz, lax.bitwise_xor(x, source)] = block.astype(BF16)


def final_sum(place, own, got):
    share = own.shape[-1]
    return pl.pallas_call(
        final_sum_kernel,
        out_shape=jax.ShapeDtypeStruct((4, 4, 8, share), BF16),
        in_specs=[pl.BlockSpec(memory_space=pltpu.SMEM)]
        + [pl.BlockSpec(memory_space=pltpu.VMEM)] * 4,
        out_specs=pl.BlockSpec(memory_space=pltpu.VMEM),
        compiler_params=vmem_params(16),
        cost_estimate=pl.CostEstimate(flops=1 << 20, bytes_accessed=1 << 20, transcendentals=0),
        name="final_sum",
    )(place, own, *got)


def mix_kernel(place_ref, routes_ref, weights_ref, *refs):
    back_refs, out_ref = refs[:4], refs[4]
    x, z = place_ref[0], place_ref[1]
    n = STEPS * ROWS
    names = routes_ref[...]
    weights = weights_ref[...]
    down_i = lax.broadcasted_iota(jnp.int32, (n, n), 0)
    over_i = lax.broadcasted_iota(jnp.int32, (n, n), 1)
    earlier = (down_i // ROWS == over_i // ROWS) & (over_i < down_i)
    across = names.T
    slot = lax.broadcasted_iota(jnp.int32, (n, 128), 1)
    step = lax.broadcasted_iota(jnp.int32, (n, 1), 0) // ROWS
    mix = jnp.zeros((n, 128), F32)
    for j in range(2):
        mine = names[:, j : j + 1]
        rank = jnp.zeros((n, 1), F32)
        for other in range(2):
            same = (across[other : other + 1, :] == mine) & earlier
            rank += jnp.sum(same.astype(F32), axis=1, keepdims=True)
        expert = mine.astype(jnp.int32)
        kz = lax.bitwise_xor(expert // 4, z)
        kx = lax.bitwise_xor(expert % 4, x)
        target = (kx * 4 + kz) * 8 + 2 * step + rank.astype(jnp.int32)
        mix += jnp.where(slot == target, weights[:, j : j + 1], 0.0)
    back = jnp.concatenate(
        [ref[kz].astype(F32) for ref in back_refs for kz in range(4)], axis=0
    ).astype(BF16)
    out_ref[...] = jnp.dot(
        jnp.concatenate(bf16_parts(mix, 3), axis=1),
        jnp.concatenate([back] * 3, axis=0),
        preferred_element_type=F32,
    ).astype(BF16)


def mixed_rows(place, routes, weights, back):
    share = back[0].shape[-1]
    n = STEPS * ROWS
    routes = jnp.pad(routes.astype(F32).reshape(n, 2), ((0, 0), (0, 126)))
    weights = jnp.pad(weights.reshape(n, 2), ((0, 0), (0, 126)))
    return pl.pallas_call(
        mix_kernel,
        out_shape=jax.ShapeDtypeStruct((n, share), BF16),
        in_specs=[pl.BlockSpec(memory_space=pltpu.SMEM)]
        + [pl.BlockSpec(memory_space=pltpu.VMEM)] * 6,
        out_specs=pl.BlockSpec(memory_space=pltpu.VMEM),
        compiler_params=vmem_params(16),
        cost_estimate=pl.CostEstimate(flops=1 << 24, bytes_accessed=1 << 19, transcendentals=0),
        name="mix",
    )(place, routes, weights, *back)


def shards(
    hidden_in,
    step_qkv,
    decay_rates,
    kv_state,
    attn_gain,
    out_proj,
    ffn_gain,
    routes,
    route_weights,
    w_gate,
    w_up,
    w_down,
):
    width = hidden_in.shape[2]
    cols = width // 16
    share = width // 8
    head, exp = lax.axis_index("head"), lax.axis_index("exp")
    y, c, z, x = head // 2, head % 2, exp // 4, exp % 4
    place = jnp.stack([x, z, y, c]).astype(jnp.int32)

    half_a, half_b = readouts(step_qkv, decay_rates, kv_state, attn_gain)
    by_z = jnp.stack([half_a] + [over_exp(half_a, 4 * k) for k in (1, 2, 3)], 0)
    by_x = jnp.stack([half_b] + [over_exp(half_b, k) for k in (1, 2, 3)], 0)
    all_a = [by_z] + [over_exp(by_z, k) for k in (1, 2, 3)]
    all_b = [by_x] + [over_exp(by_x, 4 * k) for k in (1, 2, 3)]
    depth = half_a.shape[1]

    pair_rows = lax.dynamic_slice(hidden_in, (2 * c, 0, y * 4 * cols), (2, ROWS, 4 * cols))
    pair_rows = pair_rows.reshape(2 * ROWS, 4 * cols)
    pair_routes = lax.dynamic_slice(routes, (2 * c, 0, 0), (2, ROWS, 2)).reshape(2 * ROWS, 2)
    pair_routes = jnp.pad(pair_routes.astype(BF16), ((0, 0), (0, 126)))
    blocks = []
    for k in range(4):
        block = lax.dynamic_slice(pair_rows, (0, (x ^ k) * cols), (2 * ROWS, cols))
        blocks.append(jnp.concatenate([block, pair_routes], axis=1))
    blocks, all_b[1] = lax.optimization_barrier((blocks, all_b[1]))
    hidden_rows = [
        over_all(blocks[k], lambda y, c, z, x, k=k: (z, c, y, x ^ k)) for k in range(4)
    ]

    def project(pieces):
        rows = jnp.concatenate([p.reshape(8 * ROWS, depth) for p in pieces], axis=0)
        out = jnp.dot(rows, out_proj, preferred_element_type=F32).astype(BF16)
        return out.reshape(4, 4, 2 * ROWS, cols)

    hidden_rows, all_b = lax.optimization_barrier((hidden_rows, all_b))
    part_a = project(all_a)
    part_b = project(all_b).transpose(1, 0, 2, 3)
    mine = jnp.where(c == 0, part_a, part_b)
    other = jnp.where(c == 0, part_b, part_a)
    mine = (mine.astype(F32) + over_head(other, 1).astype(F32)).astype(BF16)

    def for_y(k):
        return lax.dynamic_index_in_dim(mine, y ^ k ^ z, 1, keepdims=False)

    got = [over_head(for_y(k), 2 * k) for k in (1, 2, 3)]
    attended, sent = attend(place, for_y(0), got, hidden_rows)

    by_kz = [sent[0]] + [over_exp(sent[k], 4 * k) for k in (1, 2, 3)]
    by_kx = [jnp.stack([by_kz[kz][kx] for kz in range(4)], 0) for kx in range(4)]
    by_kx = by_kx[:1] + [over_exp(by_kx[k], k) for k in (1, 2, 3)]
    normed = norm(place, ffn_gain, by_kx)
    by_y = [normed] + [over_head(normed, 2 * k) for k in (1, 2, 3)]

    by_core = [over_head(piece, 1) for piece in by_y]

    gate, up, down_weight = fetch(
        by_y[1], w_gate[0].swapaxes(0, 1), w_up[0].swapaxes(0, 1), w_down[0]
    )
    hidden, theirs = hidden_units(place, by_y + by_core, gate, up, down_weight, share)
    both = down(place, hidden, down_weight, over_head(theirs, 1))
    both = both.reshape(4, 2, 4, 16, share)
    got = [over_head(both[k], 2 * k) for k in (1, 2, 3)]

    attended, got[0] = lax.optimization_barrier((attended, got[0]))
    pieces = []
    for k in range(4):
        source = (2 * c + x % 2) ^ k
        block = lax.dynamic_index_in_dim(attended, source ^ x, 0, keepdims=False)
        pieces.append(
            over_all(block, lambda y, c, z, x, k=k: (z, x // 2, y, (2 * c + x % 2) ^ k))
        )
    pieces, got[1] = lax.optimization_barrier((pieces, got[1]))
    pieces = jnp.stack(pieces, 0)
    ordered = [lax.dynamic_index_in_dim(pieces, j ^ x, 0, keepdims=False) for j in range(4)]
    attended_out = jnp.concatenate(
        [jnp.concatenate(ordered[:2], axis=1), jnp.concatenate(ordered[2:], axis=1)], axis=0
    ).reshape(STEPS, ROWS, share)

    results = final_sum(place, both, got)
    by_kz = [results[0]] + [over_exp(results[k], 4 * k) for k in (1, 2, 3)]
    by_kx = [jnp.stack([by_kz[kz][kx] for kz in range(4)], 0) for kx in range(4)]
    by_kx = by_kx[:1] + [over_exp(by_kx[k], k) for k in (1, 2, 3)]
    mixed = mixed_rows(place, routes, route_weights, by_kx)
    return attended_out, mixed.reshape(STEPS, ROWS, share)


def solution(mesh):
    return jax.shard_map(
        shards,
        mesh=mesh,
        in_specs=(
            P(None, "exp", None),
            P(None, "exp", None, "head"),
            P(None, "head"),
            P("exp", "head", None, None),
            P("head"),
            P("head", "exp"),
            P(),
            P(None, "exp", None),
            P(None, "exp", None),
            P("exp", None, "head"),
            P("exp", None, "head"),
            P("exp", "head", None),
        ),
        out_specs=(P(None, "exp", "head"), P(None, "exp", "head")),
        check_vma=False,
    )
```

```python
import functools

import jax
import jax.numpy as jnp
from jax import lax
from jax.experimental import pallas as pl
from jax.experimental.pallas import tpu as pltpu
from jax.sharding import PartitionSpec as P

STEPS = 4
ROWS = 8
EPS = 1e-06
F32 = jnp.float32
BF16 = jnp.bfloat16
MIB = 1 << 20


def vmem_params(mib):
    return pltpu.CompilerParams(vmem_limit_bytes=mib * MIB)


def over_head(value, bits):
    return lax.ppermute(value, "head", [(i, i ^ bits) for i in range(8)])


def over_exp(value, bits):
    return lax.ppermute(value, "exp", [(i, i ^ bits) for i in range(16)])


def call(kernel, name, out_shape, place, *arrays, flops=0, limit=30, scratch=()):
    moved = sum(a.size * a.dtype.itemsize for a in arrays)
    result = pl.pallas_call(
        kernel,
        out_shape=out_shape,
        in_specs=[pl.BlockSpec(memory_space=pltpu.SMEM)]
        + [pl.BlockSpec(memory_space=pltpu.VMEM)] * len(arrays),
        out_specs=jax.tree.map(lambda _: pl.BlockSpec(memory_space=pltpu.VMEM), out_shape),
        scratch_shapes=scratch,
        compiler_params=vmem_params(limit),
        cost_estimate=pl.CostEstimate(flops=flops, bytes_accessed=moved, transcendentals=0),
        name=name,
    )(place, *arrays)
    return list(result) if isinstance(out_shape, list) else result


def xor(a, b):
    return lax.bitwise_xor(a, b)


def lanes_from(start, size):
    return pl.ds(pl.multiple_of(start, 128), size)


def columns_of(table):
    rows = lax.broadcasted_iota(jnp.int32, (ROWS, ROWS), 0)
    lanes = lax.broadcasted_iota(jnp.int32, (ROWS, ROWS), 1)
    return lax.dot_general(
        (rows == lanes).astype(F32),
        table,
        (((1,), (1,)), ((), ())),
        precision=lax.Precision.HIGHEST,
        preferred_element_type=F32,
    )


def widened(pair):
    lane = lax.broadcasted_iota(jnp.int32, (pair.shape[0], 128), 1)
    return jnp.where(lane == 0, pair[:, :1], jnp.where(lane == 1, pair[:, 1:2], 0.0))


def bf16_parts(value, count):
    parts = []
    for _ in range(count - 1):
        parts.append(value.astype(BF16))
        value = value - parts[-1].astype(F32)
    return parts + [value.astype(BF16)]


def readout_kernel(
    place_ref, decay_ref, routes_ref, hidden_ref, qkv_ref, state_ref, gain_ref, *out_refs
):
    first_refs, last_ref = out_refs[:4], out_refs[4]
    z, c = place_ref[1], place_ref[3]
    depth = last_ref.shape[1]
    quarter = hidden_ref.shape[2] // 4

    @pl.when(pl.program_id(0) == 0)
    def _():
        names = [columns_of(routes_ref[2 * c + t].astype(F32)) for t in range(2)]
        names = widened(jnp.concatenate(names, axis=0)).astype(BF16)
        for k, ref in enumerate(first_refs):
            at = lanes_from(xor(z, k) * quarter, quarter)
            rows = [hidden_ref[2 * c + t, :, at].astype(F32) for t in range(2)]
            ref[:, depth : depth + quarter] = jnp.concatenate(rows, axis=0).astype(BF16)
            ref[:, depth + quarter :] = names

    n, size = STEPS * ROWS, state_ref.shape[2]
    heads = state_ref.shape[1]
    row = lax.broadcasted_iota(jnp.int32, (n, size), 0)
    row_in = row % ROWS
    row_t = lax.broadcasted_iota(jnp.int32, (n, n), 0)
    row_s = lax.broadcasted_iota(jnp.int32, (n, n), 1)
    for h in range(heads):
        lanes = slice(h * size, (h + 1) * size)
        q, k, v = [
            qkv_ref[:, i, :, lanes].astype(F32).reshape(n, size).astype(BF16) for i in range(3)
        ]
        q_twice = jnp.concatenate([q, q], axis=1)
        carried = jnp.zeros((n, size), F32)
        for pair in range(ROWS // 2):
            wide = jnp.concatenate([state_ref[2 * pair, h], state_ref[2 * pair + 1, h]], axis=1)
            both = jnp.dot(
                q_twice, jnp.concatenate(bf16_parts(wide, 2), axis=0), preferred_element_type=F32
            )
            carried = jnp.where(row_in == 2 * pair, both[:, :size], carried)
            carried = jnp.where(row_in == 2 * pair + 1, both[:, size:], carried)
        decay = [decay_ref[t, pl.program_id(0) * heads + h] for t in range(STEPS)]
        run = decay[0]
        first = jnp.full((n, size), run, F32)
        for t in range(1, STEPS):
            run = run * decay[t]
            first = jnp.where(row // ROWS == t, run, first)
        mix = jnp.zeros((n, n), F32)
        for t in range(STEPS):
            run = None
            for s in range(t, -1, -1):
                here = row_t - row_s == (t - s) * ROWS
                mix = jnp.where(here & (row_s // ROWS == s), 1.0 if run is None else run, mix)
                run = decay[s] if run is None else run * decay[s]
        scores = lax.dot_general(q, k, (((1,), (1,)), ((), ())), preferred_element_type=F32)
        o = carried * first + jnp.dot(
            jnp.concatenate(bf16_parts(scores * mix, 2), axis=1),
            jnp.concatenate([v, v], axis=0),
            preferred_element_type=F32,
        )
        o = o * lax.rsqrt(jnp.mean(o * o, axis=-1, keepdims=True) + EPS) * gain_ref[:, lanes]
        o = o.astype(BF16)
        at = lanes_from((pl.program_id(0) * heads + h) * size, size)
        for ref in first_refs:
            ref[:, at] = o[: n // 2]
        last_ref[:, at] = o[n // 2 :]


def readouts(place, step_qkv, decay, state, attn_gain, hidden_in, routes):
    heads, size = state.shape[1], state.shape[2]
    at_once = min(heads, 4)
    half = STEPS * ROWS // 2
    depth = heads * size
    packed = depth + hidden_in.shape[2] // 4 + 128
    whole = lambda i: (0, 0)
    return pl.pallas_call(
        readout_kernel,
        out_shape=[jax.ShapeDtypeStruct((half, packed), BF16)] * 4
        + [jax.ShapeDtypeStruct((half, depth), BF16)],
        grid=(heads // at_once,),
        in_specs=[
            pl.BlockSpec(memory_space=pltpu.SMEM),
            pl.BlockSpec(memory_space=pltpu.SMEM),
            pl.BlockSpec((STEPS, 2, ROWS), lambda i: (0, 0, 0)),
            pl.BlockSpec(hidden_in.shape, lambda i: (0, 0, 0)),
            pl.BlockSpec((STEPS, 3, ROWS, at_once * size), lambda i: (0, 0, 0, i)),
            pl.BlockSpec((ROWS, at_once, size, size), lambda i: (0, i, 0, 0)),
            pl.BlockSpec((1, at_once * size), lambda i: (0, i)),
        ],
        out_specs=[pl.BlockSpec((half, packed), whole)] * 4 + [pl.BlockSpec((half, depth), whole)],
        compiler_params=vmem_params(56),
        cost_estimate=pl.CostEstimate(
            flops=2 * STEPS * ROWS * ROWS * heads * size * size * 2,
            bytes_accessed=state.size * 4,
            transcendentals=0,
        ),
        name="readout",
    )(
        place,
        decay,
        routes.transpose(0, 2, 1),
        hidden_in,
        step_qkv.transpose(0, 2, 1, 3),
        state,
        attn_gain.reshape(1, -1),
    )


def spread_kernel(place_ref, *refs):
    in_refs, out_refs, held_ref = refs[:4], refs[4:8], refs[8]
    x, z, y = place_ref[0], place_ref[1], place_ref[2]
    wide = out_refs[0].shape[2]
    depth = wide - 128
    held = in_refs[0][:, depth:]
    for k in (1, 2, 3):
        held = jnp.where(xor(z, y) == k, in_refs[k][:, depth:], held)
    held_ref[...] = held
    cols = (held.shape[1] - 128) // 4
    for kx, ref in enumerate(out_refs):
        for kz in range(4):
            ref[kz, :, :depth] = in_refs[kz][:, :depth]
            if kz * 128 < cols:
                at = lanes_from(xor(x, kx) * cols + kz * 128, 128)
                ref[kz, :, depth:] = held_ref[:, at]
            else:
                ref[kz, :, depth:] = held[:, 4 * cols :]


def spread(place, pieces, depth):
    out = [jax.ShapeDtypeStruct((4, 16, depth + 128), BF16)] * 4
    scratch = [pltpu.VMEM((16, pieces[0].shape[1] - depth), BF16)]
    return call(spread_kernel, "spread", out, place, *pieces, scratch=scratch)


def project_kernel(place_ref, *refs):
    a_refs, b_refs, (weight_ref, mine_ref, other_ref) = refs[:4], refs[4:8], refs[8:]
    c = place_ref[3]
    depth = weight_ref.shape[0]

    def product(ref):
        rows = ref[:, :, :depth].reshape(64, depth)
        return jnp.dot(rows, weight_ref[...], preferred_element_type=F32).astype(BF16)

    for k in range(4):
        a, b = product(a_refs[k]), product(b_refs[k])
        for j in range(4):
            at = slice(16 * j, 16 * j + 16)

            @pl.when(c == 0)
            def _():
                mine_ref[k, j] = a[at]
                other_ref[j, k] = b[at]

            @pl.when(c == 1)
            def _():
                other_ref[k, j] = a[at]
                mine_ref[j, k] = b[at]


def project(place, all_a, all_b, weight):
    out = [jax.ShapeDtypeStruct((4, 4, 16, weight.shape[1]), BF16)] * 2
    flops = 2 * 512 * weight.size
    return call(project_kernel, "project", out, place, *all_a, *all_b, weight, flops=flops)


def by_y_kernel(place_ref, mine_ref, got_ref, *out_refs):
    z, y = place_ref[1], place_ref[2]
    for k, ref in enumerate(out_refs):
        kz = xor(xor(y, z), k)
        for kx in range(4):
            total = mine_ref[kx, kz].astype(F32) + got_ref[kx, kz].astype(F32)
            ref[kx] = total.astype(BF16)


def sums_by_y(place, mine, got):
    out = [jax.ShapeDtypeStruct((4, 16, mine.shape[3]), BF16)] * 4
    return call(by_y_kernel, "sums_by_y", out, place, mine, got)


def attend_kernel(place_ref, *refs):
    sum_refs, hidden_refs, out_refs = refs[:4], refs[4:8], refs[8:12]
    x, z = place_ref[0], place_ref[1]
    cols = out_refs[0].shape[2]
    depth = hidden_refs[0].shape[2] - 128
    rows, names = [], []
    for k in range(4):
        parts = [hidden_refs[k][j, :, depth:].astype(F32) for j in range(4)]
        names.append(parts[3])
        total = jnp.concatenate(parts[: cols // 128], axis=1)
        for ref in sum_refs:
            total += ref[k].astype(F32)
        rows.append(total.astype(BF16))
        for ref in out_refs:
            ref[4 + k] = rows[k]
    rows = jnp.concatenate(rows, axis=0)
    n = rows.shape[0]
    names = jnp.concatenate(names, axis=0)
    across = names.T
    down_i = lax.broadcasted_iota(jnp.int32, (n, n), 0)
    over_i = lax.broadcasted_iota(jnp.int32, (n, n), 1)
    earlier = (down_i // ROWS == over_i // ROWS) & (down_i < over_i)
    slot = lax.broadcasted_iota(jnp.int32, (256, n), 0)
    lane = lax.broadcasted_iota(jnp.int32, (1, n), 1)
    base = lax.bitwise_xor(lane // 16, x) * 4 + lane // ROWS % 2 * 2
    select = jnp.zeros((256, n), F32)
    for j in range(2):
        mine = across[j : j + 1, :]
        rank = jnp.zeros((1, n), F32)
        for other in range(2):
            same = (names[:, other : other + 1] == mine) & earlier
            rank += jnp.sum(same.astype(F32), axis=0, keepdims=True)
        expert = mine.astype(jnp.int32)
        kz = lax.bitwise_xor(expert // 4, z)
        kx = lax.bitwise_xor(expert % 4, x)
        target = (kz * 4 + kx) * 16 + base + rank.astype(jnp.int32)
        select += (slot == target).astype(F32)
    sent = jnp.dot(select.astype(BF16), rows, preferred_element_type=F32).astype(BF16)
    for k in range(16):
        out_refs[k // 4][k % 4] = sent[16 * k : 16 * k + 16]


def attend(place, sums, hidden):
    out = [jax.ShapeDtypeStruct((8,) + sums[0].shape[1:], BF16)] * 4
    return call(attend_kernel, "attend", out, place, *sums, *hidden, flops=1 << 23)


def turn_kernel(place_ref, *refs):
    in_refs, out_refs = refs[:4], refs[4:8]
    for kx, ref in enumerate(out_refs):
        for kz in range(4):
            ref[kz] = in_refs[kz][kx]
            ref[4 + kz] = in_refs[kz][4 + kx]


def turn(place, pieces):
    out = [jax.ShapeDtypeStruct(pieces[0].shape, BF16)] * 4
    return call(turn_kernel, "turn", out, place, *pieces)


def norm_kernel(place_ref, gain_ref, *refs):
    got_refs, out_refs = refs[:4], refs[4:8]
    x, z, y = place_ref[0], place_ref[1], place_ref[2]
    cols = got_refs[0].shape[2]
    total = jnp.zeros((16, cols), F32)
    for ref in got_refs:
        for kz in range(4):
            value = ref[kz].astype(F32)
            total += value * value
    mean = jnp.sum(total, axis=-1, keepdims=True) / (16 * cols)
    scale = lax.rsqrt(mean + EPS)
    for kx, ref in enumerate(got_refs):
        for kz in range(4):
            at = lanes_from((xor(z, kz) * 4 + xor(x, kx)) * cols, cols)
            value = (ref[kz].astype(F32) * scale * gain_ref[:, at]).astype(BF16)
            for out_ref in out_refs:
                out_ref[:, at] = value
        for k, out_ref in enumerate(out_refs):
            at = lanes_from((16 + xor(x, kx)) * cols, cols)
            out_ref[:, at] = ref[4 + xor(xor(z, y), k)]


def norm(place, gain, got):
    out = [jax.ShapeDtypeStruct((16, 20 * got[0].shape[2]), BF16)] * 4
    return call(norm_kernel, "norm", out, place, gain.reshape(1, -1), *got)


def owned_kernel(place_ref, *refs):
    own_refs, other_refs, out_ref = refs[:4], refs[4:8], refs[8]
    z, y, c = place_ref[1], place_ref[2], place_ref[3]
    share = out_ref.shape[1]
    start = own_refs[0].shape[1] - 2 * share
    at = lanes_from(start + c * share, share)
    for k in range(4):

        @pl.when(xor(z, y) == k)
        def _():
            out_ref[pl.ds(pl.multiple_of(16 * c, 16), 16), :] = own_refs[k][:, at]
            out_ref[pl.ds(pl.multiple_of(16 - 16 * c, 16), 16), :] = other_refs[k][:, at]


def owned(place, by_y, by_core, share):
    out = jax.ShapeDtypeStruct((STEPS * ROWS, share), BF16)
    return call(owned_kernel, "owned", out, place, *by_y, *by_core)


def fetch_kernel(after_ref, in_ref, out_ref, sem):
    copy = pltpu.make_async_copy(in_ref, out_ref, sem)
    copy.start()
    copy.wait()


def fetch(after, weight):
    return pl.pallas_call(
        fetch_kernel,
        out_shape=pltpu.VMEM(weight.shape, weight.dtype),
        in_specs=[pl.BlockSpec(memory_space=pl.ANY), pl.BlockSpec(memory_space=pltpu.HBM)],
        out_specs=pl.BlockSpec(memory_space=pltpu.VMEM),
        scratch_shapes=[pltpu.SemaphoreType.DMA],
        compiler_params=vmem_params(12),
        cost_estimate=pl.CostEstimate(
            flops=0, bytes_accessed=2 * weight.size, transcendentals=0
        ),
        name="fetch",
    )(after, weight)


def hidden_kernel(place_ref, *refs):
    x_refs, (gate_ref, up_ref, down_ref, hidden_ref, theirs_ref) = refs[:8], refs[8:]
    share = theirs_ref.shape[2]
    y, c = place_ref[2], place_ref[3]
    x = jnp.concatenate([r[:, : gate_ref.shape[1]] for r in x_refs], axis=0)
    across = (((1,), (1,)), ((), ()))
    gate = lax.dot_general(gate_ref[...], x, across, preferred_element_type=F32)
    up = lax.dot_general(up_ref[...], x, across, preferred_element_type=F32)
    hidden = (gate / (1.0 + jnp.exp(-gate)) * up).T.astype(BF16)
    hidden_ref[...] = hidden
    for k in range(4):
        block = lax.bitwise_xor(y, k) * 2 + (1 - c)
        at = pl.ds(pl.multiple_of(block * share, 128), share)
        theirs_ref[k] = jnp.dot(hidden, down_ref[:, at], preferred_element_type=F32).astype(BF16)


def hidden_units(place, pieces, gate, up, down_weight, share):
    units = gate.shape[0]
    rows = sum(p.shape[0] for p in pieces)
    out = [
        jax.ShapeDtypeStruct((rows, units), BF16),
        jax.ShapeDtypeStruct((4, rows, share), BF16),
    ]
    flops = 5 * rows * gate.size
    return call(
        hidden_kernel, "hidden_units", out, place, *pieces, gate, up, down_weight, flops=flops
    )


def down_kernel(place_ref, hidden_ref, down_ref, theirs_ref, *out_refs):
    share = out_refs[0].shape[1]
    y, c = place_ref[2], place_ref[3]
    half = hidden_ref.shape[0] // 2
    for k in range(4):
        block = lax.bitwise_xor(y, k) * 2 + c
        at = pl.ds(pl.multiple_of(block * share, 128), share)
        ours = jnp.dot(hidden_ref[...], down_ref[:, at], preferred_element_type=F32)
        out_refs[k][:half] = (ours[:half] + theirs_ref[k, half:].astype(F32)).astype(BF16)
        out_refs[k][half:] = (ours[half:] + theirs_ref[k, :half].astype(F32)).astype(BF16)


def down(place, hidden, weight, theirs):
    out = [jax.ShapeDtypeStruct(theirs.shape[1:], BF16)] * 4
    flops = hidden.shape[0] * weight.size
    return call(down_kernel, "down", out, place, hidden, weight, theirs, flops=flops)


def final_sum_kernel(place_ref, own_ref, got1_ref, got2_ref, got3_ref, out_ref):
    x, z, y, c = [place_ref[i] for i in range(4)]
    for ky in range(4):
        sums = []
        for kc in range(2):
            at = slice((kc * 4 + ky) * 16, (kc * 4 + ky) * 16 + 16)
            total = own_ref[at].astype(F32)
            for k, ref in ((1, got1_ref), (2, got2_ref), (3, got3_ref)):
                at = slice((kc * 4 + (ky ^ k)) * 16, (kc * 4 + (ky ^ k)) * 16 + 16)
                total += ref[at].astype(F32)
            sums.append(total)
        low = jnp.where(c == 0, sums[0], sums[1])
        high = jnp.where(c == 0, sums[1], sums[0])
        for source in range(4):
            at = slice(4 * source, 4 * source + 4)
            block = jnp.concatenate([low[at], high[at]], axis=0)
            kz = lax.bitwise_xor(lax.bitwise_xor(y, ky), z)
            out_ref[kz, lax.bitwise_xor(x, source)] = block.astype(BF16)


def final_sum(place, sums):
    out = jax.ShapeDtypeStruct((4, 4, 8, sums[0].shape[1]), BF16)
    return call(final_sum_kernel, "final_sum", out, place, *sums)


def mix_kernel(place_ref, routes_ref, weights_ref, *refs):
    back_refs, out_ref = refs[:4], refs[4]
    x, z = place_ref[0], place_ref[1]
    n = STEPS * ROWS
    names = [columns_of(routes_ref[t].astype(F32)) for t in range(STEPS)]
    names = widened(jnp.concatenate(names, axis=0))
    weights = [columns_of(weights_ref[t]) for t in range(STEPS)]
    weights = jnp.concatenate(weights, axis=0)
    down_i = lax.broadcasted_iota(jnp.int32, (n, n), 0)
    over_i = lax.broadcasted_iota(jnp.int32, (n, n), 1)
    earlier = (down_i // ROWS == over_i // ROWS) & (over_i < down_i)
    across = names.T
    slot = lax.broadcasted_iota(jnp.int32, (n, 128), 1)
    step = lax.broadcasted_iota(jnp.int32, (n, 1), 0) // ROWS
    mix = jnp.zeros((n, 128), F32)
    for j in range(2):
        mine = names[:, j : j + 1]
        rank = jnp.zeros((n, 1), F32)
        for other in range(2):
            same = (across[other : other + 1, :] == mine) & earlier
            rank += jnp.sum(same.astype(F32), axis=1, keepdims=True)
        expert = mine.astype(jnp.int32)
        kz = lax.bitwise_xor(expert // 4, z)
        kx = lax.bitwise_xor(expert % 4, x)
        target = (kx * 4 + kz) * 8 + 2 * step + rank.astype(jnp.int32)
        mix += jnp.where(slot == target, weights[:, j : j + 1], 0.0)
    back = jnp.concatenate(
        [ref[kz].astype(F32) for ref in back_refs for kz in range(4)], axis=0
    ).astype(BF16)
    out_ref[...] = jnp.dot(
        jnp.concatenate(bf16_parts(mix, 3), axis=1),
        jnp.concatenate([back] * 3, axis=0),
        preferred_element_type=F32,
    ).astype(BF16)


def mixed_rows(place, routes, weights, back):
    out = jax.ShapeDtypeStruct((STEPS * ROWS, back[0].shape[-1]), BF16)
    arrays = (routes.transpose(0, 2, 1), weights.transpose(0, 2, 1), *back)
    return call(mix_kernel, "mix", out, place, *arrays, flops=1 << 24)


def shards(
    hidden_in,
    step_qkv,
    decay_rates,
    kv_state,
    attn_gain,
    out_proj,
    ffn_gain,
    routes,
    route_weights,
    w_gate,
    w_up,
    w_down,
):
    share = hidden_in.shape[2] // 8
    head, exp = lax.axis_index("head"), lax.axis_index("exp")
    y, c, z, x = head // 2, head % 2, exp // 4, exp % 4
    place = jnp.stack([x, z, y, c]).astype(jnp.int32)

    *half_a, half_b = readouts(
        place, step_qkv, decay_rates, kv_state, attn_gain, hidden_in, routes
    )
    by_z = half_a[:1] + [over_exp(half_a[k], 4 * k) for k in (1, 2, 3)]
    by_x = jnp.stack([half_b] + [over_exp(half_b, k) for k in (1, 2, 3)], 0)
    by_z = spread(place, by_z, half_b.shape[1])
    all_a = by_z[:1] + [over_exp(by_z[k], k) for k in (1, 2, 3)]
    all_b = [by_x] + [over_exp(by_x, 4 * k) for k in (1, 2, 3)]

    mine, other = project(place, all_a, all_b, out_proj)
    sums = sums_by_y(place, mine, over_head(other, 1))
    sums = sums[:1] + [over_head(sums[k], 2 * k) for k in (1, 2, 3)]

    pieces = attend(place, sums, all_a)
    pieces = turn(place, pieces[:1] + [over_exp(pieces[k], 4 * k) for k in (1, 2, 3)])
    pieces = norm(place, ffn_gain, pieces[:1] + [over_exp(pieces[k], k) for k in (1, 2, 3)])
    by_y = pieces[:1] + [over_head(pieces[k], 2 * k) for k in (1, 2, 3)]
    by_core = [over_head(piece, 1) for piece in by_y]
    attended = owned(place, by_y, by_core, share)

    gate = fetch(by_x, w_gate[0].swapaxes(0, 1))
    up = fetch(by_x, w_up[0].swapaxes(0, 1))
    down_weight = fetch(by_x, w_down[0])
    hidden, theirs = hidden_units(place, by_y + by_core, gate, up, down_weight, share)
    sums = down(place, hidden, down_weight, over_head(theirs, 1))
    results = final_sum(place, sums[:1] + [over_head(sums[k], 2 * k) for k in (1, 2, 3)])

    by_kz = [results[0]] + [over_exp(results[k], 4 * k) for k in (1, 2, 3)]
    by_kx = [jnp.stack([by_kz[kz][kx] for kz in range(4)], 0) for kx in range(4)]
    by_kx = by_kx[:1] + [over_exp(by_kx[k], k) for k in (1, 2, 3)]
    mixed = mixed_rows(place, routes, route_weights, by_kx)
    return attended.reshape(STEPS, ROWS, share), mixed.reshape(STEPS, ROWS, share)


def solution(mesh):
    return jax.shard_map(
        shards,
        mesh=mesh,
        in_specs=(
            P(None, "exp", None),
            P(None, "exp", None, "head"),
            P(None, "head"),
            P("exp", "head", None, None),
            P("head"),
            P("head", "exp"),
            P(),
            P(None, "exp", None),
            P(None, "exp", None),
            P("exp", None, "head"),
            P("exp", None, "head"),
            P("exp", "head", None),
        ),
        out_specs=(P(None, "exp", "head"), P(None, "exp", "head")),
        check_vma=False,
    )
```

```python
import functools

import jax
import jax.numpy as jnp
from jax import lax
from jax.experimental import pallas as pl
from jax.experimental.pallas import tpu as pltpu
from jax.sharding import PartitionSpec as P

STEPS = 4
ROWS = 8
EPS = 1e-06
F32 = jnp.float32
BF16 = jnp.bfloat16
MIB = 1 << 20


def vmem_params(mib):
    return pltpu.CompilerParams(vmem_limit_bytes=mib * MIB)


def over(axis, value, bits):
    return lax.ppermute(value, axis, [(i, i ^ bits) for i in range(lax.axis_size(axis))])


def exchange(value, axes):
    return lax.all_to_all(value, axes, split_axis=0, concat_axis=0, tiled=True)


def call(kernel, name, out_shape, place, *arrays, flops=0, limit=16, scratch=()):
    moved = sum(a.size * a.dtype.itemsize for a in arrays)
    result = pl.pallas_call(
        kernel,
        out_shape=out_shape,
        in_specs=[pl.BlockSpec(memory_space=pltpu.SMEM)]
        + [pl.BlockSpec(memory_space=pltpu.VMEM)] * len(arrays),
        out_specs=jax.tree.map(lambda _: pl.BlockSpec(memory_space=pltpu.VMEM), out_shape),
        scratch_shapes=scratch,
        compiler_params=vmem_params(limit),
        cost_estimate=pl.CostEstimate(flops=flops, bytes_accessed=moved, transcendentals=0),
        name=name,
    )(place, *arrays)
    return list(result) if isinstance(out_shape, list) else result


def xor(a, b):
    return lax.bitwise_xor(a, b)


def lanes_from(start, size):
    return pl.ds(pl.multiple_of(start, 128), size)


def columns_of(table):
    rows = lax.broadcasted_iota(jnp.int32, (ROWS, ROWS), 0)
    lanes = lax.broadcasted_iota(jnp.int32, (ROWS, ROWS), 1)
    return lax.dot_general(
        (rows == lanes).astype(F32),
        table,
        (((1,), (1,)), ((), ())),
        precision=lax.Precision.HIGHEST,
        preferred_element_type=F32,
    )


def widened(pair):
    lane = lax.broadcasted_iota(jnp.int32, (pair.shape[0], 128), 1)
    return jnp.where(lane == 0, pair[:, :1], jnp.where(lane == 1, pair[:, 1:2], 0.0))


def bf16_parts(value, count):
    parts = []
    for _ in range(count - 1):
        parts.append(value.astype(BF16))
        value = value - parts[-1].astype(F32)
    return parts + [value.astype(BF16)]


def readout_kernel(
    place_ref, decay_ref, routes_ref, hidden_ref, qkv_ref, state_ref, gain_ref, out_ref
):
    c = place_ref[2]
    cols = hidden_ref.shape[2] // 16
    depth = out_ref.shape[2] - 256

    @pl.when(pl.program_id(0) == 0)
    def _():
        names = [columns_of(routes_ref[2 * c + t].astype(F32)) for t in range(2)]
        names = widened(jnp.concatenate(names, axis=0)).astype(BF16)
        for i in range(16):
            at = slice(i * cols, (i + 1) * cols)
            rows = [hidden_ref[2 * c + t, :, at].astype(F32) for t in range(2)]
            rows = jnp.concatenate(rows, axis=0).astype(BF16)
            out_ref[i, :16, depth:] = rows[:, :256]
            out_ref[i, 16:, depth : depth + 128] = rows[:, 256:]
            out_ref[i, 16:, depth + 128 :] = names

    n, size = STEPS * ROWS, state_ref.shape[2]
    heads = state_ref.shape[1]
    row = lax.broadcasted_iota(jnp.int32, (n, size), 0)
    row_in = row % ROWS
    row_t = lax.broadcasted_iota(jnp.int32, (n, n), 0)
    row_s = lax.broadcasted_iota(jnp.int32, (n, n), 1)
    for h in range(heads):
        lanes = slice(h * size, (h + 1) * size)
        q, k, v = [
            qkv_ref[:, i, :, lanes].astype(F32).reshape(n, size).astype(BF16) for i in range(3)
        ]
        q_twice = jnp.concatenate([q, q], axis=1)
        carried = jnp.zeros((n, size), F32)
        for pair in range(ROWS // 2):
            wide = jnp.concatenate([state_ref[2 * pair, h], state_ref[2 * pair + 1, h]], axis=1)
            both = jnp.dot(
                q_twice, jnp.concatenate(bf16_parts(wide, 2), axis=0), preferred_element_type=F32
            )
            carried = jnp.where(row_in == 2 * pair, both[:, :size], carried)
            carried = jnp.where(row_in == 2 * pair + 1, both[:, size:], carried)
        decay = [decay_ref[t, pl.program_id(0) * heads + h] for t in range(STEPS)]
        run = decay[0]
        first = jnp.full((n, size), run, F32)
        for t in range(1, STEPS):
            run = run * decay[t]
            first = jnp.where(row // ROWS == t, run, first)
        mix = jnp.zeros((n, n), F32)
        for t in range(STEPS):
            run = None
            for s in range(t, -1, -1):
                here = row_t - row_s == (t - s) * ROWS
                mix = jnp.where(here & (row_s // ROWS == s), 1.0 if run is None else run, mix)
                run = decay[s] if run is None else run * decay[s]
        scores = lax.dot_general(q, k, (((1,), (1,)), ((), ())), preferred_element_type=F32)
        o = carried * first + jnp.dot(
            jnp.concatenate(bf16_parts(scores * mix, 2), axis=1),
            jnp.concatenate([v, v], axis=0),
            preferred_element_type=F32,
        )
        o = o * lax.rsqrt(jnp.mean(o * o, axis=-1, keepdims=True) + EPS) * gain_ref[:, lanes]
        o = o.astype(BF16)
        at = lanes_from((pl.program_id(0) * heads + h) * size, size)
        for i in range(16):
            out_ref[i, :, at] = o


def readouts(place, step_qkv, decay, state, attn_gain, hidden_in, routes):
    heads, size = state.shape[1], state.shape[2]
    at_once = min(heads, 4)
    n = STEPS * ROWS
    packed = heads * size + 256
    return pl.pallas_call(
        readout_kernel,
        out_shape=jax.ShapeDtypeStruct((16, n, packed), BF16),
        grid=(heads // at_once,),
        in_specs=[
            pl.BlockSpec(memory_space=pltpu.SMEM),
            pl.BlockSpec(memory_space=pltpu.SMEM),
            pl.BlockSpec((STEPS, 2, ROWS), lambda i: (0, 0, 0)),
            pl.BlockSpec(hidden_in.shape, lambda i: (0, 0, 0)),
            pl.BlockSpec((STEPS, 3, ROWS, at_once * size), lambda i: (0, 0, 0, i)),
            pl.BlockSpec((ROWS, at_once, size, size), lambda i: (0, i, 0, 0)),
            pl.BlockSpec((1, at_once * size), lambda i: (0, i)),
        ],
        out_specs=pl.BlockSpec((16, n, packed), lambda i: (0, 0, 0)),
        compiler_params=vmem_params(56),
        cost_estimate=pl.CostEstimate(
            flops=2 * STEPS * ROWS * ROWS * heads * size * size * 2,
            bytes_accessed=state.size * 4,
            transcendentals=0,
        ),
        name="readout",
    )(
        place,
        decay,
        routes.transpose(0, 2, 1),
        hidden_in,
        step_qkv.transpose(0, 2, 1, 3),
        state,
        attn_gain.reshape(1, -1),
    )


def project_kernel(place_ref, got_ref, weight_ref, mine_ref, other_ref):
    c = place_ref[2]
    depth = weight_ref.shape[0]
    for part in range(2):
        rows = got_ref[8 * part : 8 * part + 8, :, :depth].reshape(256, depth)
        out = jnp.dot(rows, weight_ref[...], preferred_element_type=F32).astype(BF16)
        for i in range(8):
            a = out[32 * i : 32 * i + 16]
            b = out[32 * i + 16 : 32 * i + 32]
            mine_ref[8 * part + i] = jnp.where(c == 0, a, b)
            other_ref[8 * part + i] = jnp.where(c == 0, b, a)


def project(place, got, weight):
    out = [jax.ShapeDtypeStruct((16, 16, weight.shape[1]), BF16)] * 2
    return call(project_kernel, "project", out, place, got, weight, flops=1024 * weight.size)


def by_y_kernel(place_ref, mine_ref, got_ref, *out_refs):
    y = place_ref[1]
    for k, ref in enumerate(out_refs):
        for x in range(4):
            i = xor(y, k) * 4 + x
            ref[x] = (mine_ref[i].astype(F32) + got_ref[i].astype(F32)).astype(BF16)


def sums_by_y(place, mine, got):
    out = [jax.ShapeDtypeStruct((4,) + mine.shape[1:], BF16)] * 4
    return call(by_y_kernel, "sums_by_y", out, place, mine, got)


def attend_kernel(place_ref, got_ref, *refs):
    sum_refs, out_ref = refs[:4], refs[4]
    y = place_ref[1]
    cols = out_ref.shape[2]
    depth = got_ref.shape[2] - 256
    rows, names = [], []
    for x in range(4):
        i = y * 4 + x
        tail = got_ref[i, 16:, depth:].astype(F32)
        names.append(tail[:, 128:])
        total = jnp.concatenate([got_ref[i, :16, depth:].astype(F32), tail[:, :128]], axis=1)
        for ref in sum_refs:
            total += ref[x].astype(F32)
        rows.append(total.astype(BF16))
        for z in range(4):
            out_ref[4 * z + x, 16:] = rows[x]
    rows = jnp.concatenate(rows, axis=0)
    n = rows.shape[0]
    names = jnp.concatenate(names, axis=0)
    across = names.T
    down_i = lax.broadcasted_iota(jnp.int32, (n, n), 0)
    over_i = lax.broadcasted_iota(jnp.int32, (n, n), 1)
    earlier = (down_i // ROWS == over_i // ROWS) & (down_i < over_i)
    slot = lax.broadcasted_iota(jnp.int32, (256, n), 0)
    lane = lax.broadcasted_iota(jnp.int32, (1, n), 1)
    base = lane // 16 * 4 + lane // ROWS % 2 * 2
    select = jnp.zeros((256, n), F32)
    for j in range(2):
        mine = across[j : j + 1, :]
        rank = jnp.zeros((1, n), F32)
        for other in range(2):
            same = (names[:, other : other + 1] == mine) & earlier
            rank += jnp.sum(same.astype(F32), axis=0, keepdims=True)
        target = mine.astype(jnp.int32) * 16 + base + rank.astype(jnp.int32)
        select += (slot == target).astype(F32)
    sent = jnp.dot(select.astype(BF16), rows, preferred_element_type=F32).astype(BF16)
    for i in range(16):
        out_ref[i, :16] = sent[16 * i : 16 * i + 16]


def attend(place, got, sums):
    out = jax.ShapeDtypeStruct((16, 32, sums[0].shape[2]), BF16)
    return call(attend_kernel, "attend", out, place, got, *sums, flops=1 << 23)


def norm_kernel(place_ref, gain_ref, got_ref, *out_refs):
    y = place_ref[1]
    cols = got_ref.shape[2]
    total = jnp.zeros((16, cols), F32)
    for i in range(16):
        value = got_ref[i, :16].astype(F32)
        total += value * value
    mean = jnp.sum(total, axis=-1, keepdims=True) / (16 * cols)
    scale = lax.rsqrt(mean + EPS)
    for i in range(16):
        at = slice(i * cols, (i + 1) * cols)
        value = (got_ref[i, :16].astype(F32) * scale * gain_ref[:, at]).astype(BF16)
        for out_ref in out_refs:
            out_ref[:, at] = value
    for k, out_ref in enumerate(out_refs):
        for x in range(4):
            at = slice((16 + x) * cols, (17 + x) * cols)
            out_ref[:, at] = got_ref[xor(y, k) * 4 + x, 16:]


def norm(place, gain, got):
    out = [jax.ShapeDtypeStruct((16, 20 * got.shape[2]), BF16)] * 4
    return call(norm_kernel, "norm", out, place, gain.reshape(1, -1), got)


def owned_kernel(place_ref, *refs):
    own_refs, other_refs, out_ref = refs[:4], refs[4:8], refs[8]
    z, y, c = place_ref[0], place_ref[1], place_ref[2]
    share = out_ref.shape[1]
    start = own_refs[0].shape[1] - 2 * share
    at = lanes_from(start + c * share, share)
    for k in range(4):

        @pl.when(xor(z, y) == k)
        def _():
            out_ref[pl.ds(pl.multiple_of(16 * c, 16), 16), :] = own_refs[k][:, at]
            out_ref[pl.ds(pl.multiple_of(16 - 16 * c, 16), 16), :] = other_refs[k][:, at]


def owned(place, by_y, by_core, share):
    out = jax.ShapeDtypeStruct((STEPS * ROWS, share), BF16)
    return call(owned_kernel, "owned", out, place, *by_y, *by_core)


def fetch_kernel(after_ref, *refs):
    in_refs, out_refs, done_ref, sems = refs[:3], refs[3:6], refs[6], refs[7]
    copies = [pltpu.make_async_copy(a, b, sems.at[i]) for i, (a, b) in enumerate(zip(in_refs, out_refs))]
    for copy in copies:
        copy.start()
    done_ref[...] = jnp.zeros_like(done_ref)
    for copy in copies:
        copy.wait()


def fetch(after, *weights):
    return pl.pallas_call(
        fetch_kernel,
        out_shape=[pltpu.VMEM(w.shape, w.dtype) for w in weights]
        + [jax.ShapeDtypeStruct((8, 128), F32)],
        in_specs=[pl.BlockSpec(memory_space=pl.ANY)]
        + [pl.BlockSpec(memory_space=pltpu.HBM)] * len(weights),
        out_specs=[pl.BlockSpec(memory_space=pltpu.VMEM)] * (len(weights) + 1),
        scratch_shapes=[pltpu.SemaphoreType.DMA((len(weights),))],
        compiler_params=vmem_params(36),
        cost_estimate=pl.CostEstimate(
            flops=0, bytes_accessed=sum(2 * w.size for w in weights), transcendentals=0
        ),
        name="fetch",
    )(after, *weights)


def hidden_kernel(place_ref, *refs):
    x_refs, (gate_ref, up_ref, down_ref, _, hidden_ref, theirs_ref) = refs[:8], refs[8:]
    share = theirs_ref.shape[2]
    y, c = place_ref[1], place_ref[2]
    x = jnp.concatenate([r[:, : gate_ref.shape[1]] for r in x_refs], axis=0)
    across = (((1,), (1,)), ((), ()))
    gate = lax.dot_general(gate_ref[...], x, across, preferred_element_type=F32)
    up = lax.dot_general(up_ref[...], x, across, preferred_element_type=F32)
    hidden = (gate / (1.0 + jnp.exp(-gate)) * up).T.astype(BF16)
    hidden_ref[...] = hidden
    for k in range(4):
        block = lax.bitwise_xor(y, k) * 2 + (1 - c)
        at = pl.ds(pl.multiple_of(block * share, 128), share)
        theirs_ref[k] = jnp.dot(hidden, down_ref[:, at], preferred_element_type=F32).astype(BF16)


def hidden_units(place, pieces, gate, up, down_weight, done, share):
    units = gate.shape[0]
    rows = sum(p.shape[0] for p in pieces)
    out = [
        jax.ShapeDtypeStruct((rows, units), BF16),
        jax.ShapeDtypeStruct((4, rows, share), BF16),
    ]
    flops = 5 * rows * gate.size
    arrays = (*pieces, gate, up, down_weight, done)
    return call(hidden_kernel, "hidden_units", out, place, *arrays, flops=flops)


def down_kernel(place_ref, hidden_ref, down_ref, theirs_ref, out_ref):
    share = out_ref.shape[2]
    y, c = place_ref[1], place_ref[2]
    half = hidden_ref.shape[0] // 2
    for k in range(4):
        column = xor(y, k)
        at = lanes_from((column * 2 + c) * share, share)
        ours = jnp.dot(hidden_ref[...], down_ref[:, at], preferred_element_type=F32)
        same = ours[:half] + theirs_ref[k, half:].astype(F32)
        flip = ours[half:] + theirs_ref[k, :half].astype(F32)
        low = jnp.where(c == 0, same, flip)
        high = jnp.where(c == 0, flip, same)
        for ky in range(4):
            for x in range(4):
                rows = slice(16 * ky + 4 * x, 16 * ky + 4 * x + 4)
                block = jnp.concatenate([low[rows], high[rows]], axis=0)
                out_ref[column * 16 + xor(y, ky) * 4 + x] = block.astype(BF16)


def down(place, hidden, weight, theirs):
    out = jax.ShapeDtypeStruct((64, 8, theirs.shape[2]), BF16)
    flops = hidden.shape[0] * weight.size
    return call(down_kernel, "down", out, place, hidden, weight, theirs, flops=flops)


def mix_kernel(place_ref, routes_ref, weights_ref, back_ref, out_ref):
    n = STEPS * ROWS
    names = [columns_of(routes_ref[t].astype(F32)) for t in range(STEPS)]
    names = widened(jnp.concatenate(names, axis=0))
    weights = [columns_of(weights_ref[t]) for t in range(STEPS)]
    weights = jnp.concatenate(weights, axis=0)
    down_i = lax.broadcasted_iota(jnp.int32, (n, n), 0)
    over_i = lax.broadcasted_iota(jnp.int32, (n, n), 1)
    earlier = (down_i // ROWS == over_i // ROWS) & (over_i < down_i)
    across = names.T
    slot = lax.broadcasted_iota(jnp.int32, (n, 128), 1)
    step = lax.broadcasted_iota(jnp.int32, (n, 1), 0) // ROWS
    mix = jnp.zeros((n, 128), F32)
    for j in range(2):
        mine = names[:, j : j + 1]
        rank = jnp.zeros((n, 1), F32)
        for other in range(2):
            same = (across[other : other + 1, :] == mine) & earlier
            rank += jnp.sum(same.astype(F32), axis=1, keepdims=True)
        target = mine.astype(jnp.int32) * 8 + 2 * step + rank.astype(jnp.int32)
        mix += jnp.where(slot == target, weights[:, j : j + 1], 0.0)
    back = back_ref[...].astype(F32)
    back = (back[:16] + back[16:32]) + (back[32:48] + back[48:])
    back = back.reshape(128, back.shape[2]).astype(BF16)
    out_ref[...] = jnp.dot(
        jnp.concatenate(bf16_parts(mix, 3), axis=1),
        jnp.concatenate([back] * 3, axis=0),
        preferred_element_type=F32,
    ).astype(BF16)


def mixed_rows(place, routes, weights, back):
    out = jax.ShapeDtypeStruct((STEPS * ROWS, back.shape[2]), BF16)
    arrays = (routes.transpose(0, 2, 1), weights.transpose(0, 2, 1), back)
    return call(mix_kernel, "mix", out, place, *arrays, flops=1 << 24)


def shards(
    hidden_in,
    step_qkv,
    decay_rates,
    kv_state,
    attn_gain,
    out_proj,
    ffn_gain,
    routes,
    route_weights,
    w_gate,
    w_up,
    w_down,
):
    share = hidden_in.shape[2] // 8
    place = jnp.stack([lax.axis_index(axis) for axis in ("z", "y", "c")]).astype(jnp.int32)

    sent = readouts(place, step_qkv, decay_rates, kv_state, attn_gain, hidden_in, routes)
    got = exchange(sent, ("z", "x"))

    mine, other = project(place, got, out_proj)
    sums = sums_by_y(place, mine, over("c", other, 1))
    sums = sums[:1] + [over("y", sums[k], k) for k in (1, 2, 3)]

    pieces = norm(place, ffn_gain, exchange(attend(place, got, sums), ("z", "x")))
    by_y = pieces[:1] + [over("y", pieces[k], k) for k in (1, 2, 3)]
    gate, up, down_weight, done = fetch(
        pieces[1], w_gate[0].swapaxes(0, 1), w_up[0].swapaxes(0, 1), w_down[0]
    )
    by_y, done = lax.optimization_barrier((by_y, done))
    by_core = [over("c", piece, 1) for piece in by_y]
    attended = owned(place, by_y, by_core, share)

    hidden, theirs = hidden_units(place, by_y + by_core, gate, up, down_weight, done, share)
    sums = down(place, hidden, down_weight, over("c", theirs, 1))

    mixed = mixed_rows(place, routes, route_weights, exchange(sums, ("y", "z", "x")))
    return attended.reshape(STEPS, ROWS, share), mixed.reshape(STEPS, ROWS, share)


def solution(mesh):
    exp, head = ("z", "x"), ("y", "c")
    return jax.shard_map(
        shards,
        mesh=jax.sharding.Mesh(mesh.devices.reshape(4, 2, 4, 4), head + exp),
        in_specs=(
            P(None, exp, None),
            P(None, exp, None, head),
            P(None, head),
            P(exp, head, None, None),
            P(head),
            P(head, exp),
            P(),
            P(None, exp, None),
            P(None, exp, None),
            P(exp, None, head),
            P(exp, None, head),
            P(exp, head, None),
        ),
        out_specs=(P(None, exp, head), P(None, exp, head)),
        check_vma=False,
    )
```

```python
import functools

import jax
import jax.numpy as jnp
from jax import lax
from jax.experimental import pallas as pl
from jax.experimental.pallas import tpu as pltpu
from jax.sharding import PartitionSpec as P

STEPS = 4
ROWS = 8
EPS = 1e-06
F32 = jnp.float32
BF16 = jnp.bfloat16
MIB = 1 << 20


def vmem_params(mib):
    return pltpu.CompilerParams(vmem_limit_bytes=mib * MIB)


def over(axis, value, shift):
    size = lax.axis_size(axis)
    return lax.ppermute(value, axis, [(i, (i + shift) % size) for i in range(size)])


def exchange(value, axes):
    return lax.all_to_all(value, axes, split_axis=0, concat_axis=0, tiled=True)


def call(kernel, name, out_shape, *arrays, flops=0, limit=10, scratch=()):
    moved = sum(a.size * a.dtype.itemsize for a in arrays)
    result = pl.pallas_call(
        lambda *refs: kernel(device_place(), *refs),
        out_shape=out_shape,
        in_specs=[pl.BlockSpec(memory_space=pltpu.VMEM)] * len(arrays),
        out_specs=jax.tree.map(lambda _: pl.BlockSpec(memory_space=pltpu.VMEM), out_shape),
        scratch_shapes=scratch,
        compiler_params=vmem_params(limit),
        cost_estimate=pl.CostEstimate(flops=flops, bytes_accessed=moved, transcendentals=0),
        name=name,
    )(*arrays)
    return list(result) if isinstance(out_shape, list) else result


def device_place():
    return [lax.axis_index(axis) for axis in ("z", "y", "c")]


def turned(a, b):
    return lax.bitwise_and(a + b, 3)


def lanes_from(start, size):
    return pl.ds(pl.multiple_of(start, 128), size)


def columns_of(table):
    rows = lax.broadcasted_iota(jnp.int32, (ROWS, ROWS), 0)
    lanes = lax.broadcasted_iota(jnp.int32, (ROWS, ROWS), 1)
    return lax.dot_general(
        (rows == lanes).astype(F32),
        table,
        (((1,), (1,)), ((), ())),
        precision=lax.Precision.HIGHEST,
        preferred_element_type=F32,
    )


def widened(pair):
    lane = lax.broadcasted_iota(jnp.int32, (pair.shape[0], 128), 1)
    return jnp.where(lane == 0, pair[:, :1], jnp.where(lane == 1, pair[:, 1:2], 0.0))


def bf16_parts(value, count):
    parts = []
    for _ in range(count - 1):
        parts.append(value.astype(BF16))
        value = value - parts[-1].astype(F32)
    return parts + [value.astype(BF16)]


def readout_kernel(
    decay_ref, routes_ref, hidden_ref, qkv_ref, state_ref, gain_ref, out_ref
):
    c = lax.axis_index("c")
    cols = hidden_ref.shape[2] // 16
    depth = out_ref.shape[2] - 256

    @pl.when(pl.program_id(0) == 0)
    def _():
        names = [columns_of(routes_ref[2 * c + t].astype(F32)) for t in range(2)]
        names = widened(jnp.concatenate(names, axis=0)).astype(BF16)
        for i in range(16):
            at = slice(i * cols, (i + 1) * cols)
            rows = [hidden_ref[2 * c + t, :, at].astype(F32) for t in range(2)]
            rows = jnp.concatenate(rows, axis=0).astype(BF16)
            out_ref[i, :16, depth:] = rows[:, :256]
            out_ref[i, 16:, depth : depth + 128] = rows[:, 256:]
            out_ref[i, 16:, depth + 128 :] = names

    n, size = STEPS * ROWS, state_ref.shape[2]
    heads = state_ref.shape[1]
    row = lax.broadcasted_iota(jnp.int32, (n, size), 0)
    row_in = row % ROWS
    row_t = lax.broadcasted_iota(jnp.int32, (n, n), 0)
    row_s = lax.broadcasted_iota(jnp.int32, (n, n), 1)
    for h in range(heads):
        lanes = slice(h * size, (h + 1) * size)
        q, k, v = [
            qkv_ref[:, i, :, lanes].astype(F32).reshape(n, size).astype(BF16) for i in range(3)
        ]
        q_twice = jnp.concatenate([q, q], axis=1)
        carried = jnp.zeros((n, size), F32)
        for pair in range(ROWS // 2):
            wide = jnp.concatenate([state_ref[2 * pair, h], state_ref[2 * pair + 1, h]], axis=1)
            both = jnp.dot(
                q_twice, jnp.concatenate(bf16_parts(wide, 2), axis=0), preferred_element_type=F32
            )
            carried = jnp.where(row_in == 2 * pair, both[:, :size], carried)
            carried = jnp.where(row_in == 2 * pair + 1, both[:, size:], carried)
        decay = [decay_ref[t, pl.program_id(0) * heads + h] for t in range(STEPS)]
        run = decay[0]
        first = jnp.full((n, size), run, F32)
        for t in range(1, STEPS):
            run = run * decay[t]
            first = jnp.where(row // ROWS == t, run, first)
        mix = jnp.zeros((n, n), F32)
        for t in range(STEPS):
            run = None
            for s in range(t, -1, -1):
                here = row_t - row_s == (t - s) * ROWS
                mix = jnp.where(here & (row_s // ROWS == s), 1.0 if run is None else run, mix)
                run = decay[s] if run is None else run * decay[s]
        scores = lax.dot_general(q, k, (((1,), (1,)), ((), ())), preferred_element_type=F32)
        o = carried * first + jnp.dot(
            jnp.concatenate(bf16_parts(scores * mix, 2), axis=1),
            jnp.concatenate([v, v], axis=0),
            preferred_element_type=F32,
        )
        o = o * lax.rsqrt(jnp.mean(o * o, axis=-1, keepdims=True) + EPS) * gain_ref[:, lanes]
        o = o.astype(BF16)
        at = lanes_from((pl.program_id(0) * heads + h) * size, size)
        for i in range(16):
            out_ref[i, :, at] = o


def readouts(step_qkv, decay, state, attn_gain, hidden_in, routes):
    heads, size = state.shape[1], state.shape[2]
    at_once = min(heads, 4)
    n = STEPS * ROWS
    packed = heads * size + 256
    return pl.pallas_call(
        readout_kernel,
        out_shape=jax.ShapeDtypeStruct((16, n, packed), BF16),
        grid=(heads // at_once,),
        in_specs=[
            pl.BlockSpec(memory_space=pltpu.SMEM),
            pl.BlockSpec((STEPS, 2, ROWS), lambda i: (0, 0, 0)),
            pl.BlockSpec(hidden_in.shape, lambda i: (0, 0, 0)),
            pl.BlockSpec((STEPS, 3, ROWS, at_once * size), lambda i: (0, 0, 0, i)),
            pl.BlockSpec((ROWS, at_once, size, size), lambda i: (0, i, 0, 0)),
            pl.BlockSpec((1, at_once * size), lambda i: (0, i)),
        ],
        out_specs=pl.BlockSpec((16, n, packed), lambda i: (0, 0, 0)),
        compiler_params=vmem_params(56),
        cost_estimate=pl.CostEstimate(
            flops=2 * STEPS * ROWS * ROWS * heads * size * size * 2,
            bytes_accessed=state.size * 4,
            transcendentals=0,
        ),
        name="readout",
    )(
        decay,
        routes.transpose(0, 2, 1),
        hidden_in,
        step_qkv.transpose(0, 2, 1, 3),
        state,
        attn_gain.reshape(1, -1),
    )


def project_kernel(place_ref, got_ref, weight_ref, done_ref, mine_ref, other_ref):
    c = place_ref[2]
    depth = weight_ref.shape[0]
    for part in range(2):
        rows = got_ref[8 * part : 8 * part + 8, :, :depth].reshape(256, depth)
        out = jnp.dot(rows, weight_ref[...], preferred_element_type=F32).astype(BF16)
        for i in range(8):
            a = out[32 * i : 32 * i + 16]
            b = out[32 * i + 16 : 32 * i + 32]
            mine_ref[8 * part + i] = jnp.where(c == 0, a, b)
            other_ref[8 * part + i] = jnp.where(c == 0, b, a)


def project(got, weight, done):
    out = [jax.ShapeDtypeStruct((16, 16, weight.shape[1]), BF16)] * 2
    flops = 1024 * weight.size
    return call(project_kernel, "project", out, got, weight, done, flops=flops)


def by_y_kernel(place_ref, mine_ref, got_ref, *out_refs):
    y = place_ref[1]
    for k, ref in enumerate(out_refs):
        for x in range(4):
            i = turned(y, k) * 4 + x
            ref[x] = (mine_ref[i].astype(F32) + got_ref[i].astype(F32)).astype(BF16)


def sums_by_y(mine, got):
    out = [jax.ShapeDtypeStruct((4,) + mine.shape[1:], BF16)] * 4
    return call(by_y_kernel, "sums_by_y", out, mine, got)


def slots_kernel(place_ref, got_ref, select_ref, hidden_ref):
    y = place_ref[1]
    depth = got_ref.shape[2] - 256
    names = []
    for x in range(4):
        i = y * 4 + x
        tail = got_ref[i, 16:, depth:]
        names.append(tail[:, 128:].astype(F32))
        hidden_ref[x] = jnp.concatenate([got_ref[i, :16, depth:], tail[:, :128]], axis=1)
    names = jnp.concatenate(names, axis=0)
    n = names.shape[0]
    across = names.T
    down_i = lax.broadcasted_iota(jnp.int32, (n, n), 0)
    over_i = lax.broadcasted_iota(jnp.int32, (n, n), 1)
    earlier = (down_i // ROWS == over_i // ROWS) & (down_i < over_i)
    slot = lax.broadcasted_iota(jnp.int32, (256, n), 0)
    lane = lax.broadcasted_iota(jnp.int32, (1, n), 1)
    base = lane // 16 * 4 + lane // ROWS % 2 * 2
    select = jnp.zeros((256, n), F32)
    for j in range(2):
        mine = across[j : j + 1, :]
        rank = jnp.zeros((1, n), F32)
        for other in range(2):
            same = (names[:, other : other + 1] == mine) & earlier
            rank += jnp.sum(same.astype(F32), axis=0, keepdims=True)
        target = mine.astype(jnp.int32) * 16 + base + rank.astype(jnp.int32)
        select += (slot == target).astype(F32)
    select_ref[...] = select.astype(BF16)


def slots(got, cols):
    out = [jax.ShapeDtypeStruct((256, 64), BF16), jax.ShapeDtypeStruct((4, 16, cols), BF16)]
    return call(slots_kernel, "slots", out, got, flops=1 << 20)


def attend_kernel(place_ref, select_ref, hidden_ref, *refs):
    sum_refs, out_ref = refs[:4], refs[4]
    rows = []
    for x in range(4):
        total = hidden_ref[x].astype(F32)
        for ref in sum_refs:
            total += ref[x].astype(F32)
        rows.append(total.astype(BF16))
        for z in range(4):
            out_ref[4 * z + x, 16:] = rows[x]
    rows = jnp.concatenate(rows, axis=0)
    sent = jnp.dot(select_ref[...], rows, preferred_element_type=F32).astype(BF16)
    for i in range(16):
        out_ref[i, :16] = sent[16 * i : 16 * i + 16]


def attend(select, hidden, sums):
    out = jax.ShapeDtypeStruct((16, 32, hidden.shape[2]), BF16)
    return call(attend_kernel, "attend", out, select, hidden, *sums, flops=1 << 23)


def norm_kernel(place_ref, gain_ref, got_ref, *out_refs):
    y = place_ref[1]
    cols = got_ref.shape[2]
    total = jnp.zeros((16, cols), F32)
    for i in range(16):
        value = got_ref[i, :16].astype(F32)
        total += value * value
    mean = jnp.sum(total, axis=-1, keepdims=True) / (16 * cols)
    scale = lax.rsqrt(mean + EPS)
    for i in range(16):
        at = slice(i * cols, (i + 1) * cols)
        value = (got_ref[i, :16].astype(F32) * scale * gain_ref[:, at]).astype(BF16)
        for out_ref in out_refs:
            out_ref[:, at] = value
    for k, out_ref in enumerate(out_refs):
        for x in range(4):
            at = slice((16 + x) * cols, (17 + x) * cols)
            out_ref[:, at] = got_ref[turned(y, 4 - k) * 4 + x, 16:]


def norm(gain, got):
    out = [jax.ShapeDtypeStruct((16, 20 * got.shape[2]), BF16)] * 4
    return call(norm_kernel, "norm", out, gain.reshape(1, -1), got)


def owned_kernel(place_ref, *refs):
    own_refs, other_refs, out_ref = refs[:4], refs[4:8], refs[8]
    z, y, c = place_ref[0], place_ref[1], place_ref[2]
    share = out_ref.shape[1]
    start = own_refs[0].shape[1] - 2 * share
    at = lanes_from(start + c * share, share)
    for k in range(4):

        @pl.when(turned(z, 4 - y) == k)
        def _():
            out_ref[pl.ds(pl.multiple_of(16 * c, 16), 16), :] = own_refs[k][:, at]
            out_ref[pl.ds(pl.multiple_of(16 - 16 * c, 16), 16), :] = other_refs[k][:, at]


def owned(by_y, by_core, share):
    out = jax.ShapeDtypeStruct((STEPS * ROWS, share), BF16)
    return call(owned_kernel, "owned", out, *by_y, *by_core)


def fetch_kernel(after_ref, *refs):
    in_refs, out_refs, done_ref, sems = refs[:3], refs[3:6], refs[6], refs[7]
    copies = [pltpu.make_async_copy(a, b, sems.at[i]) for i, (a, b) in enumerate(zip(in_refs, out_refs))]
    for copy in copies:
        copy.start()
    done_ref[...] = jnp.zeros_like(done_ref)
    for copy in copies:
        copy.wait()


def fetch(after, *weights):
    return pl.pallas_call(
        fetch_kernel,
        out_shape=[pltpu.VMEM(w.shape, w.dtype) for w in weights]
        + [jax.ShapeDtypeStruct((8, 128), F32)],
        in_specs=[pl.BlockSpec(memory_space=pl.ANY)]
        + [pl.BlockSpec(memory_space=pltpu.HBM)] * len(weights),
        out_specs=[pl.BlockSpec(memory_space=pltpu.VMEM)] * (len(weights) + 1),
        scratch_shapes=[pltpu.SemaphoreType.DMA((len(weights),))],
        compiler_params=vmem_params(36),
        cost_estimate=pl.CostEstimate(
            flops=0, bytes_accessed=sum(2 * w.size for w in weights), transcendentals=0
        ),
        name="fetch",
    )(after, *weights)


def hidden_kernel(place_ref, *refs):
    x_refs, (gate_ref, up_ref, down_ref, hidden_ref, theirs_ref) = refs[:8], refs[8:]
    share = theirs_ref.shape[2]
    y, c = place_ref[1], place_ref[2]
    x = jnp.concatenate([r[:, : gate_ref.shape[1]] for r in x_refs], axis=0)
    across = (((1,), (1,)), ((), ()))
    gate = lax.dot_general(gate_ref[...], x, across, preferred_element_type=F32)
    up = lax.dot_general(up_ref[...], x, across, preferred_element_type=F32)
    hidden = (gate / (1.0 + jnp.exp(-gate)) * up).T.astype(BF16)
    hidden_ref[...] = hidden
    for k in range(4):
        block = turned(y, k) * 2 + (1 - c)
        at = pl.ds(pl.multiple_of(block * share, 128), share)
        theirs_ref[k] = jnp.dot(hidden, down_ref[:, at], preferred_element_type=F32).astype(BF16)


def hidden_units(pieces, gate, up, down_weight, share):
    units = gate.shape[0]
    rows = sum(p.shape[0] for p in pieces)
    out = [
        jax.ShapeDtypeStruct((rows, units), BF16),
        jax.ShapeDtypeStruct((4, rows, share), BF16),
    ]
    flops = 5 * rows * gate.size
    arrays = (*pieces, gate, up, down_weight)
    return call(hidden_kernel, "hidden_units", out, *arrays, flops=flops)


def down_kernel(place_ref, hidden_ref, down_ref, out_ref):
    share = out_ref.shape[2]
    y, c = place_ref[1], place_ref[2]
    for k in range(4):
        at = lanes_from((turned(y, k) * 2 + c) * share, share)
        out_ref[k] = jnp.dot(hidden_ref[...], down_ref[:, at], preferred_element_type=F32)


def down(hidden, weight, share):
    out = jax.ShapeDtypeStruct((4, hidden.shape[0], share), F32)
    flops = hidden.shape[0] * weight.size
    return call(down_kernel, "down", out, hidden, weight, flops=flops)


def cores_kernel(place_ref, ours_ref, theirs_ref, out_ref):
    y, c = place_ref[1], place_ref[2]
    half = ours_ref.shape[1] // 2
    for k in range(4):
        same = ours_ref[k, :half] + theirs_ref[k, half:].astype(F32)
        flip = ours_ref[k, half:] + theirs_ref[k, :half].astype(F32)
        low = jnp.where(c == 0, same, flip)
        high = jnp.where(c == 0, flip, same)
        for ky in range(4):
            for x in range(4):
                rows = slice(16 * ky + 4 * x, 16 * ky + 4 * x + 4)
                block = jnp.concatenate([low[rows], high[rows]], axis=0)
                out_ref[turned(y, k) * 16 + turned(y, ky) * 4 + x] = block.astype(BF16)


def cores_sum(ours, theirs):
    out = jax.ShapeDtypeStruct((64, 8, theirs.shape[2]), BF16)
    return call(cores_kernel, "cores_sum", out, ours, theirs)


def weights_kernel(place_ref, routes_ref, weights_ref, out_ref):
    n = STEPS * ROWS
    names = [columns_of(routes_ref[t].astype(F32)) for t in range(STEPS)]
    names = widened(jnp.concatenate(names, axis=0))
    weights = [columns_of(weights_ref[t]) for t in range(STEPS)]
    weights = jnp.concatenate(weights, axis=0)
    down_i = lax.broadcasted_iota(jnp.int32, (n, n), 0)
    over_i = lax.broadcasted_iota(jnp.int32, (n, n), 1)
    earlier = (down_i // ROWS == over_i // ROWS) & (over_i < down_i)
    across = names.T
    slot = lax.broadcasted_iota(jnp.int32, (n, 128), 1)
    step = lax.broadcasted_iota(jnp.int32, (n, 1), 0) // ROWS
    mix = jnp.zeros((n, 128), F32)
    for j in range(2):
        mine = names[:, j : j + 1]
        rank = jnp.zeros((n, 1), F32)
        for other in range(2):
            same = (across[other : other + 1, :] == mine) & earlier
            rank += jnp.sum(same.astype(F32), axis=1, keepdims=True)
        target = mine.astype(jnp.int32) * 8 + 2 * step + rank.astype(jnp.int32)
        mix += jnp.where(slot == target, weights[:, j : j + 1], 0.0)
    out_ref[...] = jnp.concatenate(bf16_parts(mix, 3), axis=1)


def mix_weights(routes, weights):
    out = jax.ShapeDtypeStruct((STEPS * ROWS, 384), BF16)
    arrays = (routes.transpose(0, 2, 1), weights.transpose(0, 2, 1))
    return call(weights_kernel, "mix_weights", out, *arrays, flops=1 << 20)


def mix_kernel(place_ref, mix_ref, back_ref, out_ref):
    back = back_ref[...].astype(F32)
    back = (back[:16] + back[16:32]) + (back[32:48] + back[48:])
    back = back.reshape(128, back.shape[2]).astype(BF16)
    out_ref[...] = jnp.dot(
        mix_ref[...], jnp.concatenate([back] * 3, axis=0), preferred_element_type=F32
    ).astype(BF16)


def mixed_rows(mix, back):
    out = jax.ShapeDtypeStruct((STEPS * ROWS, back.shape[2]), BF16)
    return call(mix_kernel, "mix", out, mix, back, flops=1 << 24)


def shards(
    hidden_in,
    step_qkv,
    decay_rates,
    kv_state,
    attn_gain,
    out_proj,
    ffn_gain,
    routes,
    route_weights,
    w_gate,
    w_up,
    w_down,
):
    share = hidden_in.shape[2] // 8

    sent = readouts(step_qkv, decay_rates, kv_state, attn_gain, hidden_in, routes)
    gate, up, down_weight, done = fetch(
        sent, w_gate[0].swapaxes(0, 1), w_up[0].swapaxes(0, 1), w_down[0]
    )
    got = exchange(sent, ("z", "x"))

    mine, other = project(got, out_proj, done)
    sums = sums_by_y(mine, over("c", other, 1))
    select, hidden = slots(got, out_proj.shape[1])
    sums = sums[:1] + [over("y", sums[k], k) for k in (1, 2, 3)]

    pieces = exchange(attend(select, hidden, sums), ("z", "x"))
    pieces = norm(ffn_gain, pieces)
    by_y = pieces[:1] + [over("y", pieces[k], -k) for k in (1, 2, 3)]
    by_core = [over("c", piece, 1) for piece in by_y]

    hidden, theirs = hidden_units(by_y + by_core, gate, up, down_weight, share)
    theirs = over("c", theirs, 1)
    sums = cores_sum(down(hidden, down_weight, share), theirs)

    attended = owned(by_y, by_core, share)
    mix = mix_weights(routes, route_weights)
    mixed = mixed_rows(mix, exchange(sums, ("y", "z", "x")))
    return attended.reshape(STEPS, ROWS, share), mixed.reshape(STEPS, ROWS, share)


def solution(mesh):
    exp, head = ("z", "x"), ("y", "c")
    return jax.shard_map(
        shards,
        mesh=jax.sharding.Mesh(mesh.devices.reshape(4, 2, 4, 4), head + exp),
        in_specs=(
            P(None, exp, None),
            P(None, exp, None, head),
            P(None, head),
            P(exp, head, None, None),
            P(head),
            P(head, exp),
            P(),
            P(None, exp, None),
            P(None, exp, None),
            P(exp, None, head),
            P(exp, None, head),
            P(exp, head, None),
        ),
        out_specs=(P(None, exp, head), P(None, exp, head)),
        check_vma=False,
    )
```

```python
import functools

import jax
import jax.numpy as jnp
from jax import lax
from jax.experimental import pallas as pl
from jax.experimental.pallas import tpu as pltpu
from jax.sharding import PartitionSpec as P

STEPS = 4
ROWS = 8
EPS = 1e-06
F32 = jnp.float32
BF16 = jnp.bfloat16
MIB = 1 << 20


def vmem_params(mib):
    return pltpu.CompilerParams(vmem_limit_bytes=mib * MIB)


def over(axis, value, shift):
    size = lax.axis_size(axis)
    return lax.ppermute(value, axis, [(i, (i + shift) % size) for i in range(size)])


def exchange(value, axes):
    return lax.all_to_all(value, axes, split_axis=0, concat_axis=0, tiled=True)


def call(kernel, name, out_shape, *arrays, flops=0, limit=10, scratch=()):
    moved = sum(a.size * a.dtype.itemsize for a in arrays)
    result = pl.pallas_call(
        lambda *refs: kernel(device_place(), *refs),
        out_shape=out_shape,
        in_specs=[pl.BlockSpec(memory_space=pltpu.VMEM)] * len(arrays),
        out_specs=jax.tree.map(lambda _: pl.BlockSpec(memory_space=pltpu.VMEM), out_shape),
        scratch_shapes=scratch,
        compiler_params=vmem_params(limit),
        cost_estimate=pl.CostEstimate(flops=flops, bytes_accessed=moved, transcendentals=0),
        name=name,
    )(*arrays)
    return list(result) if isinstance(out_shape, list) else result


def device_place():
    return [lax.axis_index(axis) for axis in ("z", "y", "c")]


def turned(a, b):
    return lax.bitwise_and(a + b, 3)


def lanes_from(start, size):
    return pl.ds(pl.multiple_of(start, 128), size)


def columns_of(table):
    rows = lax.broadcasted_iota(jnp.int32, (ROWS, ROWS), 0)
    lanes = lax.broadcasted_iota(jnp.int32, (ROWS, ROWS), 1)
    return lax.dot_general(
        (rows == lanes).astype(F32),
        table,
        (((1,), (1,)), ((), ())),
        precision=lax.Precision.HIGHEST,
        preferred_element_type=F32,
    )


def widened(pair):
    lane = lax.broadcasted_iota(jnp.int32, (pair.shape[0], 128), 1)
    return jnp.where(lane == 0, pair[:, :1], jnp.where(lane == 1, pair[:, 1:2], 0.0))


def bf16_parts(value, count):
    parts = []
    for _ in range(count - 1):
        parts.append(value.astype(BF16))
        value = value - parts[-1].astype(F32)
    return parts + [value.astype(BF16)]


def readout_kernel(
    decay_ref, routes_ref, hidden_ref, qkv_ref, state_ref, gain_ref, out_ref
):
    c = lax.axis_index("c")
    cols = hidden_ref.shape[2] // 16
    depth = out_ref.shape[2] - 256

    @pl.when(pl.program_id(0) == 0)
    def _():
        names = [columns_of(routes_ref[2 * c + t].astype(F32)) for t in range(2)]
        names = widened(jnp.concatenate(names, axis=0)).astype(BF16)
        for i in range(16):
            at = slice(i * cols, (i + 1) * cols)
            rows = [hidden_ref[2 * c + t, :, at].astype(F32) for t in range(2)]
            rows = jnp.concatenate(rows, axis=0).astype(BF16)
            out_ref[i, :16, depth:] = rows[:, :256]
            out_ref[i, 16:, depth : depth + 128] = rows[:, 256:]
            out_ref[i, 16:, depth + 128 :] = names

    n, size = STEPS * ROWS, state_ref.shape[2]
    heads = state_ref.shape[1]
    row = lax.broadcasted_iota(jnp.int32, (n, size), 0)
    row_in = row % ROWS
    row_t = lax.broadcasted_iota(jnp.int32, (n, n), 0)
    row_s = lax.broadcasted_iota(jnp.int32, (n, n), 1)
    for h in range(heads):
        lanes = slice(h * size, (h + 1) * size)
        q, k, v = [
            qkv_ref[:, i, :, lanes].astype(F32).reshape(n, size).astype(BF16) for i in range(3)
        ]
        q_twice = jnp.concatenate([q, q], axis=1)
        carried = jnp.zeros((n, size), F32)
        for pair in range(ROWS // 2):
            wide = jnp.concatenate([state_ref[2 * pair, h], state_ref[2 * pair + 1, h]], axis=1)
            both = jnp.dot(
                q_twice, jnp.concatenate(bf16_parts(wide, 2), axis=0), preferred_element_type=F32
            )
            carried = jnp.where(row_in == 2 * pair, both[:, :size], carried)
            carried = jnp.where(row_in == 2 * pair + 1, both[:, size:], carried)
        here = lax.broadcasted_iota(jnp.int32, decay_ref.shape, 1) == pl.program_id(0) * heads + h
        decay = jnp.sum(jnp.where(here, decay_ref[...], 0.0), axis=1, keepdims=True)
        decay = [decay[t : t + 1] for t in range(STEPS)]
        run = decay[0]
        first = jnp.broadcast_to(run, (n, size))
        for t in range(1, STEPS):
            run = run * decay[t]
            first = jnp.where(row // ROWS == t, run, first)
        mix = jnp.zeros((n, n), F32)
        for t in range(STEPS):
            run = None
            for s in range(t, -1, -1):
                here = row_t - row_s == (t - s) * ROWS
                mix = jnp.where(here & (row_s // ROWS == s), 1.0 if run is None else run, mix)
                run = decay[s] if run is None else run * decay[s]
        scores = lax.dot_general(q, k, (((1,), (1,)), ((), ())), preferred_element_type=F32)
        o = carried * first + jnp.dot(
            jnp.concatenate(bf16_parts(scores * mix, 2), axis=1),
            jnp.concatenate([v, v], axis=0),
            preferred_element_type=F32,
        )
        o = o * lax.rsqrt(jnp.mean(o * o, axis=-1, keepdims=True) + EPS) * gain_ref[:, lanes]
        o = o.astype(BF16)
        at = lanes_from((pl.program_id(0) * heads + h) * size, size)
        for i in range(16):
            out_ref[i, :, at] = o


def readouts(step_qkv, decay, state, attn_gain, hidden_in, routes):
    heads, size = state.shape[1], state.shape[2]
    at_once = min(heads, 4)
    n = STEPS * ROWS
    packed = heads * size + 256
    return pl.pallas_call(
        readout_kernel,
        out_shape=jax.ShapeDtypeStruct((16, n, packed), BF16),
        grid=(heads // at_once,),
        in_specs=[
            pl.BlockSpec(decay.shape, lambda i: (0, 0)),
            pl.BlockSpec((STEPS, 2, ROWS), lambda i: (0, 0, 0)),
            pl.BlockSpec(hidden_in.shape, lambda i: (0, 0, 0)),
            pl.BlockSpec((STEPS, 3, ROWS, at_once * size), lambda i: (0, 0, 0, i)),
            pl.BlockSpec((ROWS, at_once, size, size), lambda i: (0, i, 0, 0)),
            pl.BlockSpec((1, at_once * size), lambda i: (0, i)),
        ],
        out_specs=pl.BlockSpec((16, n, packed), lambda i: (0, 0, 0)),
        compiler_params=vmem_params(56),
        cost_estimate=pl.CostEstimate(
            flops=2 * STEPS * ROWS * ROWS * heads * size * size * 2,
            bytes_accessed=state.size * 4,
            transcendentals=0,
        ),
        name="readout",
    )(
        decay,
        routes.transpose(0, 2, 1),
        hidden_in,
        step_qkv.transpose(0, 2, 1, 3),
        state,
        attn_gain.reshape(1, -1),
    )


def project_kernel(place_ref, got_ref, weight_ref, mine_ref, other_ref):
    c = place_ref[2]
    depth = weight_ref.shape[0]
    for part in range(2):
        rows = got_ref[8 * part : 8 * part + 8, :, :depth].reshape(256, depth)
        out = jnp.dot(rows, weight_ref[...], preferred_element_type=F32).astype(BF16)
        for i in range(8):
            a = out[32 * i : 32 * i + 16]
            b = out[32 * i + 16 : 32 * i + 32]
            mine_ref[8 * part + i] = jnp.where(c == 0, a, b)
            other_ref[8 * part + i] = jnp.where(c == 0, b, a)


def project(got, weight):
    out = [jax.ShapeDtypeStruct((16, 16, weight.shape[1]), BF16)] * 2
    flops = 1024 * weight.size
    return call(project_kernel, "project", out, got, weight, flops=flops)


def by_y_kernel(place_ref, mine_ref, got_ref, *out_refs):
    y = place_ref[1]
    for k, ref in enumerate(out_refs):
        for x in range(4):
            i = turned(y, k) * 4 + x
            ref[x] = (mine_ref[i].astype(F32) + got_ref[i].astype(F32)).astype(BF16)


def sums_by_y(mine, got):
    out = [jax.ShapeDtypeStruct((4,) + mine.shape[1:], BF16)] * 4
    return call(by_y_kernel, "sums_by_y", out, mine, got)


def slots_kernel(place_ref, got_ref, select_ref, hidden_ref):
    y = place_ref[1]
    depth = got_ref.shape[2] - 256
    names = []
    for x in range(4):
        i = y * 4 + x
        tail = got_ref[i, 16:, depth:]
        names.append(tail[:, 128:].astype(F32))
        hidden_ref[x] = jnp.concatenate([got_ref[i, :16, depth:], tail[:, :128]], axis=1)
    names = jnp.concatenate(names, axis=0)
    n = names.shape[0]
    across = names.T
    down_i = lax.broadcasted_iota(jnp.int32, (n, n), 0)
    over_i = lax.broadcasted_iota(jnp.int32, (n, n), 1)
    earlier = (down_i // ROWS == over_i // ROWS) & (down_i < over_i)
    slot = lax.broadcasted_iota(jnp.int32, (256, n), 0)
    lane = lax.broadcasted_iota(jnp.int32, (1, n), 1)
    base = lane // 16 * 4 + lane // ROWS % 2 * 2
    select = jnp.zeros((256, n), F32)
    for j in range(2):
        mine = across[j : j + 1, :]
        rank = jnp.zeros((1, n), F32)
        for other in range(2):
            same = (names[:, other : other + 1] == mine) & earlier
            rank += jnp.sum(same.astype(F32), axis=0, keepdims=True)
        target = mine.astype(jnp.int32) * 16 + base + rank.astype(jnp.int32)
        select += (slot == target).astype(F32)
    select_ref[...] = select.astype(BF16)


def slots(got, cols):
    out = [jax.ShapeDtypeStruct((256, 64), BF16), jax.ShapeDtypeStruct((4, 16, cols), BF16)]
    return call(slots_kernel, "slots", out, got, flops=1 << 20)


def attend_kernel(place_ref, select_ref, hidden_ref, *refs):
    sum_refs, out_ref = refs[:4], refs[4]
    rows = []
    for x in range(4):
        total = hidden_ref[x].astype(F32)
        for ref in sum_refs:
            total += ref[x].astype(F32)
        rows.append(total.astype(BF16))
        for z in range(4):
            out_ref[4 * z + x, 16:] = rows[x]
    rows = jnp.concatenate(rows, axis=0)
    sent = jnp.dot(select_ref[...], rows, preferred_element_type=F32).astype(BF16)
    for i in range(16):
        out_ref[i, :16] = sent[16 * i : 16 * i + 16]


def attend(select, hidden, sums):
    out = jax.ShapeDtypeStruct((16, 32, hidden.shape[2]), BF16)
    return call(attend_kernel, "attend", out, select, hidden, *sums, flops=1 << 23)


def norm_kernel(place_ref, gain_ref, got_ref, *out_refs):
    y = place_ref[1]
    cols = got_ref.shape[2]
    total = jnp.zeros((16, cols), F32)
    for i in range(16):
        value = got_ref[i, :16].astype(F32)
        total += value * value
    mean = jnp.sum(total, axis=-1, keepdims=True) / (16 * cols)
    scale = lax.rsqrt(mean + EPS)
    for i in range(16):
        at = slice(i * cols, (i + 1) * cols)
        value = (got_ref[i, :16].astype(F32) * scale * gain_ref[:, at]).astype(BF16)
        for out_ref in out_refs:
            out_ref[:, at] = value
    for k, out_ref in enumerate(out_refs):
        for x in range(4):
            at = slice((16 + x) * cols, (17 + x) * cols)
            out_ref[:, at] = got_ref[turned(y, 4 - k) * 4 + x, 16:]


def norm(gain, got):
    out = [jax.ShapeDtypeStruct((16, 20 * got.shape[2]), BF16)] * 4
    return call(norm_kernel, "norm", out, gain.reshape(1, -1), got)


def owned_kernel(place_ref, *refs):
    own_refs, other_refs, out_ref = refs[:4], refs[4:8], refs[8]
    z, y, c = place_ref[0], place_ref[1], place_ref[2]
    share = out_ref.shape[1]
    start = own_refs[0].shape[1] - 2 * share
    at = lanes_from(start + c * share, share)
    for k in range(4):

        @pl.when(turned(z, 4 - y) == k)
        def _():
            out_ref[pl.ds(pl.multiple_of(16 * c, 16), 16), :] = own_refs[k][:, at]
            out_ref[pl.ds(pl.multiple_of(16 - 16 * c, 16), 16), :] = other_refs[k][:, at]


def owned(by_y, by_core, share):
    out = jax.ShapeDtypeStruct((STEPS * ROWS, share), BF16)
    return call(owned_kernel, "owned", out, *by_y, *by_core)


def fetch_kernel(after_ref, *refs):
    in_refs, out_refs, done_ref, sems = refs[:3], refs[3:6], refs[6], refs[7]
    copies = [pltpu.make_async_copy(a, b, sems.at[i]) for i, (a, b) in enumerate(zip(in_refs, out_refs))]
    for copy in copies:
        copy.start()
    done_ref[...] = jnp.zeros_like(done_ref)
    for copy in copies:
        copy.wait()


def fetch(after, *weights):
    return pl.pallas_call(
        fetch_kernel,
        out_shape=[pltpu.VMEM(w.shape, w.dtype) for w in weights]
        + [pltpu.VMEM((8, 128), F32)],
        in_specs=[pl.BlockSpec(memory_space=pl.ANY)]
        + [pl.BlockSpec(memory_space=pltpu.HBM)] * len(weights),
        out_specs=[pl.BlockSpec(memory_space=pltpu.VMEM)] * (len(weights) + 1),
        scratch_shapes=[pltpu.SemaphoreType.DMA((len(weights),))],
        compiler_params=vmem_params(36),
        cost_estimate=pl.CostEstimate(
            flops=0, bytes_accessed=sum(2 * w.size for w in weights), transcendentals=0
        ),
        name="fetch",
    )(after, *weights)


def hidden_kernel(place_ref, *refs):
    x_refs, (gate_ref, up_ref, down_ref, _, hidden_ref, theirs_ref) = refs[:8], refs[8:]
    share = theirs_ref.shape[2]
    y, c = place_ref[1], place_ref[2]
    x = jnp.concatenate([r[:, : gate_ref.shape[1]] for r in x_refs], axis=0)
    across = (((1,), (1,)), ((), ()))
    gate = lax.dot_general(gate_ref[...], x, across, preferred_element_type=F32)
    up = lax.dot_general(up_ref[...], x, across, preferred_element_type=F32)
    hidden = (gate / (1.0 + jnp.exp(-gate)) * up).T.astype(BF16)
    hidden_ref[...] = hidden
    for k in range(4):
        block = turned(y, k) * 2 + (1 - c)
        at = pl.ds(pl.multiple_of(block * share, 128), share)
        theirs_ref[k] = jnp.dot(hidden, down_ref[:, at], preferred_element_type=F32).astype(BF16)


def hidden_units(pieces, gate, up, down_weight, done, share):
    units = gate.shape[0]
    rows = sum(p.shape[0] for p in pieces)
    out = [
        jax.ShapeDtypeStruct((rows, units), BF16),
        jax.ShapeDtypeStruct((4, rows, share), BF16),
    ]
    flops = 5 * rows * gate.size
    arrays = (*pieces, gate, up, down_weight, done)
    return call(hidden_kernel, "hidden_units", out, *arrays, flops=flops)


def down_kernel(place_ref, hidden_ref, down_ref, out_ref):
    share = out_ref.shape[2]
    y, c = place_ref[1], place_ref[2]
    for k in range(4):
        at = lanes_from((turned(y, k) * 2 + c) * share, share)
        out_ref[k] = jnp.dot(hidden_ref[...], down_ref[:, at], preferred_element_type=F32)


def down(hidden, weight, share):
    out = jax.ShapeDtypeStruct((4, hidden.shape[0], share), F32)
    flops = hidden.shape[0] * weight.size
    return call(down_kernel, "down", out, hidden, weight, flops=flops)


def cores_kernel(place_ref, ours_ref, theirs_ref, out_ref):
    y, c = place_ref[1], place_ref[2]
    half = ours_ref.shape[1] // 2
    for k in range(4):
        same = ours_ref[k, :half] + theirs_ref[k, half:].astype(F32)
        flip = ours_ref[k, half:] + theirs_ref[k, :half].astype(F32)
        low = jnp.where(c == 0, same, flip)
        high = jnp.where(c == 0, flip, same)
        for ky in range(4):
            for x in range(4):
                rows = slice(16 * ky + 4 * x, 16 * ky + 4 * x + 4)
                block = jnp.concatenate([low[rows], high[rows]], axis=0)
                out_ref[turned(y, k) * 16 + turned(y, ky) * 4 + x] = block.astype(BF16)


def cores_sum(ours, theirs):
    out = jax.ShapeDtypeStruct((64, 8, theirs.shape[2]), BF16)
    return call(cores_kernel, "cores_sum", out, ours, theirs)


def weights_kernel(place_ref, routes_ref, weights_ref, out_ref):
    n = STEPS * ROWS
    names = [columns_of(routes_ref[t].astype(F32)) for t in range(STEPS)]
    names = widened(jnp.concatenate(names, axis=0))
    weights = [columns_of(weights_ref[t]) for t in range(STEPS)]
    weights = jnp.concatenate(weights, axis=0)
    down_i = lax.broadcasted_iota(jnp.int32, (n, n), 0)
    over_i = lax.broadcasted_iota(jnp.int32, (n, n), 1)
    earlier = (down_i // ROWS == over_i // ROWS) & (over_i < down_i)
    across = names.T
    slot = lax.broadcasted_iota(jnp.int32, (n, 128), 1)
    step = lax.broadcasted_iota(jnp.int32, (n, 1), 0) // ROWS
    mix = jnp.zeros((n, 128), F32)
    for j in range(2):
        mine = names[:, j : j + 1]
        rank = jnp.zeros((n, 1), F32)
        for other in range(2):
            same = (across[other : other + 1, :] == mine) & earlier
            rank += jnp.sum(same.astype(F32), axis=1, keepdims=True)
        target = mine.astype(jnp.int32) * 8 + 2 * step + rank.astype(jnp.int32)
        mix += jnp.where(slot == target, weights[:, j : j + 1], 0.0)
    out_ref[...] = jnp.concatenate(bf16_parts(mix, 3), axis=1)


def mix_weights(routes, weights):
    out = jax.ShapeDtypeStruct((STEPS * ROWS, 384), BF16)
    arrays = (routes.transpose(0, 2, 1), weights.transpose(0, 2, 1))
    return call(weights_kernel, "mix_weights", out, *arrays, flops=1 << 20)


def mix_kernel(place_ref, mix_ref, back_ref, out_ref):
    back = back_ref[...].astype(F32)
    back = (back[:16] + back[16:32]) + (back[32:48] + back[48:])
    back = back.reshape(128, back.shape[2]).astype(BF16)
    out_ref[...] = jnp.dot(
        mix_ref[...], jnp.concatenate([back] * 3, axis=0), preferred_element_type=F32
    ).astype(BF16)


def mixed_rows(mix, back):
    out = jax.ShapeDtypeStruct((STEPS * ROWS, back.shape[2]), BF16)
    return call(mix_kernel, "mix", out, mix, back, flops=1 << 24)


def shards(
    hidden_in,
    step_qkv,
    decay_rates,
    kv_state,
    attn_gain,
    out_proj,
    ffn_gain,
    routes,
    route_weights,
    w_gate,
    w_up,
    w_down,
):
    share = hidden_in.shape[2] // 8

    sent = readouts(step_qkv, decay_rates, kv_state, attn_gain, hidden_in, routes)
    got = exchange(sent, ("z", "x"))

    mine, other = project(got, out_proj)
    sums = sums_by_y(mine, over("c", other, 1))
    select, hidden = slots(got, out_proj.shape[1])
    sums = sums[:1] + [over("y", sums[k], k) for k in (1, 2, 3)]

    pieces = exchange(attend(select, hidden, sums), ("z", "x"))
    pieces = norm(ffn_gain, pieces)
    by_y = pieces[:1] + [over("y", pieces[k], -k) for k in (1, 2, 3)]
    gate, up, down_weight, done = fetch(
        pieces[1], w_gate[0].swapaxes(0, 1), w_up[0].swapaxes(0, 1), w_down[0]
    )
    by_y, done = lax.optimization_barrier((by_y, done))
    by_core = [over("c", piece, 1) for piece in by_y]

    hidden, theirs = hidden_units(by_y + by_core, gate, up, down_weight, done, share)
    theirs = over("c", theirs, 1)
    sums = cores_sum(down(hidden, down_weight, share), theirs)

    attended = owned(by_y, by_core, share)
    mix = mix_weights(routes, route_weights)
    mixed = mixed_rows(mix, exchange(sums, ("y", "z", "x")))
    return attended.reshape(STEPS, ROWS, share), mixed.reshape(STEPS, ROWS, share)


def solution(mesh):
    exp, head = ("z", "x"), ("y", "c")
    return jax.shard_map(
        shards,
        mesh=jax.sharding.Mesh(mesh.devices.reshape(4, 2, 4, 4), head + exp),
        in_specs=(
            P(None, exp, None),
            P(None, exp, None, head),
            P(None, head),
            P(exp, head, None, None),
            P(head),
            P(head, exp),
            P(),
            P(None, exp, None),
            P(None, exp, None),
            P(exp, None, head),
            P(exp, None, head),
            P(exp, head, None),
        ),
        out_specs=(P(None, exp, head), P(None, exp, head)),
        check_vma=False,
    )
```

```python
import functools

import jax
import jax.numpy as jnp
from jax import lax
from jax.experimental import pallas as pl
from jax.experimental.pallas import tpu as pltpu
from jax.sharding import PartitionSpec as P

STEPS = 4
ROWS = 8
EPS = 1e-06
F32 = jnp.float32
BF16 = jnp.bfloat16
MIB = 1 << 20


def vmem_params(mib):
    return pltpu.CompilerParams(vmem_limit_bytes=mib * MIB)


def over(axis, value, shift):
    size = lax.axis_size(axis)
    return lax.ppermute(value, axis, [(i, (i + shift) % size) for i in range(size)])


def exchange(value, axes):
    return lax.all_to_all(value, axes, split_axis=0, concat_axis=0, tiled=True)


def call(kernel, name, out_shape, *arrays, flops=0, limit=10, scratch=()):
    moved = sum(a.size * a.dtype.itemsize for a in arrays)
    result = pl.pallas_call(
        lambda *refs: kernel(device_place(), *refs),
        out_shape=out_shape,
        in_specs=[pl.BlockSpec(memory_space=pltpu.VMEM)] * len(arrays),
        out_specs=jax.tree.map(lambda _: pl.BlockSpec(memory_space=pltpu.VMEM), out_shape),
        scratch_shapes=scratch,
        compiler_params=vmem_params(limit),
        cost_estimate=pl.CostEstimate(flops=flops, bytes_accessed=moved, transcendentals=0),
        name=name,
    )(*arrays)
    return list(result) if isinstance(out_shape, list) else result


def device_place():
    return [lax.axis_index(axis) for axis in ("z", "y", "c")]


def turned(a, b):
    return lax.bitwise_and(a + b, 3)


def lanes_from(start, size):
    return pl.ds(pl.multiple_of(start, 128), size)


def columns_of(table):
    rows = lax.broadcasted_iota(jnp.int32, (ROWS, ROWS), 0)
    lanes = lax.broadcasted_iota(jnp.int32, (ROWS, ROWS), 1)
    return lax.dot_general(
        (rows == lanes).astype(F32),
        table,
        (((1,), (1,)), ((), ())),
        precision=lax.Precision.HIGHEST,
        preferred_element_type=F32,
    )


def widened(pair):
    lane = lax.broadcasted_iota(jnp.int32, (pair.shape[0], 128), 1)
    return jnp.where(lane == 0, pair[:, :1], jnp.where(lane == 1, pair[:, 1:2], 0.0))


def bf16_parts(value, count):
    parts = []
    for _ in range(count - 1):
        parts.append(value.astype(BF16))
        value = value - parts[-1].astype(F32)
    return parts + [value.astype(BF16)]


def readout_kernel(
    decay_ref, routes_ref, hidden_ref, qkv_ref, state_ref, gain_ref, out_ref
):
    y = lax.axis_index("y")
    cols = hidden_ref.shape[2] // 16
    depth = out_ref.shape[2] - 128

    @pl.when(pl.program_id(0) == 0)
    def _():
        names = widened(columns_of(routes_ref[y].astype(F32)))
        for i in range(16):
            rows = hidden_ref[y, :, i * cols : (i + 1) * cols].astype(F32)
            first = jnp.concatenate([rows[:, :128], rows[:, 128:256]], axis=0)
            last = jnp.concatenate([rows[:, 256:], names], axis=0)
            out_ref[i, :16, depth:] = first.astype(BF16)
            out_ref[i, 16:, depth:] = last.astype(BF16)

    n, size = STEPS * ROWS, state_ref.shape[2]
    heads = state_ref.shape[1]
    row = lax.broadcasted_iota(jnp.int32, (n, size), 0)
    row_in = row % ROWS
    row_t = lax.broadcasted_iota(jnp.int32, (n, n), 0)
    row_s = lax.broadcasted_iota(jnp.int32, (n, n), 1)
    for h in range(heads):
        lanes = slice(h * size, (h + 1) * size)
        q, k, v = [
            qkv_ref[:, i, :, lanes].astype(F32).reshape(n, size).astype(BF16) for i in range(3)
        ]
        q_twice = jnp.concatenate([q, q], axis=1)
        carried = jnp.zeros((n, size), F32)
        for pair in range(ROWS // 2):
            wide = jnp.concatenate([state_ref[2 * pair, h], state_ref[2 * pair + 1, h]], axis=1)
            both = jnp.dot(
                q_twice, jnp.concatenate(bf16_parts(wide, 2), axis=0), preferred_element_type=F32
            )
            carried = jnp.where(row_in == 2 * pair, both[:, :size], carried)
            carried = jnp.where(row_in == 2 * pair + 1, both[:, size:], carried)
        here = lax.broadcasted_iota(jnp.int32, decay_ref.shape, 1) == pl.program_id(0) * heads + h
        decay = jnp.sum(jnp.where(here, decay_ref[...], 0.0), axis=1, keepdims=True)
        decay = [decay[t : t + 1] for t in range(STEPS)]
        run = decay[0]
        first = jnp.broadcast_to(run, (n, size))
        for t in range(1, STEPS):
            run = run * decay[t]
            first = jnp.where(row // ROWS == t, run, first)
        mix = jnp.zeros((n, n), F32)
        for t in range(STEPS):
            run = None
            for s in range(t, -1, -1):
                here = row_t - row_s == (t - s) * ROWS
                mix = jnp.where(here & (row_s // ROWS == s), 1.0 if run is None else run, mix)
                run = decay[s] if run is None else run * decay[s]
        scores = lax.dot_general(q, k, (((1,), (1,)), ((), ())), preferred_element_type=F32)
        o = carried * first + jnp.dot(
            jnp.concatenate(bf16_parts(scores * mix, 2), axis=1),
            jnp.concatenate([v, v], axis=0),
            preferred_element_type=F32,
        )
        o = o * lax.rsqrt(jnp.mean(o * o, axis=-1, keepdims=True) + EPS) * gain_ref[:, lanes]
        o = o.astype(BF16)
        at = lanes_from((pl.program_id(0) * heads + h) * size, size)
        for i in range(16):
            out_ref[i, :, at] = o


def readouts(step_qkv, decay, state, attn_gain, hidden_in, routes):
    heads, size = state.shape[1], state.shape[2]
    at_once = min(heads, 4)
    n = STEPS * ROWS
    packed = heads * size + 128
    return pl.pallas_call(
        readout_kernel,
        out_shape=jax.ShapeDtypeStruct((16, n, packed), BF16),
        grid=(heads // at_once,),
        in_specs=[
            pl.BlockSpec(decay.shape, lambda i: (0, 0)),
            pl.BlockSpec((STEPS, 2, ROWS), lambda i: (0, 0, 0)),
            pl.BlockSpec(hidden_in.shape, lambda i: (0, 0, 0)),
            pl.BlockSpec((STEPS, 3, ROWS, at_once * size), lambda i: (0, 0, 0, i)),
            pl.BlockSpec((ROWS, at_once, size, size), lambda i: (0, i, 0, 0)),
            pl.BlockSpec((1, at_once * size), lambda i: (0, i)),
        ],
        out_specs=pl.BlockSpec((16, n, packed), lambda i: (0, 0, 0)),
        compiler_params=vmem_params(56),
        cost_estimate=pl.CostEstimate(
            flops=2 * STEPS * ROWS * ROWS * heads * size * size * 2,
            bytes_accessed=state.size * 4,
            transcendentals=0,
        ),
        name="readout",
    )(
        decay,
        routes.transpose(0, 2, 1),
        hidden_in,
        step_qkv.transpose(0, 2, 1, 3),
        state,
        attn_gain.reshape(1, -1),
    )


def project_kernel(place_ref, got_ref, weight_ref, mine_ref, other_ref):
    c = place_ref[2]
    depth = weight_ref.shape[0]
    halves = []
    for part in range(2):
        rows = got_ref[8 * part : 8 * part + 8, :, :depth].reshape(256, depth)
        halves.append(jnp.dot(rows, weight_ref[...], preferred_element_type=F32))
    mine = jnp.where(c == 0, halves[0], halves[1]).astype(BF16)
    other = jnp.where(c == 0, halves[1], halves[0]).astype(BF16)
    mine_ref[...] = mine.reshape(mine_ref.shape)
    other_ref[...] = other.reshape(other_ref.shape)


def project(got, weight):
    out = [jax.ShapeDtypeStruct((8, STEPS, ROWS, weight.shape[1]), BF16)] * 2
    return call(project_kernel, "project", out, got, weight, flops=1024 * weight.size)


def by_y_kernel(place_ref, mine_ref, got_ref, *out_refs):
    y = place_ref[1]
    for k, ref in enumerate(out_refs):
        t = turned(y, k)
        for i in range(8):
            ref[i] = (mine_ref[i, t].astype(F32) + got_ref[i, t].astype(F32)).astype(BF16)


def sums_by_y(mine, got):
    out = [jax.ShapeDtypeStruct((8,) + mine.shape[2:], BF16)] * 4
    return call(by_y_kernel, "sums_by_y", out, mine, got)


def slots_kernel(place_ref, got_ref, select_ref, hidden_ref):
    c = place_ref[2]
    depth = got_ref.shape[2] - 128
    names = []
    for i in range(8):
        tail = got_ref[8 * c + i, :, depth:].astype(F32)
        hidden_ref[i] = jnp.concatenate([tail[:8], tail[8:16], tail[16:24]], axis=1)
        names.append(tail[24:])
    names = jnp.concatenate(names, axis=0)
    n = names.shape[0]
    across = names.T
    down_i = lax.broadcasted_iota(jnp.int32, (n, n), 0)
    over_i = lax.broadcasted_iota(jnp.int32, (n, n), 1)
    earlier = (down_i // ROWS == over_i // ROWS) & (down_i < over_i)
    slot = lax.broadcasted_iota(jnp.int32, (256, n), 0)
    base = lax.broadcasted_iota(jnp.int32, (1, n), 1) // ROWS * 2
    select = jnp.zeros((256, n), F32)
    for j in range(2):
        mine = across[j : j + 1, :]
        rank = jnp.zeros((1, n), F32)
        for other in range(2):
            same = (names[:, other : other + 1] == mine) & earlier
            rank += jnp.sum(same.astype(F32), axis=0, keepdims=True)
        target = mine.astype(jnp.int32) * 16 + base + rank.astype(jnp.int32)
        select += (slot == target).astype(F32)
    select_ref[...] = select.astype(BF16)


def slots(got, cols):
    out = [jax.ShapeDtypeStruct((256, 64), BF16), jax.ShapeDtypeStruct((8, ROWS, cols), F32)]
    return call(slots_kernel, "slots", out, got, flops=1 << 20)


def attend_kernel(place_ref, select_ref, hidden_ref, *refs):
    sum_refs, out_ref = refs[:4], refs[4]
    rows = []
    for i in range(8):
        total = hidden_ref[i]
        for ref in sum_refs:
            total += ref[i].astype(F32)
        rows.append(total)
        total = total.astype(BF16)
        for j in range(2):
            out_ref[8 * j + i, 2] = total
    rows = jnp.concatenate(rows, axis=0).astype(BF16)
    sent = jnp.dot(select_ref[...], rows, preferred_element_type=F32)
    for i in range(16):
        for j in range(2):
            out_ref[i, j] = sent[16 * i + 8 * j : 16 * i + 8 * j + 8].astype(BF16)


def attend(select, hidden, sums):
    out = jax.ShapeDtypeStruct((16, 3) + hidden.shape[1:], BF16)
    return call(attend_kernel, "attend", out, select, hidden, *sums, flops=1 << 23)


def norm_kernel(place_ref, gain_ref, got_ref, *out_refs):
    y = place_ref[1]
    cols = got_ref.shape[3]
    total = jnp.zeros((16, cols), F32)
    slots = []
    for i in range(16):
        value = jnp.concatenate([got_ref[i, j].astype(F32) for j in range(2)], axis=0)
        slots.append(value)
        total += value * value
    mean = jnp.sum(total, axis=-1, keepdims=True) / (16 * cols)
    scale = lax.rsqrt(mean + EPS)
    for i in range(16):
        at = slice(i * cols, (i + 1) * cols)
        value = (slots[i] * scale * gain_ref[:, at]).astype(BF16)
        for out_ref in out_refs:
            out_ref[:, at] = value
    for k, out_ref in enumerate(out_refs):
        for i in range(2):
            at = slice((16 + i) * cols, (17 + i) * cols)
            rows = [got_ref[turned(y, 4 - k) * 4 + 2 * core + i, 2] for core in range(2)]
            rows = jnp.concatenate([r.astype(F32) for r in rows], axis=0)
            out_ref[:, at] = rows.astype(BF16)


def norm(gain, got):
    out = [jax.ShapeDtypeStruct((16, 18 * got.shape[3]), BF16)] * 4
    return call(norm_kernel, "norm", out, gain.reshape(1, -1), got)


def owned_kernel(place_ref, *refs):
    own_refs, other_refs, out_ref = refs[:4], refs[4:8], refs[8]
    z, y, c = place_ref
    start = own_refs[0].shape[1] - out_ref.shape[2]
    for k in range(4):
        rows = jnp.where(z // 2 == c, own_refs[k][:, start:], other_refs[k][:, start:])
        rows = rows.astype(F32)
        out_ref[turned(y, k)] = jnp.where(c == 0, rows[:ROWS], rows[ROWS:]).astype(BF16)


def owned(by_y, by_core, share):
    out = jax.ShapeDtypeStruct((STEPS, ROWS, share), BF16)
    return call(owned_kernel, "owned", out, *by_y, *by_core)


def fetch_kernel(after_ref, *refs):
    in_refs, out_refs, done_ref, sems = refs[:3], refs[3:6], refs[6], refs[7]
    copies = [pltpu.make_async_copy(a, b, sems.at[i]) for i, (a, b) in enumerate(zip(in_refs, out_refs))]
    for copy in copies:
        copy.start()
    done_ref[...] = jnp.zeros_like(done_ref)
    for copy in copies:
        copy.wait()


def fetch(after, *weights):
    return pl.pallas_call(
        fetch_kernel,
        out_shape=[pltpu.VMEM(w.shape, w.dtype) for w in weights]
        + [pltpu.VMEM((8, 128), F32)],
        in_specs=[pl.BlockSpec(memory_space=pl.ANY)]
        + [pl.BlockSpec(memory_space=pltpu.HBM)] * len(weights),
        out_specs=[pl.BlockSpec(memory_space=pltpu.VMEM)] * (len(weights) + 1),
        scratch_shapes=[pltpu.SemaphoreType.DMA((len(weights),))],
        compiler_params=vmem_params(36),
        cost_estimate=pl.CostEstimate(
            flops=0, bytes_accessed=sum(2 * w.size for w in weights), transcendentals=0
        ),
        name="fetch",
    )(after, *weights)


def hidden_kernel(place_ref, *refs):
    x_refs, (gate_ref, up_ref, down_ref, _, hidden_ref, theirs_ref) = refs[:8], refs[8:]
    share = theirs_ref.shape[2]
    y, c = place_ref[1], place_ref[2]
    x = jnp.concatenate([r[:, : gate_ref.shape[1]] for r in x_refs], axis=0)
    across = (((1,), (1,)), ((), ()))
    gate = lax.dot_general(gate_ref[...], x, across, preferred_element_type=F32)
    up = lax.dot_general(up_ref[...], x, across, preferred_element_type=F32)
    hidden = (gate / (1.0 + jnp.exp(-gate)) * up).T.astype(BF16)
    n = hidden.shape[0]
    row = lax.broadcasted_iota(jnp.int32, (n, n), 0)
    lane = lax.broadcasted_iota(jnp.int32, (n, n), 1)
    source = lax.bitwise_xor(row // 64, c) * 64 + turned(row // 2, 4 - y) * 16
    source += row // 8 % 8 * 2 + row % 2
    moved = (lane == source).astype(F32).astype(BF16)
    hidden = jnp.dot(moved, hidden, preferred_element_type=F32).astype(BF16)
    hidden_ref[...] = hidden
    for k in range(4):
        block = turned(y, k) * 2 + (1 - c)
        at = pl.ds(pl.multiple_of(block * share, 128), share)
        theirs_ref[k] = jnp.dot(hidden, down_ref[:, at], preferred_element_type=F32).astype(BF16)


def hidden_units(pieces, gate, up, down_weight, done, share):
    units = gate.shape[0]
    rows = sum(p.shape[0] for p in pieces)
    out = [
        jax.ShapeDtypeStruct((rows, units), BF16),
        jax.ShapeDtypeStruct((4, rows, share), BF16),
    ]
    flops = 5 * rows * gate.size
    arrays = (*pieces, gate, up, down_weight, done)
    return call(hidden_kernel, "hidden_units", out, *arrays, flops=flops)


def down_kernel(place_ref, hidden_ref, down_ref, out_ref):
    share = out_ref.shape[2]
    y, c = place_ref[1], place_ref[2]
    for k in range(4):
        at = lanes_from((turned(y, k) * 2 + c) * share, share)
        out_ref[k] = jnp.dot(hidden_ref[...], down_ref[:, at], preferred_element_type=F32)


def down(hidden, weight, share):
    out = jax.ShapeDtypeStruct((4, hidden.shape[0], share), F32)
    flops = hidden.shape[0] * weight.size
    return call(down_kernel, "down", out, hidden, weight, flops=flops)


def cores_kernel(place_ref, ours_ref, theirs_ref, out_ref):
    for k in range(4):
        total = ours_ref[k] + theirs_ref[k].astype(F32)
        out_ref[turned(place_ref[1], k)] = total.astype(BF16)


def cores_sum(ours, theirs):
    out = jax.ShapeDtypeStruct(theirs.shape, BF16)
    out = call(cores_kernel, "cores_sum", out, ours, theirs)
    return out.reshape(64, 8, theirs.shape[2])


def weights_kernel(place_ref, routes_ref, weights_ref, out_ref):
    n = STEPS * ROWS
    names = [columns_of(routes_ref[t].astype(F32)) for t in range(STEPS)]
    names = widened(jnp.concatenate(names, axis=0))
    weights = [columns_of(weights_ref[t]) for t in range(STEPS)]
    weights = jnp.concatenate(weights, axis=0)
    down_i = lax.broadcasted_iota(jnp.int32, (n, n), 0)
    over_i = lax.broadcasted_iota(jnp.int32, (n, n), 1)
    earlier = (down_i // ROWS == over_i // ROWS) & (over_i < down_i)
    across = names.T
    slot = lax.broadcasted_iota(jnp.int32, (n, 128), 1)
    step = lax.broadcasted_iota(jnp.int32, (n, 1), 0) // ROWS
    mix = jnp.zeros((n, 128), F32)
    for j in range(2):
        mine = names[:, j : j + 1]
        rank = jnp.zeros((n, 1), F32)
        for other in range(2):
            same = (across[other : other + 1, :] == mine) & earlier
            rank += jnp.sum(same.astype(F32), axis=1, keepdims=True)
        target = mine.astype(jnp.int32) * 8 + 2 * step + rank.astype(jnp.int32)
        mix += jnp.where(slot == target, weights[:, j : j + 1], 0.0)
    out_ref[...] = jnp.concatenate(bf16_parts(mix, 3), axis=1)


def mix_weights(routes, weights):
    out = jax.ShapeDtypeStruct((STEPS * ROWS, 384), BF16)
    arrays = (routes.transpose(0, 2, 1), weights.transpose(0, 2, 1))
    return call(weights_kernel, "mix_weights", out, *arrays, flops=1 << 20)


def mix_kernel(place_ref, mix_ref, back_ref, out_ref):
    back = back_ref[...].astype(F32)
    back = (back[:16] + back[16:32]) + (back[32:48] + back[48:])
    back = back.reshape(128, back.shape[2]).astype(BF16)
    out_ref[...] = jnp.dot(
        mix_ref[...], jnp.concatenate([back] * 3, axis=0), preferred_element_type=F32
    ).astype(BF16)


def mixed_rows(mix, back):
    out = jax.ShapeDtypeStruct((STEPS * ROWS, back.shape[2]), BF16)
    return call(mix_kernel, "mix", out, mix, back, flops=1 << 24)


def shards(
    hidden_in,
    step_qkv,
    decay_rates,
    kv_state,
    attn_gain,
    out_proj,
    ffn_gain,
    routes,
    route_weights,
    w_gate,
    w_up,
    w_down,
):
    share = hidden_in.shape[2] // 8

    sent = readouts(step_qkv, decay_rates, kv_state, attn_gain, hidden_in, routes)
    got = exchange(sent, ("z", "x"))

    mine, other = project(got, out_proj)
    sums = sums_by_y(mine, over("c", other, 1))
    select, hidden = slots(got, out_proj.shape[1])
    sums = sums[:1] + [over("y", sums[k], k) for k in (1, 2, 3)]

    pieces = norm(ffn_gain, exchange(attend(select, hidden, sums), ("z", "x")))
    by_y = pieces[:1] + [over("y", pieces[k], -k) for k in (1, 2, 3)]
    gate, up, down_weight, done = fetch(
        pieces[1], w_gate[0].swapaxes(0, 1), w_up[0].swapaxes(0, 1), w_down[0]
    )
    by_y, done = lax.optimization_barrier((by_y, done))
    by_core = [over("c", piece, 1) for piece in by_y]

    hidden, theirs = hidden_units(by_y + by_core, gate, up, down_weight, done, share)
    theirs = over("c", theirs, 1)
    sums = cores_sum(down(hidden, down_weight, share), theirs)

    attended = owned(by_y, by_core, share)
    mix = mix_weights(routes, route_weights)
    mixed = mixed_rows(mix, exchange(sums, ("y", "z", "x")))
    return attended, mixed.reshape(STEPS, ROWS, share)


def solution(mesh):
    exp, head = ("z", "x"), ("y", "c")
    return jax.shard_map(
        shards,
        mesh=jax.sharding.Mesh(mesh.devices.reshape(4, 2, 4, 4), head + exp),
        in_specs=(
            P(None, exp, None),
            P(None, exp, None, head),
            P(None, head),
            P(exp, head, None, None),
            P(head),
            P(head, exp),
            P(),
            P(None, exp, None),
            P(None, exp, None),
            P(exp, None, head),
            P(exp, None, head),
            P(exp, head, None),
        ),
        out_specs=(P(None, exp, head), P(None, exp, head)),
        check_vma=False,
    )
```

```python
import functools

import jax
import jax.numpy as jnp
from jax import lax
from jax.experimental import pallas as pl
from jax.experimental.pallas import tpu as pltpu
from jax.sharding import PartitionSpec as P

STEPS = 4
ROWS = 8
EPS = 1e-06
F32 = jnp.float32
BF16 = jnp.bfloat16
MIB = 1 << 20


def vmem_params(mib):
    return pltpu.CompilerParams(vmem_limit_bytes=mib * MIB)


def over(axis, value, shift):
    size = lax.axis_size(axis)
    return lax.ppermute(value, axis, [(i, (i + shift) % size) for i in range(size)])


def exchange(value, axes):
    return lax.all_to_all(value, axes, split_axis=0, concat_axis=0, tiled=True)


def call(kernel, name, out_shape, *arrays, flops=0, limit=10, scratch=()):
    moved = sum(a.size * a.dtype.itemsize for a in arrays)
    result = pl.pallas_call(
        lambda *refs: kernel(device_place(), *refs),
        out_shape=out_shape,
        in_specs=[pl.BlockSpec(memory_space=pltpu.VMEM)] * len(arrays),
        out_specs=jax.tree.map(lambda _: pl.BlockSpec(memory_space=pltpu.VMEM), out_shape),
        scratch_shapes=scratch,
        compiler_params=vmem_params(limit),
        cost_estimate=pl.CostEstimate(flops=flops, bytes_accessed=moved, transcendentals=0),
        name=name,
    )(*arrays)
    return list(result) if isinstance(out_shape, list) else result


def device_place():
    return [lax.axis_index(axis) for axis in ("z", "y", "c")]


def turned(a, b):
    return lax.bitwise_and(a + b, 3)


def lanes_from(start, size):
    return pl.ds(pl.multiple_of(start, 128), size)


def columns_of(table):
    rows = lax.broadcasted_iota(jnp.int32, (ROWS, ROWS), 0)
    lanes = lax.broadcasted_iota(jnp.int32, (ROWS, ROWS), 1)
    return lax.dot_general(
        (rows == lanes).astype(F32),
        table,
        (((1,), (1,)), ((), ())),
        precision=lax.Precision.HIGHEST,
        preferred_element_type=F32,
    )


def widened(pair):
    lane = lax.broadcasted_iota(jnp.int32, (pair.shape[0], 128), 1)
    return jnp.where(lane == 0, pair[:, :1], jnp.where(lane == 1, pair[:, 1:2], 0.0))


def bf16_parts(value, count):
    parts = []
    for _ in range(count - 1):
        parts.append(value.astype(BF16))
        value = value - parts[-1].astype(F32)
    return parts + [value.astype(BF16)]


def readout_kernel(
    decay_ref, routes_ref, hidden_ref, qkv_ref, state_ref, gain_ref, out_ref
):
    y = lax.axis_index("y")
    cols = hidden_ref.shape[2] // 16
    depth = out_ref.shape[2] - 128

    @pl.when(pl.program_id(0) == 0)
    def _():
        names = widened(columns_of(routes_ref[y].astype(F32)))
        for i in range(16):
            rows = hidden_ref[y, :, i * cols : (i + 1) * cols].astype(F32)
            first = jnp.concatenate([rows[:, :128], rows[:, 128:256]], axis=0)
            last = jnp.concatenate([rows[:, 256:], names], axis=0)
            out_ref[i, :16, depth:] = first.astype(BF16)
            out_ref[i, 16:, depth:] = last.astype(BF16)

    n, size = STEPS * ROWS, state_ref.shape[2]
    heads = state_ref.shape[1]
    row = lax.broadcasted_iota(jnp.int32, (n, size), 0)
    row_in = row % ROWS
    row_t = lax.broadcasted_iota(jnp.int32, (n, n), 0)
    row_s = lax.broadcasted_iota(jnp.int32, (n, n), 1)
    for h in range(heads):
        lanes = slice(h * size, (h + 1) * size)
        q, k, v = [
            qkv_ref[:, i, :, lanes].astype(F32).reshape(n, size).astype(BF16) for i in range(3)
        ]
        q_twice = jnp.concatenate([q, q], axis=1)
        carried = jnp.zeros((n, size), F32)
        for pair in range(ROWS // 2):
            wide = jnp.concatenate([state_ref[2 * pair, h], state_ref[2 * pair + 1, h]], axis=1)
            both = jnp.dot(
                q_twice, jnp.concatenate(bf16_parts(wide, 2), axis=0), preferred_element_type=F32
            )
            carried = jnp.where(row_in == 2 * pair, both[:, :size], carried)
            carried = jnp.where(row_in == 2 * pair + 1, both[:, size:], carried)
        here = lax.broadcasted_iota(jnp.int32, decay_ref.shape, 1) == pl.program_id(0) * heads + h
        decay = jnp.sum(jnp.where(here, decay_ref[...], 0.0), axis=1, keepdims=True)
        decay = [decay[t : t + 1] for t in range(STEPS)]
        run = decay[0]
        first = jnp.broadcast_to(run, (n, size))
        for t in range(1, STEPS):
            run = run * decay[t]
            first = jnp.where(row // ROWS == t, run, first)
        mix = jnp.zeros((n, n), F32)
        for t in range(STEPS):
            run = None
            for s in range(t, -1, -1):
                here = row_t - row_s == (t - s) * ROWS
                mix = jnp.where(here & (row_s // ROWS == s), 1.0 if run is None else run, mix)
                run = decay[s] if run is None else run * decay[s]
        scores = lax.dot_general(q, k, (((1,), (1,)), ((), ())), preferred_element_type=F32)
        o = carried * first + jnp.dot(
            jnp.concatenate(bf16_parts(scores * mix, 2), axis=1),
            jnp.concatenate([v, v], axis=0),
            preferred_element_type=F32,
        )
        o = o * lax.rsqrt(jnp.mean(o * o, axis=-1, keepdims=True) + EPS) * gain_ref[:, lanes]
        o = o.astype(BF16)
        at = lanes_from((pl.program_id(0) * heads + h) * size, size)
        for i in range(16):
            out_ref[i, :, at] = o


def readouts(step_qkv, decay, state, attn_gain, hidden_in, routes):
    heads, size = state.shape[1], state.shape[2]
    at_once = min(heads, 4)
    n = STEPS * ROWS
    packed = heads * size + 128
    return pl.pallas_call(
        readout_kernel,
        out_shape=pltpu.VMEM((16, n, packed), BF16),
        grid=(heads // at_once,),
        in_specs=[
            pl.BlockSpec(decay.shape, lambda i: (0, 0)),
            pl.BlockSpec((STEPS, 2, ROWS), lambda i: (0, 0, 0)),
            pl.BlockSpec(hidden_in.shape, lambda i: (0, 0, 0)),
            pl.BlockSpec((STEPS, 3, ROWS, at_once * size), lambda i: (0, 0, 0, i)),
            pl.BlockSpec((ROWS, at_once, size, size), lambda i: (0, i, 0, 0)),
            pl.BlockSpec((1, at_once * size), lambda i: (0, i)),
        ],
        out_specs=pl.BlockSpec((16, n, packed), lambda i: (0, 0, 0)),
        compiler_params=vmem_params(58),
        cost_estimate=pl.CostEstimate(
            flops=2 * STEPS * ROWS * ROWS * heads * size * size * 2,
            bytes_accessed=state.size * 4,
            transcendentals=0,
        ),
        name="readout",
    )(
        decay,
        routes.transpose(0, 2, 1),
        hidden_in,
        step_qkv.transpose(0, 2, 1, 3),
        state,
        attn_gain.reshape(1, -1),
    )


def project_kernel(place_ref, got_ref, weight_ref, mine_ref, other_ref):
    c = place_ref[2]
    depth = weight_ref.shape[0]
    halves = []
    for part in range(2):
        rows = got_ref[8 * part : 8 * part + 8, :, :depth].reshape(256, depth)
        halves.append(jnp.dot(rows, weight_ref[...], preferred_element_type=F32))
    mine = jnp.where(c == 0, halves[0], halves[1]).astype(BF16)
    other = jnp.where(c == 0, halves[1], halves[0]).astype(BF16)
    mine_ref[...] = mine.reshape(mine_ref.shape)
    other_ref[...] = other.reshape(other_ref.shape)


def project(got, weight):
    out = [jax.ShapeDtypeStruct((8, STEPS, ROWS, weight.shape[1]), BF16)] * 2
    return call(project_kernel, "project", out, got, weight, flops=1024 * weight.size)


def by_y_kernel(place_ref, mine_ref, got_ref, *out_refs):
    y = place_ref[1]
    for k, ref in enumerate(out_refs):
        t = turned(y, k)
        for i in range(8):
            ref[i] = (mine_ref[i, t].astype(F32) + got_ref[i, t].astype(F32)).astype(BF16)


def sums_by_y(mine, got):
    out = [jax.ShapeDtypeStruct((8,) + mine.shape[2:], BF16)] * 4
    return call(by_y_kernel, "sums_by_y", out, mine, got)


def slots_kernel(place_ref, got_ref, select_ref, hidden_ref):
    c = place_ref[2]
    depth = got_ref.shape[2] - 128
    names = []
    for i in range(8):
        tail = got_ref[8 * c + i, :, depth:].astype(F32)
        hidden_ref[i] = jnp.concatenate([tail[:8], tail[8:16], tail[16:24]], axis=1)
        names.append(tail[24:])
    names = jnp.concatenate(names, axis=0)
    n = names.shape[0]
    across = names.T
    down_i = lax.broadcasted_iota(jnp.int32, (n, n), 0)
    over_i = lax.broadcasted_iota(jnp.int32, (n, n), 1)
    earlier = (down_i // ROWS == over_i // ROWS) & (down_i < over_i)
    slot = lax.broadcasted_iota(jnp.int32, (256, n), 0)
    base = lax.broadcasted_iota(jnp.int32, (1, n), 1) // ROWS * 2
    select = jnp.zeros((256, n), F32)
    for j in range(2):
        mine = across[j : j + 1, :]
        rank = jnp.zeros((1, n), F32)
        for other in range(2):
            same = (names[:, other : other + 1] == mine) & earlier
            rank += jnp.sum(same.astype(F32), axis=0, keepdims=True)
        target = mine.astype(jnp.int32) * 16 + base + rank.astype(jnp.int32)
        select += (slot == target).astype(F32)
    select_ref[...] = select.astype(BF16)


def slots(got, cols):
    out = [jax.ShapeDtypeStruct((256, 64), BF16), jax.ShapeDtypeStruct((8, ROWS, cols), F32)]
    return call(slots_kernel, "slots", out, got, flops=1 << 20)


def attend_kernel(place_ref, select_ref, hidden_ref, *refs):
    sum_refs, out_ref = refs[:4], refs[4]
    rows = []
    for i in range(8):
        total = hidden_ref[i]
        for ref in sum_refs:
            total += ref[i].astype(F32)
        rows.append(total)
        total = total.astype(BF16)
        for j in range(2):
            out_ref[8 * j + i, 2] = total
    rows = jnp.concatenate(rows, axis=0).astype(BF16)
    sent = jnp.dot(select_ref[...], rows, preferred_element_type=F32)
    for i in range(16):
        for j in range(2):
            out_ref[i, j] = sent[16 * i + 8 * j : 16 * i + 8 * j + 8].astype(BF16)


def attend(select, hidden, sums):
    out = jax.ShapeDtypeStruct((16, 3) + hidden.shape[1:], BF16)
    return call(attend_kernel, "attend", out, select, hidden, *sums, flops=1 << 23)


def norm_kernel(place_ref, gain_ref, got_ref, *out_refs):
    y = place_ref[1]
    cols = got_ref.shape[3]
    total = jnp.zeros((16, cols), F32)
    slots = []
    for i in range(16):
        value = jnp.concatenate([got_ref[i, j].astype(F32) for j in range(2)], axis=0)
        slots.append(value)
        total += value * value
    mean = jnp.sum(total, axis=-1, keepdims=True) / (16 * cols)
    scale = lax.rsqrt(mean + EPS)
    for i in range(16):
        at = slice(i * cols, (i + 1) * cols)
        value = (slots[i] * scale * gain_ref[:, at]).astype(BF16)
        for out_ref in out_refs:
            out_ref[:, at] = value
    for k, out_ref in enumerate(out_refs):
        for i in range(2):
            at = slice((16 + i) * cols, (17 + i) * cols)
            rows = [got_ref[turned(y, 4 - k) * 4 + 2 * core + i, 2] for core in range(2)]
            rows = jnp.concatenate([r.astype(F32) for r in rows], axis=0)
            out_ref[:, at] = rows.astype(BF16)


def norm(gain, got):
    out = [jax.ShapeDtypeStruct((16, 18 * got.shape[3]), BF16)] * 4
    return call(norm_kernel, "norm", out, gain.reshape(1, -1), got)


def owned_kernel(place_ref, *refs):
    own_refs, other_refs, out_ref = refs[:4], refs[4:8], refs[8]
    z, y, c = place_ref
    start = own_refs[0].shape[1] - out_ref.shape[2]
    for k in range(4):
        rows = jnp.where(z // 2 == c, own_refs[k][:, start:], other_refs[k][:, start:])
        rows = rows.astype(F32)
        out_ref[turned(y, k)] = jnp.where(c == 0, rows[:ROWS], rows[ROWS:]).astype(BF16)


def owned(by_y, by_core, share):
    out = jax.ShapeDtypeStruct((STEPS, ROWS, share), BF16)
    return call(owned_kernel, "owned", out, *by_y, *by_core)


def fetch_kernel(after_ref, *refs):
    in_refs, out_refs, done_ref, sems = refs[:3], refs[3:6], refs[6], refs[7]
    copies = [pltpu.make_async_copy(a, b, sems.at[i]) for i, (a, b) in enumerate(zip(in_refs, out_refs))]
    for copy in copies:
        copy.start()
    done_ref[...] = jnp.zeros_like(done_ref)
    for copy in copies:
        copy.wait()


def fetch(after, *weights):
    return pl.pallas_call(
        fetch_kernel,
        out_shape=[pltpu.VMEM(w.shape, w.dtype) for w in weights]
        + [pltpu.VMEM((8, 128), F32)],
        in_specs=[pl.BlockSpec(memory_space=pl.ANY)]
        + [pl.BlockSpec(memory_space=pltpu.HBM)] * len(weights),
        out_specs=[pl.BlockSpec(memory_space=pltpu.VMEM)] * (len(weights) + 1),
        scratch_shapes=[pltpu.SemaphoreType.DMA((len(weights),))],
        compiler_params=vmem_params(36),
        cost_estimate=pl.CostEstimate(
            flops=0, bytes_accessed=sum(2 * w.size for w in weights), transcendentals=0
        ),
        name="fetch",
    )(after, *weights)


def hidden_kernel(place_ref, *refs):
    x_refs, (gate_ref, up_ref, down_ref, _, hidden_ref, theirs_ref) = refs[:8], refs[8:]
    share = theirs_ref.shape[2]
    y, c = place_ref[1], place_ref[2]
    x = jnp.concatenate([r[:, : gate_ref.shape[1]] for r in x_refs], axis=0)
    across = (((1,), (1,)), ((), ()))
    gate = lax.dot_general(gate_ref[...], x, across, preferred_element_type=F32)
    up = lax.dot_general(up_ref[...], x, across, preferred_element_type=F32)
    hidden = (gate / (1.0 + jnp.exp(-gate)) * up).T.astype(BF16)
    n = hidden.shape[0]
    row = lax.broadcasted_iota(jnp.int32, (n, n), 0)
    lane = lax.broadcasted_iota(jnp.int32, (n, n), 1)
    source = lax.bitwise_xor(row // 64, c) * 64 + turned(row // 2, 4 - y) * 16
    source += row // 8 % 8 * 2 + row % 2
    moved = (lane == source).astype(F32).astype(BF16)
    hidden = jnp.dot(moved, hidden, preferred_element_type=F32).astype(BF16)
    hidden_ref[...] = hidden
    for k in range(4):
        block = turned(y, k) * 2 + (1 - c)
        at = pl.ds(pl.multiple_of(block * share, 128), share)
        theirs_ref[k] = jnp.dot(hidden, down_ref[:, at], preferred_element_type=F32).astype(BF16)


def hidden_units(pieces, gate, up, down_weight, done, share):
    units = gate.shape[0]
    rows = sum(p.shape[0] for p in pieces)
    out = [
        jax.ShapeDtypeStruct((rows, units), BF16),
        jax.ShapeDtypeStruct((4, rows, share), BF16),
    ]
    flops = 5 * rows * gate.size
    arrays = (*pieces, gate, up, down_weight, done)
    return call(hidden_kernel, "hidden_units", out, *arrays, flops=flops)


def down_kernel(place_ref, hidden_ref, down_ref, out_ref):
    share = out_ref.shape[2]
    y, c = place_ref[1], place_ref[2]
    for k in range(4):
        at = lanes_from((turned(y, k) * 2 + c) * share, share)
        out_ref[k] = jnp.dot(hidden_ref[...], down_ref[:, at], preferred_element_type=F32)


def down(hidden, weight, share):
    out = jax.ShapeDtypeStruct((4, hidden.shape[0], share), F32)
    flops = hidden.shape[0] * weight.size
    return call(down_kernel, "down", out, hidden, weight, flops=flops)


def cores_kernel(place_ref, ours_ref, theirs_ref, out_ref):
    for k in range(4):
        total = ours_ref[k] + theirs_ref[k].astype(F32)
        out_ref[turned(place_ref[1], k)] = total.astype(BF16)


def cores_sum(ours, theirs):
    out = jax.ShapeDtypeStruct(theirs.shape, BF16)
    out = call(cores_kernel, "cores_sum", out, ours, theirs)
    return out.reshape(64, 8, theirs.shape[2])


def weights_kernel(place_ref, routes_ref, weights_ref, out_ref):
    n = STEPS * ROWS
    names = [columns_of(routes_ref[t].astype(F32)) for t in range(STEPS)]
    names = widened(jnp.concatenate(names, axis=0))
    weights = [columns_of(weights_ref[t]) for t in range(STEPS)]
    weights = jnp.concatenate(weights, axis=0)
    down_i = lax.broadcasted_iota(jnp.int32, (n, n), 0)
    over_i = lax.broadcasted_iota(jnp.int32, (n, n), 1)
    earlier = (down_i // ROWS == over_i // ROWS) & (over_i < down_i)
    across = names.T
    slot = lax.broadcasted_iota(jnp.int32, (n, 128), 1)
    step = lax.broadcasted_iota(jnp.int32, (n, 1), 0) // ROWS
    mix = jnp.zeros((n, 128), F32)
    for j in range(2):
        mine = names[:, j : j + 1]
        rank = jnp.zeros((n, 1), F32)
        for other in range(2):
            same = (across[other : other + 1, :] == mine) & earlier
            rank += jnp.sum(same.astype(F32), axis=1, keepdims=True)
        target = mine.astype(jnp.int32) * 8 + 2 * step + rank.astype(jnp.int32)
        mix += jnp.where(slot == target, weights[:, j : j + 1], 0.0)
    out_ref[...] = jnp.concatenate(bf16_parts(mix, 3), axis=1)


def mix_weights(routes, weights):
    out = jax.ShapeDtypeStruct((STEPS * ROWS, 384), BF16)
    arrays = (routes.transpose(0, 2, 1), weights.transpose(0, 2, 1))
    return call(weights_kernel, "mix_weights", out, *arrays, flops=1 << 20)


def mix_kernel(place_ref, mix_ref, back_ref, out_ref):
    back = back_ref[...].astype(F32)
    back = (back[:16] + back[16:32]) + (back[32:48] + back[48:])
    back = back.reshape(128, back.shape[2]).astype(BF16)
    out_ref[...] = jnp.dot(
        mix_ref[...], jnp.concatenate([back] * 3, axis=0), preferred_element_type=F32
    ).astype(BF16)


def mixed_rows(mix, back):
    out = jax.ShapeDtypeStruct((STEPS * ROWS, back.shape[2]), BF16)
    return call(mix_kernel, "mix", out, mix, back, flops=1 << 24)


def shards(
    hidden_in,
    step_qkv,
    decay_rates,
    kv_state,
    attn_gain,
    out_proj,
    ffn_gain,
    routes,
    route_weights,
    w_gate,
    w_up,
    w_down,
):
    share = hidden_in.shape[2] // 8

    sent = readouts(step_qkv, decay_rates, kv_state, attn_gain, hidden_in, routes)
    got = exchange(sent, ("z", "x"))

    mine, other = project(got, out_proj)
    sums = sums_by_y(mine, over("c", other, 1))
    select, hidden = slots(got, out_proj.shape[1])
    sums = sums[:1] + [over("y", sums[k], k) for k in (1, 2, 3)]

    pieces = norm(ffn_gain, exchange(attend(select, hidden, sums), ("z", "x")))
    by_y = pieces[:1] + [over("y", pieces[k], -k) for k in (1, 2, 3)]
    gate, up, down_weight, done = fetch(
        pieces[1], w_gate[0].swapaxes(0, 1), w_up[0].swapaxes(0, 1), w_down[0]
    )
    by_y[2], done = lax.optimization_barrier((by_y[2], done))
    by_core = [over("c", piece, 1) for piece in by_y]

    hidden, theirs = hidden_units(by_y + by_core, gate, up, down_weight, done, share)
    theirs = over("c", theirs, 1)
    sums = cores_sum(down(hidden, down_weight, share), theirs)

    attended = owned(by_y, by_core, share)
    mix = mix_weights(routes, route_weights)
    mixed = mixed_rows(mix, exchange(sums, ("y", "z", "x")))
    return attended, mixed.reshape(STEPS, ROWS, share)


def solution(mesh):
    exp, head = ("z", "x"), ("y", "c")
    return jax.shard_map(
        shards,
        mesh=jax.sharding.Mesh(mesh.devices.reshape(4, 2, 4, 4), head + exp),
        in_specs=(
            P(None, exp, None),
            P(None, exp, None, head),
            P(None, head),
            P(exp, head, None, None),
            P(head),
            P(head, exp),
            P(),
            P(None, exp, None),
            P(None, exp, None),
            P(exp, None, head),
            P(exp, None, head),
            P(exp, head, None),
        ),
        out_specs=(P(None, exp, head), P(None, exp, head)),
        check_vma=False,
    )
```

```python
import functools

import jax
import jax.numpy as jnp
from jax import lax
from jax.experimental import pallas as pl
from jax.experimental.pallas import tpu as pltpu
from jax.sharding import PartitionSpec as P

STEPS = 4
ROWS = 8
EPS = 1e-06
F32 = jnp.float32
BF16 = jnp.bfloat16
MIB = 1 << 20


def vmem_params(mib):
    return pltpu.CompilerParams(vmem_limit_bytes=mib * MIB)


def over(axis, value, shift):
    size = lax.axis_size(axis)
    return lax.ppermute(value, axis, [(i, (i + shift) % size) for i in range(size)])


def exchange(value, axes):
    return lax.all_to_all(value, axes, split_axis=0, concat_axis=0, tiled=True)


def call(kernel, name, out_shape, *arrays, flops=0, limit=10, scratch=()):
    moved = sum(a.size * a.dtype.itemsize for a in arrays)
    result = pl.pallas_call(
        lambda *refs: kernel(device_place(), *refs),
        out_shape=out_shape,
        in_specs=[pl.BlockSpec(memory_space=pltpu.VMEM)] * len(arrays),
        out_specs=jax.tree.map(lambda _: pl.BlockSpec(memory_space=pltpu.VMEM), out_shape),
        scratch_shapes=scratch,
        compiler_params=vmem_params(limit),
        cost_estimate=pl.CostEstimate(flops=flops, bytes_accessed=moved, transcendentals=0),
        name=name,
    )(*arrays)
    return list(result) if isinstance(out_shape, list) else result


def device_place():
    return [lax.axis_index(axis) for axis in ("z", "y", "c")]


def turned(a, b):
    return lax.bitwise_and(a + b, 3)


def lanes_from(start, size):
    return pl.ds(pl.multiple_of(start, 128), size)


def columns_of(table):
    rows = lax.broadcasted_iota(jnp.int32, (ROWS, ROWS), 0)
    lanes = lax.broadcasted_iota(jnp.int32, (ROWS, ROWS), 1)
    return lax.dot_general(
        (rows == lanes).astype(F32),
        table,
        (((1,), (1,)), ((), ())),
        precision=lax.Precision.HIGHEST,
        preferred_element_type=F32,
    )


def widened(pair):
    lane = lax.broadcasted_iota(jnp.int32, (pair.shape[0], 128), 1)
    return jnp.where(lane == 0, pair[:, :1], jnp.where(lane == 1, pair[:, 1:2], 0.0))


def bf16_parts(value, count):
    parts = []
    for _ in range(count - 1):
        parts.append(value.astype(BF16))
        value = value - parts[-1].astype(F32)
    return parts + [value.astype(BF16)]


def readout_kernel(
    decay_ref, routes_ref, hidden_ref, qkv_ref, state_ref, gain_ref, out_ref
):
    y = lax.axis_index("y")
    cols = hidden_ref.shape[2] // 16
    depth = out_ref.shape[2] - 128

    @pl.when(pl.program_id(0) == 0)
    def _():
        names = widened(columns_of(routes_ref[y].astype(F32)))
        for i in range(16):
            rows = hidden_ref[0, :, i * cols : (i + 1) * cols].astype(F32)
            first = jnp.concatenate([rows[:, :128], rows[:, 128:256]], axis=0)
            last = jnp.concatenate([rows[:, 256:], names], axis=0)
            out_ref[i, :16, depth:] = first.astype(BF16)
            out_ref[i, 16:, depth:] = last.astype(BF16)

    n, size = STEPS * ROWS, state_ref.shape[2]
    heads = state_ref.shape[1]
    row = lax.broadcasted_iota(jnp.int32, (n, size), 0)
    row_in = row % ROWS
    row_t = lax.broadcasted_iota(jnp.int32, (n, n), 0)
    row_s = lax.broadcasted_iota(jnp.int32, (n, n), 1)
    for h in range(heads):
        lanes = slice(h * size, (h + 1) * size)
        q, k, v = [
            qkv_ref[:, i, :, lanes].astype(F32).reshape(n, size).astype(BF16) for i in range(3)
        ]
        q_twice = jnp.concatenate([q, q], axis=1)
        carried = jnp.zeros((n, size), F32)
        for pair in range(ROWS // 2):
            wide = jnp.concatenate([state_ref[2 * pair, h], state_ref[2 * pair + 1, h]], axis=1)
            both = jnp.dot(
                q_twice, jnp.concatenate(bf16_parts(wide, 2), axis=0), preferred_element_type=F32
            )
            carried = jnp.where(row_in == 2 * pair, both[:, :size], carried)
            carried = jnp.where(row_in == 2 * pair + 1, both[:, size:], carried)
        here = lax.broadcasted_iota(jnp.int32, decay_ref.shape, 1) == pl.program_id(0) * heads + h
        decay = jnp.sum(jnp.where(here, decay_ref[...], 0.0), axis=1, keepdims=True)
        decay = [decay[t : t + 1] for t in range(STEPS)]
        run = decay[0]
        first = jnp.broadcast_to(run, (n, size))
        for t in range(1, STEPS):
            run = run * decay[t]
            first = jnp.where(row // ROWS == t, run, first)
        mix = jnp.zeros((n, n), F32)
        for t in range(STEPS):
            run = None
            for s in range(t, -1, -1):
                here = row_t - row_s == (t - s) * ROWS
                mix = jnp.where(here & (row_s // ROWS == s), 1.0 if run is None else run, mix)
                run = decay[s] if run is None else run * decay[s]
        scores = lax.dot_general(q, k, (((1,), (1,)), ((), ())), preferred_element_type=F32)
        o = carried * first + jnp.dot(
            jnp.concatenate(bf16_parts(scores * mix, 2), axis=1),
            jnp.concatenate([v, v], axis=0),
            preferred_element_type=F32,
        )
        o = o * lax.rsqrt(jnp.mean(o * o, axis=-1, keepdims=True) + EPS) * gain_ref[:, lanes]
        o = o.astype(BF16)
        at = lanes_from((pl.program_id(0) * heads + h) * size, size)
        for i in range(16):
            out_ref[i, :, at] = o


def readouts(step_qkv, decay, state, attn_gain, hidden_in, routes):
    heads, size = state.shape[1], state.shape[2]
    at_once = min(heads, 4)
    n = STEPS * ROWS
    packed = heads * size + 128
    return pl.pallas_call(
        readout_kernel,
        out_shape=pltpu.VMEM((16, n, packed), BF16),
        grid=(heads // at_once,),
        in_specs=[
            pl.BlockSpec(decay.shape, lambda i: (0, 0)),
            pl.BlockSpec((STEPS, 2, ROWS), lambda i: (0, 0, 0)),
            pl.BlockSpec((1,) + hidden_in.shape[1:], lambda i: (lax.axis_index("y"), 0, 0)),
            pl.BlockSpec((STEPS, 3, ROWS, at_once * size), lambda i: (0, 0, 0, i)),
            pl.BlockSpec((ROWS, at_once, size, size), lambda i: (0, i, 0, 0)),
            pl.BlockSpec((1, at_once * size), lambda i: (0, i)),
        ],
        out_specs=pl.BlockSpec((16, n, packed), lambda i: (0, 0, 0)),
        compiler_params=vmem_params(58),
        cost_estimate=pl.CostEstimate(
            flops=2 * STEPS * ROWS * ROWS * heads * size * size * 2,
            bytes_accessed=state.size * 4,
            transcendentals=0,
        ),
        name="readout",
    )(
        decay,
        routes.transpose(0, 2, 1),
        hidden_in,
        step_qkv.transpose(0, 2, 1, 3),
        state,
        attn_gain.reshape(1, -1),
    )


def project_kernel(place_ref, got_ref, weight_ref, mine_ref, other_ref):
    c = place_ref[2]
    depth = weight_ref.shape[0]
    halves = []
    for part in range(2):
        rows = got_ref[8 * part : 8 * part + 8, :, :depth].reshape(256, depth)
        halves.append(jnp.dot(rows, weight_ref[...], preferred_element_type=F32))
    mine = jnp.where(c == 0, halves[0], halves[1]).astype(BF16)
    other = jnp.where(c == 0, halves[1], halves[0]).astype(BF16)
    mine_ref[...] = mine.reshape(mine_ref.shape)
    other_ref[...] = other.reshape(other_ref.shape)


def project(got, weight):
    out = [jax.ShapeDtypeStruct((8, STEPS, ROWS, weight.shape[1]), BF16)] * 2
    return call(project_kernel, "project", out, got, weight, flops=1024 * weight.size)


def by_y_kernel(place_ref, mine_ref, got_ref, *out_refs):
    y = place_ref[1]
    for k, ref in enumerate(out_refs):
        t = turned(y, k)
        for i in range(8):
            ref[i] = (mine_ref[i, t].astype(F32) + got_ref[i, t].astype(F32)).astype(BF16)


def sums_by_y(mine, got):
    out = [jax.ShapeDtypeStruct((8,) + mine.shape[2:], BF16)] * 4
    return call(by_y_kernel, "sums_by_y", out, mine, got)


def slots_kernel(place_ref, got_ref, select_ref, hidden_ref):
    c = place_ref[2]
    depth = got_ref.shape[2] - 128
    names = []
    for i in range(8):
        tail = got_ref[8 * c + i, :, depth:].astype(F32)
        hidden_ref[i] = jnp.concatenate([tail[:8], tail[8:16], tail[16:24]], axis=1)
        names.append(tail[24:])
    names = jnp.concatenate(names, axis=0)
    n = names.shape[0]
    across = names.T
    down_i = lax.broadcasted_iota(jnp.int32, (n, n), 0)
    over_i = lax.broadcasted_iota(jnp.int32, (n, n), 1)
    earlier = (down_i // ROWS == over_i // ROWS) & (down_i < over_i)
    slot = lax.broadcasted_iota(jnp.int32, (256, n), 0)
    base = lax.broadcasted_iota(jnp.int32, (1, n), 1) // ROWS * 2
    select = jnp.zeros((256, n), F32)
    for j in range(2):
        mine = across[j : j + 1, :]
        rank = jnp.zeros((1, n), F32)
        for other in range(2):
            same = (names[:, other : other + 1] == mine) & earlier
            rank += jnp.sum(same.astype(F32), axis=0, keepdims=True)
        target = mine.astype(jnp.int32) * 16 + base + rank.astype(jnp.int32)
        select += (slot == target).astype(F32)
    select_ref[...] = select.astype(BF16)


def slots(got, cols):
    out = [jax.ShapeDtypeStruct((256, 64), BF16), jax.ShapeDtypeStruct((8, ROWS, cols), F32)]
    return call(slots_kernel, "slots", out, got, flops=1 << 20)


def attend_kernel(place_ref, select_ref, hidden_ref, *refs):
    sum_refs, out_ref = refs[:4], refs[4]
    rows = []
    for i in range(8):
        total = hidden_ref[i]
        for ref in sum_refs:
            total += ref[i].astype(F32)
        rows.append(total)
        total = total.astype(BF16)
        for j in range(2):
            out_ref[8 * j + i, 2] = total
    rows = jnp.concatenate(rows, axis=0).astype(BF16)
    sent = jnp.dot(select_ref[...], rows, preferred_element_type=F32)
    for i in range(16):
        for j in range(2):
            out_ref[i, j] = sent[16 * i + 8 * j : 16 * i + 8 * j + 8].astype(BF16)


def attend(select, hidden, sums):
    out = jax.ShapeDtypeStruct((16, 3) + hidden.shape[1:], BF16)
    return call(attend_kernel, "attend", out, select, hidden, *sums, flops=1 << 23)


def norm_kernel(place_ref, gain_ref, got_ref, *out_refs):
    y = place_ref[1]
    cols = got_ref.shape[3]
    total = jnp.zeros((16, cols), F32)
    slots = []
    for i in range(16):
        value = jnp.concatenate([got_ref[i, j].astype(F32) for j in range(2)], axis=0)
        slots.append(value)
        total += value * value
    mean = jnp.sum(total, axis=-1, keepdims=True) / (16 * cols)
    scale = lax.rsqrt(mean + EPS)
    for i in range(16):
        at = slice(i * cols, (i + 1) * cols)
        value = (slots[i] * scale * gain_ref[:, at]).astype(BF16)
        for out_ref in out_refs:
            out_ref[:, at] = value
    for k, out_ref in enumerate(out_refs):
        for i in range(2):
            at = slice((16 + i) * cols, (17 + i) * cols)
            rows = [got_ref[turned(y, 4 - k) * 4 + 2 * core + i, 2] for core in range(2)]
            rows = jnp.concatenate([r.astype(F32) for r in rows], axis=0)
            out_ref[:, at] = rows.astype(BF16)


def norm(gain, got):
    out = [jax.ShapeDtypeStruct((16, 18 * got.shape[3]), BF16)] * 4
    return call(norm_kernel, "norm", out, gain.reshape(1, -1), got)


def owned_kernel(place_ref, *refs):
    own_refs, other_refs, out_ref = refs[:4], refs[4:8], refs[8]
    z, y, c = place_ref
    start = own_refs[0].shape[1] - out_ref.shape[2]
    for k in range(4):
        rows = jnp.where(z // 2 == c, own_refs[k][:, start:], other_refs[k][:, start:])
        rows = rows.astype(F32)
        out_ref[turned(y, k)] = jnp.where(c == 0, rows[:ROWS], rows[ROWS:]).astype(BF16)


def owned(by_y, by_core, share):
    out = jax.ShapeDtypeStruct((STEPS, ROWS, share), BF16)
    return call(owned_kernel, "owned", out, *by_y, *by_core)


def fetch_kernel(after_ref, *refs):
    in_refs, out_refs, done_ref, sems = refs[:3], refs[3:6], refs[6], refs[7]
    copies = [pltpu.make_async_copy(a, b, sems.at[i]) for i, (a, b) in enumerate(zip(in_refs, out_refs))]
    for copy in copies:
        copy.start()
    done_ref[...] = jnp.zeros_like(done_ref)
    for copy in copies:
        copy.wait()


def fetch(after, *weights):
    return pl.pallas_call(
        fetch_kernel,
        out_shape=[pltpu.VMEM(w.shape, w.dtype) for w in weights]
        + [pltpu.VMEM((8, 128), F32)],
        in_specs=[pl.BlockSpec(memory_space=pl.ANY)]
        + [pl.BlockSpec(memory_space=pltpu.HBM)] * len(weights),
        out_specs=[pl.BlockSpec(memory_space=pltpu.VMEM)] * (len(weights) + 1),
        scratch_shapes=[pltpu.SemaphoreType.DMA((len(weights),))],
        compiler_params=vmem_params(36),
        cost_estimate=pl.CostEstimate(
            flops=0, bytes_accessed=sum(2 * w.size for w in weights), transcendentals=0
        ),
        name="fetch",
    )(after, *weights)


def hidden_kernel(place_ref, *refs):
    x_refs, (gate_ref, up_ref, down_ref, _, hidden_ref, theirs_ref) = refs[:8], refs[8:]
    share = theirs_ref.shape[2]
    y, c = place_ref[1], place_ref[2]
    x = jnp.concatenate([r[:, : gate_ref.shape[1]] for r in x_refs], axis=0)
    across = (((1,), (1,)), ((), ()))
    gate = lax.dot_general(gate_ref[...], x, across, preferred_element_type=F32)
    up = lax.dot_general(up_ref[...], x, across, preferred_element_type=F32)
    hidden = (gate / (1.0 + jnp.exp(-gate)) * up).T.astype(BF16)
    n = hidden.shape[0]
    row = lax.broadcasted_iota(jnp.int32, (n, n), 0)
    lane = lax.broadcasted_iota(jnp.int32, (n, n), 1)
    source = lax.bitwise_xor(row // 64, c) * 64 + turned(row // 2, 4 - y) * 16
    source += row // 8 % 8 * 2 + row % 2
    moved = (lane == source).astype(F32).astype(BF16)
    hidden = jnp.dot(moved, hidden, preferred_element_type=F32).astype(BF16)
    hidden_ref[...] = hidden
    for k in range(4):
        block = turned(y, k) * 2 + (1 - c)
        at = pl.ds(pl.multiple_of(block * share, 128), share)
        theirs_ref[k] = jnp.dot(hidden, down_ref[:, at], preferred_element_type=F32).astype(BF16)


def hidden_units(pieces, gate, up, down_weight, done, share):
    units = gate.shape[0]
    rows = sum(p.shape[0] for p in pieces)
    out = [
        jax.ShapeDtypeStruct((rows, units), BF16),
        jax.ShapeDtypeStruct((4, rows, share), BF16),
    ]
    flops = 5 * rows * gate.size
    arrays = (*pieces, gate, up, down_weight, done)
    return call(hidden_kernel, "hidden_units", out, *arrays, flops=flops)


def down_kernel(place_ref, hidden_ref, down_ref, out_ref):
    share = out_ref.shape[2]
    y, c = place_ref[1], place_ref[2]
    for k in range(4):
        at = lanes_from((turned(y, k) * 2 + c) * share, share)
        out_ref[k] = jnp.dot(hidden_ref[...], down_ref[:, at], preferred_element_type=F32)


def down(hidden, weight, share):
    out = jax.ShapeDtypeStruct((4, hidden.shape[0], share), F32)
    flops = hidden.shape[0] * weight.size
    return call(down_kernel, "down", out, hidden, weight, flops=flops)


def cores_kernel(place_ref, ours_ref, theirs_ref, out_ref):
    for k in range(4):
        total = ours_ref[k] + theirs_ref[k].astype(F32)
        out_ref[turned(place_ref[1], k)] = total.astype(BF16)


def cores_sum(ours, theirs):
    out = jax.ShapeDtypeStruct(theirs.shape, BF16)
    out = call(cores_kernel, "cores_sum", out, ours, theirs)
    return out.reshape(64, 8, theirs.shape[2])


def weights_kernel(place_ref, routes_ref, weights_ref, out_ref):
    n = STEPS * ROWS
    names = [columns_of(routes_ref[t].astype(F32)) for t in range(STEPS)]
    names = widened(jnp.concatenate(names, axis=0))
    weights = [columns_of(weights_ref[t]) for t in range(STEPS)]
    weights = jnp.concatenate(weights, axis=0)
    down_i = lax.broadcasted_iota(jnp.int32, (n, n), 0)
    over_i = lax.broadcasted_iota(jnp.int32, (n, n), 1)
    earlier = (down_i // ROWS == over_i // ROWS) & (over_i < down_i)
    across = names.T
    slot = lax.broadcasted_iota(jnp.int32, (n, 128), 1)
    step = lax.broadcasted_iota(jnp.int32, (n, 1), 0) // ROWS
    mix = jnp.zeros((n, 128), F32)
    for j in range(2):
        mine = names[:, j : j + 1]
        rank = jnp.zeros((n, 1), F32)
        for other in range(2):
            same = (across[other : other + 1, :] == mine) & earlier
            rank += jnp.sum(same.astype(F32), axis=1, keepdims=True)
        target = mine.astype(jnp.int32) * 8 + 2 * step + rank.astype(jnp.int32)
        mix += jnp.where(slot == target, weights[:, j : j + 1], 0.0)
    out_ref[...] = jnp.concatenate(bf16_parts(mix, 3), axis=1)


def mix_weights(routes, weights):
    out = jax.ShapeDtypeStruct((STEPS * ROWS, 384), BF16)
    arrays = (routes.transpose(0, 2, 1), weights.transpose(0, 2, 1))
    return call(weights_kernel, "mix_weights", out, *arrays, flops=1 << 20)


def mix_kernel(place_ref, mix_ref, back_ref, out_ref):
    back = back_ref[...].astype(F32)
    back = (back[:16] + back[16:32]) + (back[32:48] + back[48:])
    back = back.reshape(128, back.shape[2]).astype(BF16)
    out_ref[...] = jnp.dot(
        mix_ref[...], jnp.concatenate([back] * 3, axis=0), preferred_element_type=F32
    ).astype(BF16)


def mixed_rows(mix, back):
    out = jax.ShapeDtypeStruct((STEPS * ROWS, back.shape[2]), BF16)
    return call(mix_kernel, "mix", out, mix, back, flops=1 << 24)


def shards(
    hidden_in,
    step_qkv,
    decay_rates,
    kv_state,
    attn_gain,
    out_proj,
    ffn_gain,
    routes,
    route_weights,
    w_gate,
    w_up,
    w_down,
):
    share = hidden_in.shape[2] // 8

    sent = readouts(step_qkv, decay_rates, kv_state, attn_gain, hidden_in, routes)
    got = exchange(sent, ("z", "x"))

    mine, other = project(got, out_proj)
    sums = sums_by_y(mine, over("c", other, 1))
    select, hidden = slots(got, out_proj.shape[1])
    sums = sums[:1] + [over("y", sums[k], k) for k in (2, 1, 3)]

    pieces = norm(ffn_gain, exchange(attend(select, hidden, sums), ("z", "x")))
    by_y = pieces[:1] + [over("y", pieces[k], -k) for k in (1, 2, 3)]
    gate, up, down_weight, done = fetch(
        pieces[1], w_gate[0].swapaxes(0, 1), w_up[0].swapaxes(0, 1), w_down[0]
    )
    by_y[2], done = lax.optimization_barrier((by_y[2], done))
    by_core = [over("c", piece, 1) for piece in by_y]

    hidden, theirs = hidden_units(by_y + by_core, gate, up, down_weight, done, share)
    theirs = over("c", theirs, 1)
    sums = cores_sum(down(hidden, down_weight, share), theirs)

    attended = owned(by_y, by_core, share)
    mix = mix_weights(routes, route_weights)
    mixed = mixed_rows(mix, exchange(sums, ("y", "z", "x")))
    return attended, mixed.reshape(STEPS, ROWS, share)


def solution(mesh):
    exp, head = ("z", "x"), ("y", "c")
    return jax.shard_map(
        shards,
        mesh=jax.sharding.Mesh(mesh.devices.reshape(4, 2, 4, 4), head + exp),
        in_specs=(
            P(None, exp, None),
            P(None, exp, None, head),
            P(None, head),
            P(exp, head, None, None),
            P(head),
            P(head, exp),
            P(),
            P(None, exp, None),
            P(None, exp, None),
            P(exp, None, head),
            P(exp, None, head),
            P(exp, head, None),
        ),
        out_specs=(P(None, exp, head), P(None, exp, head)),
        check_vma=False,
    )
```
